256 devices in a mesh: grp: 2 (over x_lo), gx: 32 (over x_hi, z, core), gy: 4 (over y).
Axes of the slice: x: 4 (x_hi: 2, x_lo: 2; x = x_hi * 2 + x_lo), y: 4, z: 8, core: 2. Of those that a mesh axis runs over, the one named last changes fastest.
Arguments:
- source: float32 [2, 512, 32, 256], P('grp', 'gx', 'gy'), may hold values from -8 to 8
- storage: float32 [2, 512, 32, 256], P('grp', 'gx', 'gy'), may hold values from 0.1 to 4
- host_device: int32 [16384, 1], P(('gx', 'gy')), may hold values from 0 to 127; in each aligned block of 128 rows (0 to 127, 128 to 255, ...) at most 2 rows name the same one
- host_column: int32 [16384], P(('gx', 'gy')), may hold values from 0 to 127
- inter_device: int32 [16384, 2], P(('gx', 'gy')), may hold values from 0 to 127, all different within a row; in each aligned block of 128 rows (0 to 127, 128 to 255, ...) at most 4 rows name the same one
- inter_slot: int32 [16384, 2], P(('gx', 'gy')), may hold values from 0 to 127
Outputs:
- pressure: float32 [2, 512, 32, 256], P('grp', 'gx', 'gy')
The draws below stay inside these ranges and needn't reach their ends.
Inputs may be any that keep to these rules, and one draw needn't show every extreme that they name: `host_device`: in the rows of one device (128 aligned rows) no matrix device is named more than 2 times; some device is named exactly 2 times. `inter_device`: in the rows of one device no device is named more than 4 times; some device is named exactly 4 times; a row names distinct devices.
All inputs are finite; a program needn't handle non-finite values.
Results may differ from the reference program's by a relative error of at most 0.0001.
Values sent between devices are 32-bit elements; how exact they have to be, the bound alone decides.
A program may use at most 128 MiB of HBM per device.

```python
import math
import jax
import jax.numpy as jnp
import numpy as np

BX = 16
BY = 8
TS = 16
INTERS = 2
SWEEPS = 2
DEGREE = 3
TILE = 256
FBLK = 128
NX = 512
NY = 32
NFB = 16384
CAP = 2
CAPI = 4
N_GX = 32
N_GY = 4


def with_ends(drawn, stream_key, least, top_value):
    shape = drawn.shape
    spot = [jax.random.randint(jax.random.fold_in(stream_key, axis), (), 0, shape[axis]) for axis in range(len(shape))]
    drawn = drawn.at[tuple(spot)].set(least)
    longest = shape.index(max(shape))
    spot[longest] = (spot[longest] + 1) % shape[longest]
    return drawn.at[tuple(spot)].set(top_value)


def level_of(rng, extent, shards, least, high):
    def one(dim, blocks):
        draws = jax.random.uniform(jax.random.fold_in(jax.random.fold_in(rng, 6), dim), (blocks,), jnp.float32, least / len(shards), high / len(shards))
        return jnp.repeat(jnp.exp(draws), extent[dim] // blocks).reshape((-1,) + (1,) * (len(extent) - dim - 1))

    factor_of = one(*shards[0])
    for cut in shards[1:]:
        factor_of = factor_of * one(*cut)
    return factor_of


def shared_out(own_key, own, number, rows, number_of, top, limit, lean):
    order = jax.random.permutation(own_key, number_of)
    crowded, usual = load_shares(number_of, rows * top, limit, lean, True), load_shares(number_of, rows * top, limit, lean, False)
    places = jnp.arange(number_of)

    def named(tallies, rotation):
        used = int((tallies > 0).sum())
        fixed = max(1, used // 4)
        passed = fixed + (places - fixed + rotation * (used - fixed)) % max(1, number_of - fixed)
        return jnp.zeros((number_of,), jnp.int32).at[order[jnp.where(places < fixed, places, passed)]].set(jnp.asarray(tallies, jnp.int32))

    tallies = jnp.where(number % 4 == 0, named(crowded, number // 4), named(usual, number - number // 4 - 1))
    mixed = jax.random.permutation(jax.random.fold_in(own, 3), number_of)
    donor, taker = mixed[0:number_of // 2 * 2:2], mixed[1:number_of // 2 * 2:2]
    margin = jnp.minimum(tallies[donor] - 1, limit - tallies[taker]) // 2
    margin = jnp.where((donor == order[0]) | (taker == order[0]) | (tallies[taker] == 0), 0, jnp.maximum(margin, 0))
    passed = jax.random.randint(jax.random.fold_in(own, 4), (number_of // 2,), 0, 1 << 20) % (margin + 1)
    tallies = tallies.at[donor].add(-passed).at[taker].add(passed)
    members = jnp.searchsorted(jnp.cumsum(tallies), jnp.arange(rows * top), side="right").astype(jnp.int32)
    table = members.reshape(top, rows).T
    table = table[jax.random.permutation(jax.random.fold_in(own, 1), rows)]
    rotation = jax.random.randint(jax.random.fold_in(own, 2), (rows, 1), 0, top)
    return jnp.take_along_axis(table, (jnp.arange(top)[None, :] + rotation) % top, axis=1)


def load_shares(count, total, most, lean, full):
    weights = [(1 << 20) // math.isqrt(standing ** lean) + 1 for standing in range(1, count + 1)]
    largest = most if full else min(most, max(-(-total // count), total * weights[0] // sum(weights)))
    least = 1 if total - largest >= count - 1 else 0
    counts, surplus = [largest] + [least] * (count - 1), total - largest - least * (count - 1)
    while surplus > 0:
        free = [i for i in range(1, count) if counts[i] < largest] or [i for i in range(1, count) if counts[i] < most]
        pool, budget = sum([weights[i] for i in free]), surplus
        for i in free:
            extra = min(most - counts[i], max(1, budget * weights[i] // pool), surplus)
            counts[i] = counts[i] + extra
            surplus = surplus - extra
    return np.array(counts)


def bell_draw(rng, shape, deviation, reach, shards=(), dtype=jnp.bfloat16):
    result = jax.random.normal(rng, shape, jnp.float32) * deviation
    if len(shards) > 0:
        result = level_of(rng, shape, shards, -0.22, 0.18) * result
    return jnp.clip(result, min=-reach, max=reach).astype(dtype)


def setup_inputs(seed: int = 0) -> dict:
    key_of = jax.random.split(jax.random.key(seed), 7)
    source = bell_draw(key_of[0], (2, NX, NY, TILE), 1.0, 8.0, ((0, 2), (1, 32), (2, 4)), jnp.float32)
    storage = jnp.clip(jnp.exp(math.log(4.0) - 3.6888794 * jax.random.uniform(key_of[1], (2, NX, NY, TILE), jnp.float32) ** level_of(key_of[1], (2, NX, NY, TILE), ((0, 2), (1, 32), (2, 4)), -0.2, 0.2)), 0.1, 4.0)
    host_device_keys = jax.random.split(jax.random.fold_in(key_of[2], 1), NFB // FBLK)
    host_device_turns = jax.random.permutation(jax.random.fold_in(key_of[2], 3), NFB // FBLK)
    host_device = jax.vmap(lambda own, number: shared_out(jax.random.fold_in(key_of[2], 2), own, number, FBLK, N_GX * N_GY, 1, CAP, 2))(host_device_keys, host_device_turns).reshape((NFB, 1))
    host_column = with_ends(jax.random.randint(key_of[3], (NFB,), 0, FBLK), jax.random.fold_in(key_of[3], 1), 0, FBLK - 1).astype(jnp.int32)
    inter_device_keys = jax.random.split(jax.random.fold_in(key_of[4], 1), NFB // FBLK)
    inter_device_turns = jax.random.permutation(jax.random.fold_in(key_of[4], 3), NFB // FBLK)
    inter_device = jax.vmap(lambda own, number: shared_out(jax.random.fold_in(key_of[4], 2), own, number, FBLK, N_GX * N_GY, INTERS, CAPI, 2))(inter_device_keys, inter_device_turns).reshape((NFB, INTERS))
    inter_slot = with_ends(jax.random.randint(key_of[5], (NFB, INTERS), 0, FBLK), jax.random.fold_in(key_of[5], 1), 0, FBLK - 1).astype(jnp.int32)
    return {"source": source, "storage": storage, "host_device": host_device, "host_column": host_column, "inter_device": inter_device, "inter_slot": inter_slot}


TF = 2.0
TI = 1.0
TM = 0.5
LMIN = 0.3
LMAX = 3.0


def to_blocks(field):
    return field.reshape(N_GX, BX, N_GY, BY, TILE).transpose(0, 2, 1, 3, 4).reshape(NFB, TILE)


def from_blocks(blocks):
    return blocks.reshape(N_GX, N_GY, BX, BY, TILE).transpose(0, 2, 1, 3, 4).reshape(NX, NY, TILE)


def in_plane(tiles):
    column = jnp.arange(TILE) % TS
    zero_col = jnp.zeros_like(tiles[:, :1])
    zero_row = jnp.zeros_like(tiles[:, :TS])
    left = jnp.where(column != 0, jnp.concatenate([zero_col, tiles[:, :-1]], 1), 0.0)
    right = jnp.where(column != TS - 1, jnp.concatenate([tiles[:, 1:], zero_col], 1), 0.0)
    upper = jnp.concatenate([zero_row, tiles[:, :-TS]], 1)
    lower = jnp.concatenate([tiles[:, TS:], zero_row], 1)
    return TF * (4.0 * tiles - left - right - upper - lower)


def operate(field, storage, host, partner):
    matrix = field[0]
    padded = jnp.pad(matrix, 1)
    beside = padded[2:, 1:-1, 1:-1] + padded[:-2, 1:-1, 1:-1]
    beside = beside + padded[1:-1, 2:, 1:-1] + padded[1:-1, :-2, 1:-1]
    beside = beside + padded[1:-1, 1:-1, 2:] + padded[1:-1, 1:-1, :-2]
    frac = to_blocks(field[1])
    mat_blocks = to_blocks(matrix)
    flux = TM * (mat_blocks[host] - frac)
    mat_out = (storage[0] + 6.0) * matrix - beside + from_blocks(jax.ops.segment_sum(flux, host, num_segments=NFB))
    frac_out = to_blocks(storage[1]) * frac + in_plane(frac) - flux
    for which in range(INTERS):
        target = partner[:, which]
        gain = TI * (frac[target] - frac)
        frac_out = frac_out - gain + jax.ops.segment_sum(gain, target, num_segments=NFB)
    return jnp.stack([mat_out, from_blocks(frac_out)])


def reference(source, storage, host_device, host_column, inter_device, inter_slot):
    host = (host_device[:, 0] * FBLK + host_column).astype(jnp.int32)
    partner = (inter_device * FBLK + inter_slot).astype(jnp.int32)
    diag = jnp.stack([storage[0] + 6.0 + TM, storage[1] + 4.0 * TF + 2.0 * INTERS * TI + TM])
    theta = (LMAX + LMIN) / 2.0
    delta = (LMAX - LMIN) / 2.0
    sigma = theta / delta
    pressure = jnp.zeros_like(source)
    for sweep in range(SWEEPS):
        residual = source - operate(pressure, storage, host, partner)
        dirn = residual / (theta * diag)
        rho = 1.0 / sigma
        for inner in range(DEGREE):
            pressure = pressure + dirn
            residual = residual - operate(dirn, storage, host, partner)
            rho_new = 1.0 / (2.0 * sigma - rho)
            dirn = rho_new * rho * dirn + (2.0 * rho_new / delta) * residual / diag
            rho = rho_new
        pressure = pressure + dirn
    return pressure
```

```python
import jax
import jax.numpy as jnp
from jax import lax
from jax.experimental import pallas as pl
from jax.experimental.pallas import tpu as pltpu
from jax.sharding import PartitionSpec as P

TF = 2.0
TI = 1.0
TM = 0.5
LMIN = 0.3
LMAX = 3.0
STEPS = 7

ROWS = 512
PEERS = 32
MSG = 48

F32 = jnp.float32
BF16 = jnp.bfloat16
I32 = jnp.int32
MESH = pl.DeviceIdType.MESH


def coefficients():
    theta = (LMAX + LMIN) / 2.0
    delta = (LMAX - LMIN) / 2.0
    sigma = theta / delta
    rho = 1.0 / sigma
    pairs = []
    for _ in range(3):
        rho_new = 1.0 / (2.0 * sigma - rho)
        pairs.append((rho_new * rho, 2.0 * rho_new / delta))
        rho = rho_new
    pairs.append((0.0, 1.0 / theta))
    return pairs, theta


def turn(x, shift):
    shift = shift % 128
    return x if shift == 0 else pltpu.roll(x, shift, 1)


def lanes(rows):
    return lax.broadcasted_iota(I32, (rows, 128), 1)


def kernel(
    src, sto, gbf, gbm, sbf, sbm, out,
    gf, gm, sf, sm, wf, wm, rf, rm,
    send, recv, hs, hz, ys, hy, hx,
    tx, rx, tx2, rx2,
    d_ref, r_ref, p_ref, c_ref, i_ref,
    send_sem, recv_sem, hsend_sem, hrecv_sem, tsend_sem, trecv_sem, usend_sem, urecv_sem,
):
    g = lax.axis_index("grp")
    gx = lax.axis_index("gx")
    gy = lax.axis_index("gy")
    x_hi = gx // 16
    cz = (gx // 2) % 8
    core = gx % 2
    w = x_hi * 4 + g * 2 + core

    def place(w_, y_, z_):
        return ((w_ // 2) % 2, (w_ // 4) * 16 + z_ * 2 + w_ % 2, y_)

    def peer(k):
        return place((w + k // 4) % 8, (gy + k % 4) % 4, cz)

    w_home = gx // 4
    u_home = gx % 4
    own = w_home == w

    barrier = pltpu.get_barrier_semaphore()

    def greet(device):
        pl.semaphore_signal(barrier, inc=1, device_id=device, device_id_type=MESH)

    def greet_peer(k, carry):
        greet(peer(k))
        return carry

    lax.fori_loop(1, PEERS, greet_peer, 0)
    greet(place(w, gy, (cz + 1) % 8))
    greet(place(w, gy, (cz + 7) % 8))

    def greet_far(n, carry):
        @pl.when(jnp.logical_not(own & (n == cz)))
        def _():
            greet(place(w_home, gy, n))

        @pl.when(jnp.logical_not(own & (n == g * 4 + u_home)))
        def _():
            greet((n // 4, w * 4 + n % 4, gy))

        return carry

    lax.fori_loop(0, 8, greet_far, 0)

    l32 = lanes(32)
    for z in range(8):
        half, part = z // 4, z % 4
        for a, ref in ((0, src), (1, sto)):
            acc = jnp.zeros((32, 128), F32)
            for q in range(4):
                piece = ref[q * 32:(q + 1) * 32, half * 128:(half + 1) * 128]
                acc = jnp.where(l32 // 32 == q, turn(piece, 32 * (q - part)), acc)
            tx[z, a * 32:(a + 1) * 32, :] = acc

    pl.semaphore_wait(barrier, PEERS - 1 + 2 + jnp.where(own, 14, 16))

    def far_copy(z):
        return pltpu.make_async_remote_copy(
            src_ref=tx.at[z],
            dst_ref=rx.at[g * 4 + u_home],
            send_sem=tsend_sem.at[z],
            recv_sem=trecv_sem.at[g * 4 + u_home],
            device_id=place(w_home, gy, z),
            device_id_type=MESH,
        )

    def far_start(z, carry):
        mine = own & (z == cz)

        @pl.when(mine)
        def _():
            rx[g * 4 + u_home] = tx[z]

        @pl.when(jnp.logical_not(mine))
        def _():
            far_copy(z).start()

        return carry

    lax.fori_loop(0, 8, far_start, 0)

    iota_cols = lax.broadcasted_iota(I32, (80, ROWS), 1)

    def build_g(j, carry):
        at = pl.multiple_of(j * 80, 80)
        rows = gbf[pl.ds(at, 80), :]
        for q in range(4):
            hit = rows[:, q:q + 1] == iota_cols
            gf[pl.ds(at, 80), q * ROWS:(q + 1) * ROWS] = jnp.where(hit, 1.0, 0.0).astype(BF16)
        at = pl.multiple_of(j * 16, 16)
        rows = gbm[pl.ds(at, 16), :]
        for q in range(4):
            hit = rows[:, q:q + 1] == iota_cols[:16]
            gm[pl.ds(at, 16), q * ROWS:(q + 1) * ROWS] = jnp.where(hit, 1.0, 0.0).astype(BF16)
        return carry

    lax.fori_loop(0, 16, build_g, 0)

    within = lax.broadcasted_iota(I32, (1, 1280), 1) % 40
    weight = jnp.where(within < 32, TI, TM)

    def build_s(j, carry):
        at = pl.multiple_of(j * 16, 16)
        block = lax.broadcasted_iota(I32, (16, 1280), 0) + at
        for q in range(4):
            sf[pl.ds(at + q * ROWS, 16), :] = jnp.where(sbf[q:q + 1, :] == block, weight, 0.0).astype(BF16)
            sm[pl.ds(at + q * ROWS, 16), :] = jnp.where(
                sbm[q:q + 1, :] == block[:, :256], TM, 0.0
            ).astype(BF16)
        return carry

    lax.fori_loop(0, 32, build_s, 0)

    ln = lanes(ROWS)
    group = ln // 32
    is_f = ln < 32
    is_m = group == 1

    entering = jnp.where(lax.broadcasted_iota(I32, (1280, 128), 0) % 40 < 16, 1.0, 0.0).astype(BF16)
    ones = jnp.ones((256, 128), BF16)
    indeg = jnp.zeros((ROWS, 128), F32)
    hosted = jnp.zeros((ROWS, 128), F32)
    for q in range(4):
        indeg = indeg + jnp.dot(sf[q * ROWS:(q + 1) * ROWS, :], entering, preferred_element_type=F32)
        hosted = hosted + jnp.dot(sm[q * ROWS:(q + 1) * ROWS, :], ones, preferred_element_type=F32)

    def far_wait(n, carry):
        mine = own & (n == g * 4 + u_home)

        @pl.when(jnp.logical_not(mine))
        def _():
            pltpu.make_async_copy(rx.at[n], rx.at[n], trecv_sem.at[n]).wait()

        @pl.when(jnp.logical_not(own & (n == cz)))
        def _():
            pltpu.make_async_copy(tx.at[n], tx.at[n], tsend_sem.at[n]).wait()

        return carry

    lax.fori_loop(0, 8, far_wait, 0)

    pairs, theta = coefficients()
    for a, ref in ((0, r_ref), (1, c_ref)):
        for u in range(4):
            fr = rx[4 + u, a * 32:(a + 1) * 32, :]
            ma = rx[u, a * 32:(a + 1) * 32, :]
            for q in range(4):
                ref[u * 128 + q * 32:u * 128 + (q + 1) * 32, :] = jnp.where(
                    l32 < 32,
                    turn(fr, -32 * q),
                    jnp.where(l32 // 32 == 1, turn(ma, 32 - 32 * q), 0.0),
                )
    stored = c_ref[...]
    inverse = 1.0 / (stored + jnp.where(is_f, 4.0 * TF + 4.0 * TI + TM, 6.0 + TM))
    i_ref[...] = inverse
    c_ref[...] = stored + jnp.where(is_f, 4.0 * TF + 2.0 * TI + TM + indeg, 6.0 + hosted)
    d_ref[...] = r_ref[...] * inverse * (1.0 / theta)
    p_ref[...] = jnp.zeros((ROWS, 128), F32)

    low = jnp.where(cz > 0, 1.0, 0.0)
    high = jnp.where(cz < 7, 1.0, 0.0)
    left = jnp.where(w > 0, 1.0, 0.0)
    right = jnp.where(w < 7, 1.0, 0.0)
    near = jnp.where(gy > 0, 1.0, 0.0)
    beyond = jnp.where(gy < 3, 1.0, 0.0)
    l128 = lanes(128)

    def packed(x):
        acc = x[0:128]
        for q in range(1, 4):
            acc = jnp.where(l128 // 32 == q, turn(x[q * 128:(q + 1) * 128], 32 * q), acc)
        return acc

    def unpacked(x):
        return jnp.concatenate([turn(x, -32 * q) for q in range(4)], axis=0)

    def step(t, carry):
        par = t % 2

        def halo(n, source, dest, device):
            return pltpu.make_async_remote_copy(
                src_ref=source,
                dst_ref=dest,
                send_sem=hsend_sem.at[n],
                recv_sem=hrecv_sem.at[par, n],
                device_id=device,
                device_id_type=MESH,
            )

        halos = [
            halo(0, hs.at[0], hz.at[par, 0], place(w, gy, (cz + 1) % 8)),
            halo(1, hs.at[1], hz.at[par, 1], place(w, gy, (cz + 7) % 8)),
            halo(2, ys.at[1], hy.at[par, 0], place(w, (gy + 1) % 4, cz)),
            halo(3, ys.at[0], hy.at[par, 1], place(w, (gy + 3) % 4, cz)),
            halo(4, d_ref.at[pl.ds(ROWS - 8, 8)], hx.at[par, 0], place((w + 1) % 8, gy, cz)),
            halo(5, d_ref.at[pl.ds(0, 8)], hx.at[par, 1], place((w + 7) % 8, gy, cz)),
        ]
        d = d_ref[...]
        high_part = d.astype(BF16).astype(F32)
        low_part = d - high_part
        for s in range(4):
            for part, x in ((0, turn(high_part, 32 * s)), (1, turn(low_part, 32 * s))):
                q = (s + 1) % 4
                wf[s * ROWS:(s + 1) * ROWS, part * 128:(part + 1) * 128] = jnp.where(
                    group == s, x, 0.0
                ).astype(BF16)
                wm[q * ROWS:(q + 1) * ROWS, part * 128:(part + 1) * 128] = jnp.where(
                    group == q, x, 0.0
                ).astype(BF16)

        def message(k):
            return pltpu.make_async_remote_copy(
                src_ref=send.at[k],
                dst_ref=recv.at[par, k],
                send_sem=send_sem,
                recv_sem=recv_sem.at[par],
                device_id=peer(k),
                device_id_type=MESH,
            )

        def gather(c, carry):
            at = pl.multiple_of(c * 320, 320)
            x = jnp.dot(gf[pl.ds(at, 320), :], wf[...], preferred_element_type=F32)
            send[pl.ds(c * 8, 8), 0:40, :] = (x[:, :128] + x[:, 128:]).reshape(8, 40, 128)
            at = pl.multiple_of(c * 64, 64)
            x = jnp.dot(gm[pl.ds(at, 64), :], wm[...], preferred_element_type=F32)
            send[pl.ds(c * 8, 8), 40:48, :] = (x[:, :128] + x[:, 128:]).reshape(8, 8, 128)
            for n in range(8):
                k = c * 8 + n
                if n == 0:
                    @pl.when(c > 0)
                    def _():
                        message(k).start()
                else:
                    message(k).start()
            return carry

        hs[0] = packed(jnp.where(ln < 16, turn(d, -16), turn(d, -47)))
        hs[1] = packed(jnp.where(ln < 16, d, turn(d, -16)))
        ys[0] = d_ref[pl.ds(0, 64, stride=8), :]
        ys[1] = d_ref[pl.ds(7, 64, stride=8), :]
        for copy in halos:
            copy.start()
        lax.fori_loop(0, 4, gather, 0)
        recv[par, 0] = send[0]

        col = ln % 16
        before = turn(d, 1)
        after = turn(d, -1)
        nb_f = jnp.where(col != 0, before, 0.0) + jnp.where(col != 15, after, 0.0)
        nb_f = nb_f + jnp.where(ln >= 16, turn(d, 16), 0.0) + jnp.where(ln < 16, turn(d, -16), 0.0)
        nb_m = jnp.where(ln != 32, before, 0.0) + jnp.where(ln != 63, after, 0.0)
        nb_m = nb_m + jnp.concatenate([jnp.zeros((8, 128), F32), d[:ROWS - 8]], axis=0)
        nb_m = nb_m + jnp.concatenate([d[8:], jnp.zeros((8, 128), F32)], axis=0)
        sub = lax.broadcasted_iota(I32, (ROWS, 128), 0) % 8
        nb_m = nb_m + jnp.where(sub != 0, pltpu.roll(d, 1, 0), 0.0)
        nb_m = nb_m + jnp.where(sub != 7, pltpu.roll(d, ROWS - 1, 0), 0.0)
        for copy in halos:
            copy.wait_recv()
        from_low = unpacked(hz[par, 0]) * low
        from_high = unpacked(hz[par, 1]) * high
        nb_f = nb_f + jnp.where(ln < 16, from_low, turn(from_high, 16))
        nb_m = nb_m + jnp.where(ln == 32, turn(from_low, 16), 0.0)
        nb_m = nb_m + jnp.where(ln == 63, turn(from_high, 47), 0.0)
        y0 = jnp.broadcast_to((hy[par, 0] * near)[:, None, :], (64, 8, 128)).reshape(ROWS, 128)
        y1 = jnp.broadcast_to((hy[par, 1] * beyond)[:, None, :], (64, 8, 128)).reshape(ROWS, 128)
        nb_m = nb_m + jnp.where(sub == 0, y0, 0.0) + jnp.where(sub == 7, y1, 0.0)
        nb_m = nb_m + jnp.concatenate(
            [hx[par, 0] * left, jnp.zeros((ROWS - 16, 128), F32), hx[par, 1] * right], axis=0
        )
        nb = jnp.where(is_f, TF * nb_f, jnp.where(is_m, nb_m, 0.0))
        p_ref[...] = p_ref[...] + d
        r_ref[...] = r_ref[...] - (c_ref[...] * d - nb)

        pltpu.make_async_copy(
            recv.at[par, pl.ds(1, PEERS - 1)], recv.at[par, pl.ds(1, PEERS - 1)], recv_sem.at[par]
        ).wait()
        x = recv[par, :, 8:48, :].reshape(1280, 128)
        hi = x.astype(BF16)
        rf[:, 0:128] = hi
        rf[:, 128:256] = (x - hi.astype(F32)).astype(BF16)
        x = recv[par, :, 0:8, :].reshape(256, 128)
        hi = x.astype(BF16)
        rm[:, 0:128] = hi
        rm[:, 128:256] = (x - hi.astype(F32)).astype(BF16)
        sum_f = jnp.zeros((ROWS, 128), F32)
        sum_m = jnp.zeros((ROWS, 128), F32)
        for q in range(4):
            x = jnp.dot(sf[q * ROWS:(q + 1) * ROWS, :], rf[...], preferred_element_type=F32)
            sum_f = jnp.where(group == q, x[:, :128] + x[:, 128:], sum_f)
            x = jnp.dot(sm[q * ROWS:(q + 1) * ROWS, :], rm[...], preferred_element_type=F32)
            sum_m = jnp.where(group == q, x[:, :128] + x[:, 128:], sum_m)
        sum_f = sum_f + turn(sum_f, 64)
        sum_f = sum_f + turn(sum_f, 32)
        sum_m = sum_m + turn(sum_m, 64)
        sum_m = sum_m + turn(sum_m, 32)
        total = jnp.where(is_f, sum_f, jnp.where(is_m, sum_m, 0.0))

        for copy in halos:
            copy.wait_send()
        pltpu.make_async_copy(
            send.at[pl.ds(1, PEERS - 1)], send.at[pl.ds(1, PEERS - 1)], send_sem
        ).wait()
        phase = t % 4
        alpha = jnp.float32(pairs[3][0])
        beta = jnp.float32(pairs[3][1])
        for n in range(3):
            alpha = jnp.where(phase == n, jnp.float32(pairs[n][0]), alpha)
            beta = jnp.where(phase == n, jnp.float32(pairs[n][1]), beta)
        r = r_ref[...] + total
        r_ref[...] = r
        d_ref[...] = alpha * d_ref[...] + beta * (r * i_ref[...])
        return carry

    lax.fori_loop(0, STEPS, step, 0)

    for n in range(8):
        acc = jnp.zeros((32, 128), F32)
        for q in range(4):
            at = (n % 4) * 128 + q * 32
            piece = p_ref[at:at + 32, :] + d_ref[at:at + 32, :]
            acc = jnp.where(l32 // 32 == q, turn(piece, 32 * q - (32 if n < 4 else 0)), acc)
        tx2[n] = acc

    def back_start(n, carry):
        mine = own & (n == g * 4 + u_home)

        @pl.when(mine)
        def _():
            rx2[cz] = tx2[n]

        @pl.when(jnp.logical_not(mine))
        def _():
            pltpu.make_async_remote_copy(
                src_ref=tx2.at[n],
                dst_ref=rx2.at[cz],
                send_sem=usend_sem.at[n],
                recv_sem=urecv_sem.at[cz],
                device_id=(n // 4, w * 4 + n % 4, gy),
                device_id_type=MESH,
            ).start()

        return carry

    lax.fori_loop(0, 8, back_start, 0)

    def back_wait(n, carry):
        @pl.when(jnp.logical_not(own & (n == cz)))
        def _():
            pltpu.make_async_copy(rx2.at[n], rx2.at[n], urecv_sem.at[n]).wait()

        @pl.when(jnp.logical_not(own & (n == g * 4 + u_home)))
        def _():
            pltpu.make_async_copy(tx2.at[n], tx2.at[n], usend_sem.at[n]).wait()

        return carry

    lax.fori_loop(0, 8, back_wait, 0)
    for half in range(2):
        for q in range(4):
            acc = jnp.zeros((32, 128), F32)
            for part in range(4):
                acc = jnp.where(l32 // 32 == part, turn(rx2[half * 4 + part], 32 * (part - q)), acc)
            out[q * 32:(q + 1) * 32, half * 128:(half + 1) * 128] = acc


def edge_table(dest, where_to, per_row, most):
    count = dest.shape[0]
    order = jnp.arange(count, dtype=I32)
    same = (dest[:, None] == dest[None, :]) & (order[None, :] < order[:, None])
    rank = jnp.sum(same.astype(I32), axis=1)
    code = 1 + (order // per_row) * 128 + where_to
    key = rank * 128 + dest
    wanted = jnp.arange(most * 128, dtype=I32)
    return jnp.sum(jnp.where(key[None, :] == wanted[:, None], code[None, :], 0), axis=1).reshape(most, 128)


def tables(host_device, host_column, inter_device, inter_slot):
    g = lax.axis_index("grp")
    gx = lax.axis_index("gx")
    gy = lax.axis_index("gy")
    w = (gx // 16) * 4 + g * 2 + gx % 2
    mine = jnp.concatenate(
        [
            edge_table(inter_device.reshape(-1), inter_slot.reshape(-1), 2, 4),
            edge_table(host_device.reshape(-1), host_column, 1, 2),
        ],
        axis=0,
    )
    every = lax.all_gather(mine, ("gx", "gy"), axis=0, tiled=False).reshape(8, 4, 4, 6, 8, 4, 4)
    sent = lax.dynamic_slice(every, (w, 0, gy, 0, 0, 0, 0), (1, 4, 1, 6, 8, 4, 4)).reshape(4, 6, 8, 4, 4)
    came = lax.dynamic_slice(every, (0, 0, 0, 0, w, 0, gy), (8, 4, 4, 6, 1, 4, 1)).reshape(8, 4, 4, 6, 4)

    def relative(x):
        x = lax.dynamic_slice_in_dim(jnp.concatenate([x, x], axis=0), w, 8, axis=0)
        return lax.dynamic_slice_in_dim(jnp.concatenate([x, x], axis=1), gy, 4, axis=1)

    sent = relative(sent.transpose(2, 4, 0, 3, 1))
    came = relative(came.transpose(0, 2, 1, 4, 3))
    u = jnp.arange(4, dtype=I32) * 128
    sent = jnp.where(sent > 0, u[:, None, None] + (sent - 1) // 128, -1)
    came = jnp.where(came > 0, u[None, :, None] + (came - 1) % 128, -1)
    f_out = sent[..., :4].reshape(8, 4, 16, 4)
    h_out = sent[..., 4:].reshape(8, 4, 8, 4)
    f_in = came[..., :4].reshape(8, 4, 16, 4)
    h_in = came[..., 4:].reshape(8, 4, 8, 4)

    def mirror(x):
        x = jnp.concatenate([x[:1], x[:0:-1]], axis=0)
        return jnp.concatenate([x[:, :1], x[:, :0:-1]], axis=1)

    gbf = jnp.concatenate([h_out, f_out, f_in], axis=2).reshape(1280, 4)
    gbm = h_in.reshape(256, 4)
    sbf = mirror(jnp.concatenate([f_in, f_out, h_out], axis=2)).reshape(1280, 4).T
    sbm = mirror(h_in).reshape(256, 4).T
    return gbf, gbm, sbf, sbm


def per_device(source, storage, host_device, host_column, inter_device, inter_slot):
    gbf, gbm, sbf, sbm = tables(host_device, host_column, inter_device, inter_slot)
    dma = pltpu.SemaphoreType.DMA
    result = pl.pallas_call(
        kernel,
        out_shape=jax.ShapeDtypeStruct((128, 256), F32),
        in_specs=[pl.BlockSpec(memory_space=pltpu.VMEM)] * 6,
        out_specs=pl.BlockSpec(memory_space=pltpu.VMEM),
        scratch_shapes=[
            pltpu.VMEM((1280, 2048), BF16),
            pltpu.VMEM((256, 2048), BF16),
            pltpu.VMEM((2048, 1280), BF16),
            pltpu.VMEM((2048, 256), BF16),
            pltpu.VMEM((2048, 256), BF16),
            pltpu.VMEM((2048, 256), BF16),
            pltpu.VMEM((1280, 256), BF16),
            pltpu.VMEM((256, 256), BF16),
            pltpu.VMEM((PEERS, MSG, 128), F32),
            pltpu.VMEM((2, PEERS, MSG, 128), F32),
            pltpu.VMEM((2, 128, 128), F32),
            pltpu.VMEM((2, 2, 128, 128), F32),
            pltpu.VMEM((2, 64, 128), F32),
            pltpu.VMEM((2, 2, 64, 128), F32),
            pltpu.VMEM((2, 2, 8, 128), F32),
            pltpu.VMEM((8, 64, 128), F32),
            pltpu.VMEM((8, 64, 128), F32),
            pltpu.VMEM((8, 32, 128), F32),
            pltpu.VMEM((8, 32, 128), F32),
        ]
        + [pltpu.VMEM((ROWS, 128), F32)] * 5
        + [
            dma,
            dma((2,)),
            dma((6,)),
            dma((2, 6)),
            dma((8,)),
            dma((8,)),
            dma((8,)),
            dma((8,)),
        ],
        compiler_params=pltpu.CompilerParams(
            collective_id=0, has_side_effects=True, vmem_limit_bytes=50 * 1024 * 1024
        ),
    )(
        source.reshape(128, 256),
        storage.reshape(128, 256),
        gbf,
        gbm,
        sbf,
        sbm,
    )
    return result.reshape(source.shape)


def solution(mesh):
    in_specs = (
        P("grp", "gx", "gy", None),
        P("grp", "gx", "gy", None),
        P(("gx", "gy"), None),
        P(("gx", "gy")),
        P(("gx", "gy"), None),
        P(("gx", "gy"), None),
    )
    return jax.shard_map(
        per_device, mesh=mesh, in_specs=in_specs, out_specs=P("grp", "gx", "gy", None), check_vma=False
    )
```

```python
import jax
import jax.numpy as jnp
from jax import lax
from jax.experimental import pallas as pl
from jax.experimental.pallas import tpu as pltpu
from jax.sharding import PartitionSpec as P

TF = 2.0
TI = 1.0
TM = 0.5
LMIN = 0.3
LMAX = 3.0
STEPS = 7

ROWS = 512
PEERS = 32
MSG = 48

F32 = jnp.float32
BF16 = jnp.bfloat16
I32 = jnp.int32
MESH = pl.DeviceIdType.MESH


def coefficients():
    theta = (LMAX + LMIN) / 2.0
    delta = (LMAX - LMIN) / 2.0
    sigma = theta / delta
    rho = 1.0 / sigma
    pairs = []
    for _ in range(3):
        rho_new = 1.0 / (2.0 * sigma - rho)
        pairs.append((rho_new * rho, 2.0 * rho_new / delta))
        rho = rho_new
    pairs.append((0.0, 1.0 / theta))
    return pairs, theta


def turn(x, shift):
    shift = shift % 128
    return x if shift == 0 else pltpu.roll(x, shift, 1)


def lanes(rows):
    return lax.broadcasted_iota(I32, (rows, 128), 1)


def kernel(
    src, sto, tab, out,
    gf, gm, sf, sm, wf, wm, rf, rm,
    send, recv, hs, hz, ys, hy, hx,
    tx, rx, tx2, rx2, mo, mi, vs,
    d_ref, r_ref, p_ref, c_ref, i_ref,
    send_sem, recv_sem, hsend_sem, hrecv_sem, tsend_sem, trecv_sem, usend_sem, urecv_sem, msend_sem, mrecv_sem,
):
    g = lax.axis_index("grp")
    gx = lax.axis_index("gx")
    gy = lax.axis_index("gy")
    x_hi = gx // 16
    cz = (gx // 2) % 8
    core = gx % 2
    w = x_hi * 4 + g * 2 + core

    def place(w_, y_, z_):
        return ((w_ // 2) % 2, (w_ // 4) * 16 + z_ * 2 + w_ % 2, y_)

    def peer(k):
        return place((w + k // 4) % 8, (gy + k % 4) % 4, cz)

    w_home = gx // 4
    u_home = gx % 4
    own = w_home == w

    barrier = pltpu.get_barrier_semaphore()

    def greet(device):
        pl.semaphore_signal(barrier, inc=1, device_id=device, device_id_type=MESH)

    def greet_peer(k, carry):
        greet(peer(k))
        return carry

    lax.fori_loop(1, PEERS, greet_peer, 0)
    greet(place(w, gy, (cz + 1) % 8))
    greet(place(w, gy, (cz + 7) % 8))

    def greet_far(n, carry):
        @pl.when(jnp.logical_not(own & (n == cz)))
        def _():
            greet(place(w_home, gy, n))

        @pl.when(jnp.logical_not(own & (n == g * 4 + u_home)))
        def _():
            greet((n // 4, w * 4 + n % 4, gy))

        return carry

    lax.fori_loop(0, 8, greet_far, 0)

    l32 = lanes(32)
    for z in range(8):
        half, part = z // 4, z % 4
        for a, ref in ((0, src), (1, sto)):
            acc = jnp.zeros((32, 128), F32)
            for q in range(4):
                piece = ref[q * 32:(q + 1) * 32, half * 128:(half + 1) * 128]
                acc = jnp.where(l32 // 32 == q, turn(piece, 32 * (q - part)), acc)
            tx[z, a * 32:(a + 1) * 32, :] = acc
        tx[z, 64:72, :] = tab[...]

    pl.semaphore_wait(barrier, PEERS - 1 + 2 + jnp.where(own, 14, 16))

    def far_copy(z):
        return pltpu.make_async_remote_copy(
            src_ref=tx.at[z],
            dst_ref=rx.at[g * 4 + u_home],
            send_sem=tsend_sem.at[z],
            recv_sem=trecv_sem.at[g * 4 + u_home],
            device_id=place(w_home, gy, z),
            device_id_type=MESH,
        )

    def far_start(z, carry):
        mine = own & (z == cz)

        @pl.when(mine)
        def _():
            rx[g * 4 + u_home] = tx[z]

        @pl.when(jnp.logical_not(mine))
        def _():
            far_copy(z).start()

        return carry

    lax.fori_loop(0, 8, far_start, 0)

    def far_wait(n, carry):
        mine = own & (n == g * 4 + u_home)

        @pl.when(jnp.logical_not(mine))
        def _():
            pltpu.make_async_copy(rx.at[n], rx.at[n], trecv_sem.at[n]).wait()

        @pl.when(jnp.logical_not(own & (n == cz)))
        def _():
            pltpu.make_async_copy(tx.at[n], tx.at[n], tsend_sem.at[n]).wait()

        return carry

    lax.fori_loop(0, 8, far_wait, 0)

    lane1 = lax.broadcasted_iota(I32, (1, 128), 1)
    ub1 = lane1 // 32
    ua1 = lane1 % 32 // 8
    t1 = lane1 % 8
    k32 = lax.broadcasted_iota(I32, (32, 128), 0)
    table = rx[0:4, 64:72, :].reshape(32, 128)
    table = jnp.concatenate([table] * 4, axis=0)
    first_of = ((w + k32 // 4) % 8) * 16 + (gy + k32 % 4) % 4
    outgoing = jnp.zeros((32, 128), F32)
    for ub in range(4):
        chosen = jnp.where(first_of + ub * 4 == l32, 1.0, 0.0)
        x = lax.dot_general(
            chosen, table, (((1,), (1,)), ((), ())),
            precision=lax.Precision.HIGHEST, preferred_element_type=F32,
        )
        outgoing = jnp.where(ub1 == ub, x, outgoing)
    mo[...] = jnp.broadcast_to(outgoing[:, None, :], (32, 8, 128)).reshape(256, 128)
    mi[0:8] = mo[0:8]

    def edge_send(k, carry):
        at = pl.multiple_of(k * 8, 8)
        pltpu.make_async_remote_copy(
            src_ref=mo.at[pl.ds(at, 8)],
            dst_ref=mi.at[pl.ds(at, 8)],
            send_sem=msend_sem,
            recv_sem=mrecv_sem,
            device_id=peer(k),
            device_id_type=MESH,
        ).start()
        return carry

    lax.fori_loop(1, PEERS, edge_send, 0)

    ln = lanes(ROWS)
    group = ln // 32
    is_f = ln < 32
    is_m = group == 1

    pairs, theta = coefficients()
    for a, ref in ((0, r_ref), (1, c_ref)):
        for u in range(4):
            fr = rx[4 + u, a * 32:(a + 1) * 32, :]
            ma = rx[u, a * 32:(a + 1) * 32, :]
            for q in range(4):
                ref[u * 128 + q * 32:u * 128 + (q + 1) * 32, :] = jnp.where(
                    l32 < 32,
                    turn(fr, -32 * q),
                    jnp.where(l32 // 32 == 1, turn(ma, 32 - 32 * q), 0.0),
                )
    stored = c_ref[...]
    inverse = 1.0 / (stored + jnp.where(is_f, 4.0 * TF + 4.0 * TI + TM, 6.0 + TM))
    i_ref[...] = inverse
    c_ref[...] = stored
    d_ref[...] = r_ref[...] * inverse * (1.0 / theta)
    p_ref[...] = jnp.zeros((ROWS, 128), F32)

    pltpu.make_async_copy(mi.at[pl.ds(8, 248)], mi.at[pl.ds(8, 248)], mrecv_sem).wait()
    incoming = mi[pl.ds(0, 32, stride=8), :]
    mirror = ((8 - k32 // 4) % 8) * 4 + (4 - k32 % 4) % 4
    mirror = jnp.where(mirror == l32, 1.0, 0.0)[:, :32]

    def mirrored(x):
        return jnp.dot(mirror, x, precision=lax.Precision.HIGHEST, preferred_element_type=F32)

    def source_row(x):
        x = x.astype(I32)
        return jnp.where(x > 0, ua1 * 128 + ((x - 1) >> 7) + 1, 0)

    def target_row(x):
        x = x.astype(I32)
        return jnp.where(x > 0, ub1 * 128 + ((x - 1) & 127) + 1, 0)

    vs[0] = source_row(outgoing)
    vs[1] = target_row(mirrored(incoming))
    vs[2] = target_row(incoming)
    vs[3] = source_row(mirrored(outgoing))

    inter_at = jnp.where(t1 < 4, ua1 * 4 + ub1, -100)
    host_at = jnp.where((t1 == 4) | (t1 == 5), ua1 * 2 + t1 - 4, -100)
    out_at = jnp.maximum(inter_at + 8, host_at)
    back_at = jnp.maximum(inter_at + 16, host_at + 32)
    i80 = lax.broadcasted_iota(I32, (80, 128), 0)
    first80 = i80 < 40
    i80 = i80 % 40
    i16 = lax.broadcasted_iota(I32, (16, 128), 0)
    first16 = i16 < 8
    i16 = i16 % 8
    ql = lax.broadcasted_iota(I32, (256, 512), 0)
    qt = ql % 8
    qh = jnp.where(qt < 4, qt, (ql % 128) // 32)
    q_rep = jnp.where(
        lax.broadcasted_iota(I32, (256, 512), 1) // 128 == qh, jnp.where(ql < 128, 32.0, 1.0), 0.0
    ).astype(BF16)
    ql = lax.broadcasted_iota(I32, (16, 256), 1)
    qt = ql % 8
    qh = jnp.where(qt < 4, qt, (ql % 128) // 32)
    q_row = jnp.where(
        lax.broadcasted_iota(I32, (16, 256), 0) == qh, jnp.where(ql < 128, 32.0, 1.0), 0.0
    ).astype(BF16)

    def halves(x):
        return jnp.concatenate([(x >> 5).astype(F32), (x & 31).astype(F32)], axis=1).astype(BF16)

    def build_g(j, carry):
        def pair(n, first):
            return jnp.where(first, vs[n, pl.ds(2 * j, 1), :], vs[n, pl.ds(2 * j + 1, 1), :])

        at = pl.multiple_of(j * 80, 80)
        x = jnp.where(i80 == out_at, pair(0, first80), 0)
        x = x + jnp.where(i80 == inter_at + 24, pair(1, first80), 0)
        rows = jnp.dot(halves(x), q_rep, preferred_element_type=F32).astype(I32)
        for q in range(4):
            for c in range(4):
                hit = rows[:, q * 128:(q + 1) * 128] == lane1 + (c * 128 + 1)
                gf[pl.ds(at, 80), q * ROWS + c * 128:q * ROWS + (c + 1) * 128] = jnp.where(
                    hit, 1.0, 0.0
                ).astype(BF16)
        x = jnp.where(i80 == inter_at, pair(2, first80), 0)
        x = x + jnp.where(i80 == back_at, pair(3, first80), 0)
        rf[pl.ds(at, 80), :] = halves(x)
        at = pl.multiple_of(j * 16, 16)
        x = jnp.where(i16 == host_at, pair(1, first16), 0)
        rows = jnp.dot(halves(x), q_rep, preferred_element_type=F32).astype(I32)
        for q in range(4):
            for c in range(4):
                hit = rows[:, q * 128:(q + 1) * 128] == lane1 + (c * 128 + 1)
                gm[pl.ds(at, 16), q * ROWS + c * 128:q * ROWS + (c + 1) * 128] = jnp.where(
                    hit, 1.0, 0.0
                ).astype(BF16)
        rm[pl.ds(at, 16), :] = halves(jnp.where(i16 == host_at, pair(2, first16), 0))
        return carry

    lax.fori_loop(0, 16, build_g, 0)

    across = (((1,), (1,)), ((), ()))
    sbf = lax.dot_general(q_row, rf[...], across, preferred_element_type=F32).astype(I32)
    sbm = lax.dot_general(q_row, rm[...], across, preferred_element_type=F32).astype(I32)
    within = lax.broadcasted_iota(I32, (1, 1280), 1) % 40
    weight = jnp.where(within < 32, TI, TM)

    def build_s(j, carry):
        at = pl.multiple_of(j * 16, 16)
        block = lax.broadcasted_iota(I32, (16, 1280), 0) + (at + 1)
        for q in range(4):
            sf[pl.ds(at + q * ROWS, 16), :] = jnp.where(sbf[q:q + 1, :] == block, weight, 0.0).astype(BF16)
            sm[pl.ds(at + q * ROWS, 16), :] = jnp.where(
                sbm[q:q + 1, :] == block[:, :256], TM, 0.0
            ).astype(BF16)
        return carry

    lax.fori_loop(0, 32, build_s, 0)

    entering = jnp.where(lax.broadcasted_iota(I32, (1280, 128), 0) % 40 < 16, 1.0, 0.0).astype(BF16)
    ones = jnp.ones((256, 128), BF16)
    indeg = jnp.zeros((ROWS, 128), F32)
    hosted = jnp.zeros((ROWS, 128), F32)
    for q in range(4):
        indeg = indeg + jnp.dot(sf[q * ROWS:(q + 1) * ROWS, :], entering, preferred_element_type=F32)
        hosted = hosted + jnp.dot(sm[q * ROWS:(q + 1) * ROWS, :], ones, preferred_element_type=F32)

    c_ref[...] = c_ref[...] + jnp.where(is_f, 4.0 * TF + 2.0 * TI + TM + indeg, 6.0 + hosted)
    pltpu.make_async_copy(mo.at[pl.ds(8, 248)], mo.at[pl.ds(8, 248)], msend_sem).wait()

    low = jnp.where(cz > 0, 1.0, 0.0)
    high = jnp.where(cz < 7, 1.0, 0.0)
    left = jnp.where(w > 0, 1.0, 0.0)
    right = jnp.where(w < 7, 1.0, 0.0)
    near = jnp.where(gy > 0, 1.0, 0.0)
    beyond = jnp.where(gy < 3, 1.0, 0.0)
    l128 = lanes(128)

    def packed(x):
        acc = x[0:128]
        for q in range(1, 4):
            acc = jnp.where(l128 // 32 == q, turn(x[q * 128:(q + 1) * 128], 32 * q), acc)
        return acc

    def unpacked(x):
        return jnp.concatenate([turn(x, -32 * q) for q in range(4)], axis=0)

    def step(t, carry):
        par = t % 2

        def halo(n, source, dest, device):
            return pltpu.make_async_remote_copy(
                src_ref=source,
                dst_ref=dest,
                send_sem=hsend_sem.at[n],
                recv_sem=hrecv_sem.at[par, n],
                device_id=device,
                device_id_type=MESH,
            )

        halos = [
            halo(0, hs.at[0], hz.at[par, 0], place(w, gy, (cz + 1) % 8)),
            halo(1, hs.at[1], hz.at[par, 1], place(w, gy, (cz + 7) % 8)),
            halo(2, ys.at[1], hy.at[par, 0], place(w, (gy + 1) % 4, cz)),
            halo(3, ys.at[0], hy.at[par, 1], place(w, (gy + 3) % 4, cz)),
            halo(4, d_ref.at[pl.ds(ROWS - 8, 8)], hx.at[par, 0], place((w + 1) % 8, gy, cz)),
            halo(5, d_ref.at[pl.ds(0, 8)], hx.at[par, 1], place((w + 7) % 8, gy, cz)),
        ]
        d = d_ref[...]
        high_part = d.astype(BF16).astype(F32)
        low_part = d - high_part
        for s in range(4):
            for part, x in ((0, turn(high_part, 32 * s)), (1, turn(low_part, 32 * s))):
                q = (s + 1) % 4
                wf[s * ROWS:(s + 1) * ROWS, part * 128:(part + 1) * 128] = jnp.where(
                    group == s, x, 0.0
                ).astype(BF16)
                wm[q * ROWS:(q + 1) * ROWS, part * 128:(part + 1) * 128] = jnp.where(
                    group == q, x, 0.0
                ).astype(BF16)

        def message(k):
            return pltpu.make_async_remote_copy(
                src_ref=send.at[k],
                dst_ref=recv.at[par, k],
                send_sem=send_sem,
                recv_sem=recv_sem.at[par],
                device_id=peer(k),
                device_id_type=MESH,
            )

        def gather(c, carry):
            at = pl.multiple_of(c * 320, 320)
            x = jnp.dot(gf[pl.ds(at, 320), :], wf[...], preferred_element_type=F32)
            send[pl.ds(c * 8, 8), 0:40, :] = (x[:, :128] + x[:, 128:]).reshape(8, 40, 128)
            at = pl.multiple_of(c * 64, 64)
            x = jnp.dot(gm[pl.ds(at, 64), :], wm[...], preferred_element_type=F32)
            send[pl.ds(c * 8, 8), 40:48, :] = (x[:, :128] + x[:, 128:]).reshape(8, 8, 128)
            for n in range(8):
                k = c * 8 + n
                if n == 0:
                    @pl.when(c > 0)
                    def _():
                        message(k).start()
                else:
                    message(k).start()
            return carry

        hs[0] = packed(jnp.where(ln < 16, turn(d, -16), turn(d, -47)))
        hs[1] = packed(jnp.where(ln < 16, d, turn(d, -16)))
        ys[0] = d_ref[pl.ds(0, 64, stride=8), :]
        ys[1] = d_ref[pl.ds(7, 64, stride=8), :]
        for copy in halos:
            copy.start()
        lax.fori_loop(0, 4, gather, 0)
        recv[par, 0] = send[0]

        col = ln % 16
        before = turn(d, 1)
        after = turn(d, -1)
        nb_f = jnp.where(col != 0, before, 0.0) + jnp.where(col != 15, after, 0.0)
        nb_f = nb_f + jnp.where(ln >= 16, turn(d, 16), 0.0) + jnp.where(ln < 16, turn(d, -16), 0.0)
        nb_m = jnp.where(ln != 32, before, 0.0) + jnp.where(ln != 63, after, 0.0)
        nb_m = nb_m + jnp.concatenate([jnp.zeros((8, 128), F32), d[:ROWS - 8]], axis=0)
        nb_m = nb_m + jnp.concatenate([d[8:], jnp.zeros((8, 128), F32)], axis=0)
        sub = lax.broadcasted_iota(I32, (ROWS, 128), 0) % 8
        nb_m = nb_m + jnp.where(sub != 0, pltpu.roll(d, 1, 0), 0.0)
        nb_m = nb_m + jnp.where(sub != 7, pltpu.roll(d, ROWS - 1, 0), 0.0)
        for copy in halos:
            copy.wait_recv()
        from_low = unpacked(hz[par, 0]) * low
        from_high = unpacked(hz[par, 1]) * high
        nb_f = nb_f + jnp.where(ln < 16, from_low, turn(from_high, 16))
        nb_m = nb_m + jnp.where(ln == 32, turn(from_low, 16), 0.0)
        nb_m = nb_m + jnp.where(ln == 63, turn(from_high, 47), 0.0)
        y0 = jnp.broadcast_to((hy[par, 0] * near)[:, None, :], (64, 8, 128)).reshape(ROWS, 128)
        y1 = jnp.broadcast_to((hy[par, 1] * beyond)[:, None, :], (64, 8, 128)).reshape(ROWS, 128)
        nb_m = nb_m + jnp.where(sub == 0, y0, 0.0) + jnp.where(sub == 7, y1, 0.0)
        nb_m = nb_m + jnp.concatenate(
            [hx[par, 0] * left, jnp.zeros((ROWS - 16, 128), F32), hx[par, 1] * right], axis=0
        )
        nb = jnp.where(is_f, TF * nb_f, jnp.where(is_m, nb_m, 0.0))
        p_ref[...] = p_ref[...] + d
        r_ref[...] = r_ref[...] - (c_ref[...] * d - nb)

        pltpu.make_async_copy(
            recv.at[par, pl.ds(1, PEERS - 1)], recv.at[par, pl.ds(1, PEERS - 1)], recv_sem.at[par]
        ).wait()
        x = recv[par, :, 8:48, :].reshape(1280, 128)
        hi = x.astype(BF16)
        rf[:, 0:128] = hi
        rf[:, 128:256] = (x - hi.astype(F32)).astype(BF16)
        x = recv[par, :, 0:8, :].reshape(256, 128)
        hi = x.astype(BF16)
        rm[:, 0:128] = hi
        rm[:, 128:256] = (x - hi.astype(F32)).astype(BF16)
        sum_f = jnp.zeros((ROWS, 128), F32)
        sum_m = jnp.zeros((ROWS, 128), F32)
        for q in range(4):
            x = jnp.dot(sf[q * ROWS:(q + 1) * ROWS, :], rf[...], preferred_element_type=F32)
            sum_f = jnp.where(group == q, x[:, :128] + x[:, 128:], sum_f)
            x = jnp.dot(sm[q * ROWS:(q + 1) * ROWS, :], rm[...], preferred_element_type=F32)
            sum_m = jnp.where(group == q, x[:, :128] + x[:, 128:], sum_m)
        sum_f = sum_f + turn(sum_f, 64)
        sum_f = sum_f + turn(sum_f, 32)
        sum_m = sum_m + turn(sum_m, 64)
        sum_m = sum_m + turn(sum_m, 32)
        total = jnp.where(is_f, sum_f, jnp.where(is_m, sum_m, 0.0))

        for copy in halos:
            copy.wait_send()
        pltpu.make_async_copy(
            send.at[pl.ds(1, PEERS - 1)], send.at[pl.ds(1, PEERS - 1)], send_sem
        ).wait()
        phase = t % 4
        alpha = jnp.float32(pairs[3][0])
        beta = jnp.float32(pairs[3][1])
        for n in range(3):
            alpha = jnp.where(phase == n, jnp.float32(pairs[n][0]), alpha)
            beta = jnp.where(phase == n, jnp.float32(pairs[n][1]), beta)
        r = r_ref[...] + total
        r_ref[...] = r
        d_ref[...] = alpha * d_ref[...] + beta * (r * i_ref[...])
        return carry

    lax.fori_loop(0, STEPS, step, 0)

    for n in range(8):
        acc = jnp.zeros((32, 128), F32)
        for q in range(4):
            at = (n % 4) * 128 + q * 32
            piece = p_ref[at:at + 32, :] + d_ref[at:at + 32, :]
            acc = jnp.where(l32 // 32 == q, turn(piece, 32 * q - (32 if n < 4 else 0)), acc)
        tx2[n] = acc

    def back_start(n, carry):
        mine = own & (n == g * 4 + u_home)

        @pl.when(mine)
        def _():
            rx2[cz] = tx2[n]

        @pl.when(jnp.logical_not(mine))
        def _():
            pltpu.make_async_remote_copy(
                src_ref=tx2.at[n],
                dst_ref=rx2.at[cz],
                send_sem=usend_sem.at[n],
                recv_sem=urecv_sem.at[cz],
                device_id=(n // 4, w * 4 + n % 4, gy),
                device_id_type=MESH,
            ).start()

        return carry

    lax.fori_loop(0, 8, back_start, 0)

    def back_wait(n, carry):
        @pl.when(jnp.logical_not(own & (n == cz)))
        def _():
            pltpu.make_async_copy(rx2.at[n], rx2.at[n], urecv_sem.at[n]).wait()

        @pl.when(jnp.logical_not(own & (n == g * 4 + u_home)))
        def _():
            pltpu.make_async_copy(tx2.at[n], tx2.at[n], usend_sem.at[n]).wait()

        return carry

    lax.fori_loop(0, 8, back_wait, 0)
    for half in range(2):
        for q in range(4):
            acc = jnp.zeros((32, 128), F32)
            for part in range(4):
                acc = jnp.where(l32 // 32 == part, turn(rx2[half * 4 + part], 32 * (part - q)), acc)
            out[q * 32:(q + 1) * 32, half * 128:(half + 1) * 128] = acc


def edge_table(dest, where_to, per_row, most):
    count = dest.shape[0]
    order = jnp.arange(count, dtype=I32)
    same = (dest[:, None] == dest[None, :]) & (order[None, :] < order[:, None])
    rank = jnp.sum(same.astype(I32), axis=1)
    code = 1 + (order // per_row) * 128 + where_to
    key = rank * 128 + dest
    wanted = jnp.arange(most * 128, dtype=I32)
    return jnp.sum(jnp.where(key[None, :] == wanted[:, None], code[None, :], 0), axis=1).reshape(most, 128)


def per_device(source, storage, host_device, host_column, inter_device, inter_slot):
    table = jnp.concatenate(
        [
            edge_table(inter_device.reshape(-1), inter_slot.reshape(-1), 2, 4),
            edge_table(host_device.reshape(-1), host_column, 1, 2),
            jnp.zeros((2, 128), I32),
        ],
        axis=0,
    ).astype(F32)
    dma = pltpu.SemaphoreType.DMA
    result = pl.pallas_call(
        kernel,
        out_shape=jax.ShapeDtypeStruct((128, 256), F32),
        in_specs=[pl.BlockSpec(memory_space=pltpu.VMEM)] * 3,
        out_specs=pl.BlockSpec(memory_space=pltpu.VMEM),
        scratch_shapes=[
            pltpu.VMEM((1280, 2048), BF16),
            pltpu.VMEM((256, 2048), BF16),
            pltpu.VMEM((2048, 1280), BF16),
            pltpu.VMEM((2048, 256), BF16),
            pltpu.VMEM((2048, 256), BF16),
            pltpu.VMEM((2048, 256), BF16),
            pltpu.VMEM((1280, 256), BF16),
            pltpu.VMEM((256, 256), BF16),
            pltpu.VMEM((PEERS, MSG, 128), F32),
            pltpu.VMEM((2, PEERS, MSG, 128), F32),
            pltpu.VMEM((2, 128, 128), F32),
            pltpu.VMEM((2, 2, 128, 128), F32),
            pltpu.VMEM((2, 64, 128), F32),
            pltpu.VMEM((2, 2, 64, 128), F32),
            pltpu.VMEM((2, 2, 8, 128), F32),
            pltpu.VMEM((8, 72, 128), F32),
            pltpu.VMEM((8, 72, 128), F32),
            pltpu.VMEM((8, 32, 128), F32),
            pltpu.VMEM((8, 32, 128), F32),
            pltpu.VMEM((256, 128), F32),
            pltpu.VMEM((256, 128), F32),
            pltpu.VMEM((4, 32, 128), I32),
        ]
        + [pltpu.VMEM((ROWS, 128), F32)] * 5
        + [
            dma,
            dma((2,)),
            dma((6,)),
            dma((2, 6)),
            dma((8,)),
            dma((8,)),
            dma((8,)),
            dma((8,)),
            dma,
            dma,
        ],
        compiler_params=pltpu.CompilerParams(
            collective_id=0, has_side_effects=True, vmem_limit_bytes=50 * 1024 * 1024
        ),
    )(
        source.reshape(128, 256),
        storage.reshape(128, 256),
        table,
    )
    return result.reshape(source.shape)


def solution(mesh):
    in_specs = (
        P("grp", "gx", "gy", None),
        P("grp", "gx", "gy", None),
        P(("gx", "gy"), None),
        P(("gx", "gy")),
        P(("gx", "gy"), None),
        P(("gx", "gy"), None),
    )
    return jax.shard_map(
        per_device, mesh=mesh, in_specs=in_specs, out_specs=P("grp", "gx", "gy", None), check_vma=False
    )
```

```python
import jax
import jax.numpy as jnp
from jax import lax
from jax.experimental import pallas as pl
from jax.experimental.pallas import tpu as pltpu
from jax.sharding import PartitionSpec as P

TF = 2.0
TI = 1.0
TM = 0.5
LMIN = 0.3
LMAX = 3.0
STEPS = 7

ROWS = 512
PEERS = 32
MSG = 48

F32 = jnp.float32
BF16 = jnp.bfloat16
I32 = jnp.int32
MESH = pl.DeviceIdType.MESH


def coefficients():
    theta = (LMAX + LMIN) / 2.0
    delta = (LMAX - LMIN) / 2.0
    sigma = theta / delta
    rho = 1.0 / sigma
    pairs = []
    for _ in range(3):
        rho_new = 1.0 / (2.0 * sigma - rho)
        pairs.append((rho_new * rho, 2.0 * rho_new / delta))
        rho = rho_new
    pairs.append((0.0, 1.0 / theta))
    return pairs, theta


def turn(x, shift):
    shift = shift % 128
    return x if shift == 0 else pltpu.roll(x, shift, 1)


def lanes(rows):
    return lax.broadcasted_iota(I32, (rows, 128), 1)


def kernel(
    src, sto, host_dev, host_col, inter_dev, inter_slot, out,
    gf, gm, sf, sm, wf, wm, rf, rm,
    send, recv, hs, hz, ys, hy, hx,
    tx, rx, tx2, rx2, mo, mi, vs, et, er,
    d_ref, r_ref, p_ref, c_ref, i_ref,
    send_sem, recv_sem, hsend_sem, hrecv_sem, tsend_sem, trecv_sem, usend_sem, urecv_sem, msend_sem, mrecv_sem, esend_sem, erecv_sem,
):
    g = lax.axis_index("grp")
    gx = lax.axis_index("gx")
    gy = lax.axis_index("gy")
    x_hi = gx // 16
    cz = (gx // 2) % 8
    core = gx % 2
    w = x_hi * 4 + g * 2 + core

    def place(w_, y_, z_):
        return ((w_ // 2) % 2, (w_ // 4) * 16 + z_ * 2 + w_ % 2, y_)

    def peer(k):
        return place((w + k % 8) % 8, (gy + k // 8 + k % 8) % 4, cz)

    w_home = gx // 4
    u_home = gx % 4
    own = w_home == w

    barrier = pltpu.get_barrier_semaphore()

    def greet(device):
        pl.semaphore_signal(barrier, inc=1, device_id=device, device_id_type=MESH)

    def greet_peer(k, carry):
        greet(peer(k))
        return carry

    lax.fori_loop(1, PEERS, greet_peer, 0)
    greet(place(w, gy, (cz + 1) % 8))
    greet(place(w, gy, (cz + 7) % 8))

    def greet_far(n, carry):
        @pl.when(jnp.logical_not(own & (n == cz)))
        def _():
            greet(place(w_home, gy, n))

        @pl.when(jnp.logical_not(own & (n == g * 4 + u_home)))
        def _():
            greet((n // 4, w * 4 + n % 4, gy))

        return carry

    lax.fori_loop(0, 8, greet_far, 0)

    l128 = lanes(128)
    s128 = lax.broadcasted_iota(I32, (128, 128), 0)
    earlier = jnp.where(l128 < s128, 1.0, 0.0).astype(BF16)

    def column(row):
        return jnp.sum(jnp.where(l128 == s128, row.astype(F32), 0.0), axis=1, keepdims=True)

    edges = jnp.zeros((8, 128), F32)
    s8 = lax.broadcasted_iota(I32, (8, 128), 0)

    def list_edges(edges, devices, rows, base, most):
        before = jnp.zeros((1, 128), F32)
        for dev, row in zip(devices, rows):
            named = column(dev) == l128.astype(F32)
            hit = jnp.where(named, 1.0, 0.0)
            rank = before + jnp.dot(earlier, hit.astype(BF16), preferred_element_type=F32)
            before = before + jnp.sum(hit, axis=0, keepdims=True)
            code = jnp.where(named, column(row) + (1 + 128 * s128).astype(F32), 0.0)
            for r in range(most):
                x = jnp.sum(jnp.where(rank == float(r), code, 0.0), axis=0, keepdims=True)
                edges = edges + jnp.where(s8 == base + r, x, 0.0)
        return edges

    edges = list_edges(
        edges, [inter_dev[0:1, :], inter_dev[1:2, :]], [inter_slot[0:1, :], inter_slot[1:2, :]], 0, 4
    )
    edges = list_edges(edges, [host_dev[...]], [host_col[...]], 4, 2)
    et[...] = edges

    l32 = lanes(32)
    for z in range(8):
        half, part = z // 4, z % 4
        for a, ref in ((0, src), (1, sto)):
            acc = jnp.zeros((32, 128), F32)
            for q in range(4):
                piece = ref[q * 32:(q + 1) * 32, half * 128:(half + 1) * 128]
                acc = jnp.where(l32 // 32 == q, turn(piece, 32 * (q - part)), acc)
            tx[z, a * 32:(a + 1) * 32, :] = acc

    pl.semaphore_wait(barrier, PEERS - 1 + 2 + jnp.where(own, 14, 16))

    def edge_start(z, carry):
        mine = own & (z == cz)

        @pl.when(mine)
        def _():
            er[u_home] = et[...]

        @pl.when(jnp.logical_not(mine))
        def _():
            pltpu.make_async_remote_copy(
                src_ref=et,
                dst_ref=er.at[u_home],
                send_sem=esend_sem.at[z],
                recv_sem=erecv_sem.at[u_home],
                device_id=place(w_home, gy, z),
                device_id_type=MESH,
            ).start()

        return carry

    @pl.when(g == 0)
    def _():
        lax.fori_loop(0, 8, edge_start, 0)

    def far_copy(z):
        return pltpu.make_async_remote_copy(
            src_ref=tx.at[z],
            dst_ref=rx.at[g * 4 + u_home],
            send_sem=tsend_sem.at[z],
            recv_sem=trecv_sem.at[g * 4 + u_home],
            device_id=place(w_home, gy, z),
            device_id_type=MESH,
        )

    def far_start(z, carry):
        mine = own & (z == cz)

        @pl.when(mine)
        def _():
            rx[g * 4 + u_home] = tx[z]

        @pl.when(jnp.logical_not(mine))
        def _():
            far_copy(z).start()

        return carry

    lax.fori_loop(0, 8, far_start, 0)

    def edge_wait(n, carry):
        @pl.when(jnp.logical_not(own & (g == 0) & (n == u_home)))
        def _():
            pltpu.make_async_copy(er.at[n], er.at[n], erecv_sem.at[n]).wait()

        return carry

    lax.fori_loop(0, 4, edge_wait, 0)

    lane1 = lax.broadcasted_iota(I32, (1, 128), 1)
    ub1 = lane1 // 32
    ua1 = lane1 % 32 // 8
    t1 = lane1 % 8
    k32 = lax.broadcasted_iota(I32, (32, 128), 0)
    table = er[...].reshape(32, 128)
    table = jnp.concatenate([table] * 4, axis=0)
    first_of = ((w + k32 % 8) % 8) * 16 + (gy + k32 // 8 + k32 % 8) % 4
    outgoing = jnp.zeros((32, 128), F32)
    for ub in range(4):
        chosen = jnp.where(first_of + ub * 4 == l32, 1.0, 0.0)
        x = lax.dot_general(
            chosen, table, (((1,), (1,)), ((), ())),
            precision=lax.Precision.HIGHEST, preferred_element_type=F32,
        )
        outgoing = jnp.where(ub1 == ub, x, outgoing)
    mo[...] = jnp.broadcast_to(outgoing[:, None, :], (32, 8, 128)).reshape(256, 128)
    mi[0:8] = mo[0:8]

    def edge_send(k, carry):
        at = pl.multiple_of(k * 8, 8)
        pltpu.make_async_remote_copy(
            src_ref=mo.at[pl.ds(at, 8)],
            dst_ref=mi.at[pl.ds(at, 8)],
            send_sem=msend_sem,
            recv_sem=mrecv_sem,
            device_id=peer(k),
            device_id_type=MESH,
        ).start()
        return carry

    lax.fori_loop(1, PEERS, edge_send, 0)

    pltpu.make_async_copy(mi.at[pl.ds(8, 248)], mi.at[pl.ds(8, 248)], mrecv_sem).wait()
    incoming = mi[pl.ds(0, 32, stride=8), :]
    mirror_w = (8 - k32 % 8) % 8
    mirror = mirror_w + 8 * ((16 - k32 // 8 - k32 % 8 - mirror_w) % 4)
    mirror = jnp.where(mirror == l32, 1.0, 0.0)[:, :32]

    def mirrored(x):
        return jnp.dot(mirror, x, precision=lax.Precision.HIGHEST, preferred_element_type=F32)

    def source_row(x):
        x = x.astype(I32)
        return jnp.where(x > 0, ua1 * 128 + ((x - 1) >> 7) + 1, 0)

    def target_row(x):
        x = x.astype(I32)
        return jnp.where(x > 0, ub1 * 128 + ((x - 1) & 127) + 1, 0)

    vs[0] = source_row(outgoing)
    vs[1] = target_row(mirrored(incoming))
    vs[2] = target_row(incoming)
    vs[3] = source_row(mirrored(outgoing))

    inter_at = jnp.where(t1 < 4, ua1 * 4 + ub1, -100)
    host_at = jnp.where((t1 == 4) | (t1 == 5), ua1 * 2 + t1 - 4, -100)
    out_at = jnp.maximum(inter_at + 8, host_at)
    back_at = jnp.maximum(inter_at + 16, host_at + 32)
    i80 = lax.broadcasted_iota(I32, (80, 128), 0)
    first80 = i80 < 40
    i80 = i80 % 40
    i16 = lax.broadcasted_iota(I32, (16, 128), 0)
    first16 = i16 < 8
    i16 = i16 % 8
    ql = lax.broadcasted_iota(I32, (256, 512), 0)
    qt = ql % 8
    qh = jnp.where(qt < 4, qt, (ql % 128) // 32)
    q_rep = jnp.where(
        lax.broadcasted_iota(I32, (256, 512), 1) // 128 == qh, jnp.where(ql < 128, 32.0, 1.0), 0.0
    ).astype(BF16)
    ql = lax.broadcasted_iota(I32, (16, 256), 1)
    qt = ql % 8
    qh = jnp.where(qt < 4, qt, (ql % 128) // 32)
    q_row = jnp.where(
        lax.broadcasted_iota(I32, (16, 256), 0) == qh, jnp.where(ql < 128, 32.0, 1.0), 0.0
    ).astype(BF16)

    def halves(x):
        return jnp.concatenate([(x >> 5).astype(F32), (x & 31).astype(F32)], axis=1).astype(BF16)

    def build_g(j, carry):
        def pair(n, first):
            return jnp.where(first, vs[n, pl.ds(2 * j, 1), :], vs[n, pl.ds(2 * j + 1, 1), :])

        at = pl.multiple_of(j * 80, 80)
        x = jnp.where(i80 == out_at, pair(0, first80), 0)
        x = x + jnp.where(i80 == inter_at + 24, pair(1, first80), 0)
        rows = jnp.dot(halves(x), q_rep, preferred_element_type=F32).astype(I32)
        for q in range(4):
            for c in range(4):
                hit = rows[:, q * 128:(q + 1) * 128] == lane1 + (c * 128 + 1)
                gf[pl.ds(at, 80), q * ROWS + c * 128:q * ROWS + (c + 1) * 128] = jnp.where(
                    hit, 1.0, 0.0
                ).astype(BF16)
        x = jnp.where(i80 == inter_at, pair(2, first80), 0)
        x = x + jnp.where(i80 == back_at, pair(3, first80), 0)
        rf[pl.ds(at, 80), :] = halves(x)
        at = pl.multiple_of(j * 16, 16)
        x = jnp.where(i16 == host_at, pair(1, first16), 0)
        rows = jnp.dot(halves(x), q_rep, preferred_element_type=F32).astype(I32)
        for q in range(4):
            for c in range(4):
                hit = rows[:, q * 128:(q + 1) * 128] == lane1 + (c * 128 + 1)
                gm[pl.ds(at, 16), q * ROWS + c * 128:q * ROWS + (c + 1) * 128] = jnp.where(
                    hit, 1.0, 0.0
                ).astype(BF16)
        rm[pl.ds(at, 16), :] = halves(jnp.where(i16 == host_at, pair(2, first16), 0))
        return carry

    lax.fori_loop(0, 16, build_g, 0)

    across = (((1,), (1,)), ((), ()))
    sbf = lax.dot_general(q_row, rf[...], across, preferred_element_type=F32).astype(I32)
    sbm = lax.dot_general(q_row, rm[...], across, preferred_element_type=F32).astype(I32)
    within = lax.broadcasted_iota(I32, (1, 1280), 1) % 40
    weight = jnp.where(within < 32, TI, TM)

    def build_s(j, carry):
        at = pl.multiple_of(j * 16, 16)
        block = lax.broadcasted_iota(I32, (16, 1280), 0) + (at + 1)
        for q in range(4):
            sf[pl.ds(at + q * ROWS, 16), :] = jnp.where(sbf[q:q + 1, :] == block, weight, 0.0).astype(BF16)
            sm[pl.ds(at + q * ROWS, 16), :] = jnp.where(
                sbm[q:q + 1, :] == block[:, :256], TM, 0.0
            ).astype(BF16)
        return carry

    lax.fori_loop(0, 32, build_s, 0)

    def far_wait(n, carry):
        mine = own & (n == g * 4 + u_home)

        @pl.when(jnp.logical_not(mine))
        def _():
            pltpu.make_async_copy(rx.at[n], rx.at[n], trecv_sem.at[n]).wait()

        @pl.when(jnp.logical_not(own & (n == cz)))
        def _():
            pltpu.make_async_copy(tx.at[n], tx.at[n], tsend_sem.at[n]).wait()

        return carry

    lax.fori_loop(0, 8, far_wait, 0)

    ln = lanes(ROWS)
    group = ln // 32
    is_f = ln < 32
    is_m = group == 1

    pairs, theta = coefficients()
    for a, ref in ((0, r_ref), (1, c_ref)):
        for u in range(4):
            fr = rx[4 + u, a * 32:(a + 1) * 32, :]
            ma = rx[u, a * 32:(a + 1) * 32, :]
            for q in range(4):
                ref[u * 128 + q * 32:u * 128 + (q + 1) * 32, :] = jnp.where(
                    l32 < 32,
                    turn(fr, -32 * q),
                    jnp.where(l32 // 32 == 1, turn(ma, 32 - 32 * q), 0.0),
                )
    stored = c_ref[...]
    inverse = 1.0 / (stored + jnp.where(is_f, 4.0 * TF + 4.0 * TI + TM, 6.0 + TM))
    i_ref[...] = inverse
    c_ref[...] = stored
    d_ref[...] = r_ref[...] * inverse * (1.0 / theta)
    p_ref[...] = jnp.zeros((ROWS, 128), F32)

    entering = jnp.where(lax.broadcasted_iota(I32, (1280, 128), 0) % 40 < 16, 1.0, 0.0).astype(BF16)
    ones = jnp.ones((256, 128), BF16)
    indeg = jnp.zeros((ROWS, 128), F32)
    hosted = jnp.zeros((ROWS, 128), F32)
    for q in range(4):
        indeg = indeg + jnp.dot(sf[q * ROWS:(q + 1) * ROWS, :], entering, preferred_element_type=F32)
        hosted = hosted + jnp.dot(sm[q * ROWS:(q + 1) * ROWS, :], ones, preferred_element_type=F32)

    c_ref[...] = c_ref[...] + jnp.where(is_f, 4.0 * TF + 2.0 * TI + TM + indeg, 6.0 + hosted)
    pltpu.make_async_copy(mo.at[pl.ds(8, 248)], mo.at[pl.ds(8, 248)], msend_sem).wait()

    def edge_sent(z, carry):
        @pl.when(jnp.logical_not(own & (z == cz)))
        def _():
            pltpu.make_async_copy(et, et, esend_sem.at[z]).wait()

        return carry

    @pl.when(g == 0)
    def _():
        lax.fori_loop(0, 8, edge_sent, 0)

    low = jnp.where(cz > 0, 1.0, 0.0)
    high = jnp.where(cz < 7, 1.0, 0.0)
    left = jnp.where(w > 0, 1.0, 0.0)
    right = jnp.where(w < 7, 1.0, 0.0)
    near = jnp.where(gy > 0, 1.0, 0.0)
    beyond = jnp.where(gy < 3, 1.0, 0.0)
    def packed(x):
        acc = x[0:128]
        for q in range(1, 4):
            acc = jnp.where(l128 // 32 == q, turn(x[q * 128:(q + 1) * 128], 32 * q), acc)
        return acc

    def unpacked(x):
        return jnp.concatenate([turn(x, -32 * q) for q in range(4)], axis=0)

    def step(t, carry):
        par = t % 2

        def halo(n, source, dest, device):
            return pltpu.make_async_remote_copy(
                src_ref=source,
                dst_ref=dest,
                send_sem=hsend_sem.at[n],
                recv_sem=hrecv_sem.at[par, n],
                device_id=device,
                device_id_type=MESH,
            )

        halos = [
            halo(0, hs.at[0], hz.at[par, 0], place(w, gy, (cz + 1) % 8)),
            halo(1, hs.at[1], hz.at[par, 1], place(w, gy, (cz + 7) % 8)),
            halo(2, ys.at[1], hy.at[par, 0], place(w, (gy + 1) % 4, cz)),
            halo(3, ys.at[0], hy.at[par, 1], place(w, (gy + 3) % 4, cz)),
            halo(4, d_ref.at[pl.ds(ROWS - 8, 8)], hx.at[par, 0], place((w + 1) % 8, gy, cz)),
            halo(5, d_ref.at[pl.ds(0, 8)], hx.at[par, 1], place((w + 7) % 8, gy, cz)),
        ]
        d = d_ref[...]
        high_part = d.astype(BF16).astype(F32)
        low_part = d - high_part
        for s in range(4):
            for part, x in ((0, turn(high_part, 32 * s)), (1, turn(low_part, 32 * s))):
                q = (s + 1) % 4
                wf[s * ROWS:(s + 1) * ROWS, part * 128:(part + 1) * 128] = jnp.where(
                    group == s, x, 0.0
                ).astype(BF16)
                wm[q * ROWS:(q + 1) * ROWS, part * 128:(part + 1) * 128] = jnp.where(
                    group == q, x, 0.0
                ).astype(BF16)

        def message(k, half):
            return pltpu.make_async_remote_copy(
                src_ref=send.at[k],
                dst_ref=recv.at[par, k],
                send_sem=send_sem,
                recv_sem=recv_sem.at[par, half],
                device_id=peer(k),
                device_id_type=MESH,
            )

        def gather(c, carry):
            at = c * 320 if isinstance(c, int) else pl.multiple_of(c * 320, 320)
            x = jnp.dot(gf[pl.ds(at, 320), :], wf[...], preferred_element_type=F32)
            send[pl.ds(c * 8, 8), 0:40, :] = (x[:, :128] + x[:, 128:]).reshape(8, 40, 128)
            at = c * 64 if isinstance(c, int) else pl.multiple_of(c * 64, 64)
            x = jnp.dot(gm[pl.ds(at, 64), :], wm[...], preferred_element_type=F32)
            send[pl.ds(c * 8, 8), 40:48, :] = (x[:, :128] + x[:, 128:]).reshape(8, 8, 128)
            for n in range(8):
                k = c * 8 + n
                if n > 0 or not isinstance(c, int):
                    message(k, c // 2).start()
            return carry

        gather(0, 0)
        hs[0] = packed(jnp.where(ln < 16, turn(d, -16), turn(d, -47)))
        hs[1] = packed(jnp.where(ln < 16, d, turn(d, -16)))
        ys[0] = d_ref[pl.ds(0, 64, stride=8), :]
        ys[1] = d_ref[pl.ds(7, 64, stride=8), :]
        for copy in halos:
            copy.start()
        lax.fori_loop(1, 4, gather, 0)
        recv[par, 0] = send[0]

        col = ln % 16
        before = turn(d, 1)
        after = turn(d, -1)
        nb_f = jnp.where(col != 0, before, 0.0) + jnp.where(col != 15, after, 0.0)
        nb_f = nb_f + jnp.where(ln >= 16, turn(d, 16), 0.0) + jnp.where(ln < 16, turn(d, -16), 0.0)
        nb_m = jnp.where(ln != 32, before, 0.0) + jnp.where(ln != 63, after, 0.0)
        nb_m = nb_m + jnp.concatenate([jnp.zeros((8, 128), F32), d[:ROWS - 8]], axis=0)
        nb_m = nb_m + jnp.concatenate([d[8:], jnp.zeros((8, 128), F32)], axis=0)
        sub = lax.broadcasted_iota(I32, (ROWS, 128), 0) % 8
        nb_m = nb_m + jnp.where(sub != 0, pltpu.roll(d, 1, 0), 0.0)
        nb_m = nb_m + jnp.where(sub != 7, pltpu.roll(d, ROWS - 1, 0), 0.0)
        for copy in halos:
            copy.wait_recv()
        from_low = unpacked(hz[par, 0]) * low
        from_high = unpacked(hz[par, 1]) * high
        nb_f = nb_f + jnp.where(ln < 16, from_low, turn(from_high, 16))
        nb_m = nb_m + jnp.where(ln == 32, turn(from_low, 16), 0.0)
        nb_m = nb_m + jnp.where(ln == 63, turn(from_high, 47), 0.0)
        y0 = jnp.broadcast_to((hy[par, 0] * near)[:, None, :], (64, 8, 128)).reshape(ROWS, 128)
        y1 = jnp.broadcast_to((hy[par, 1] * beyond)[:, None, :], (64, 8, 128)).reshape(ROWS, 128)
        nb_m = nb_m + jnp.where(sub == 0, y0, 0.0) + jnp.where(sub == 7, y1, 0.0)
        nb_m = nb_m + jnp.concatenate(
            [hx[par, 0] * left, jnp.zeros((ROWS - 16, 128), F32), hx[par, 1] * right], axis=0
        )
        nb = jnp.where(is_f, TF * nb_f, jnp.where(is_m, nb_m, 0.0))
        p_ref[...] = p_ref[...] + d
        r_ref[...] = r_ref[...] - (c_ref[...] * d - nb)

        sum_f = jnp.zeros((ROWS, 128), F32)
        sum_m = jnp.zeros((ROWS, 128), F32)
        for half in range(2):
            came = recv.at[par, pl.ds(1, 15)] if half == 0 else recv.at[par, pl.ds(16, 16)]
            pltpu.make_async_copy(came, came, recv_sem.at[par, half]).wait()
            x = recv[par, half * 16:(half + 1) * 16, 8:48, :].reshape(640, 128)
            hi = x.astype(BF16)
            rf[half * 640:(half + 1) * 640, 0:128] = hi
            rf[half * 640:(half + 1) * 640, 128:256] = (x - hi.astype(F32)).astype(BF16)
            x = recv[par, half * 16:(half + 1) * 16, 0:8, :].reshape(128, 128)
            hi = x.astype(BF16)
            rm[half * 128:(half + 1) * 128, 0:128] = hi
            rm[half * 128:(half + 1) * 128, 128:256] = (x - hi.astype(F32)).astype(BF16)
            add_f = jnp.zeros((ROWS, 128), F32)
            add_m = jnp.zeros((ROWS, 128), F32)
            for q in range(4):
                x = jnp.dot(
                    sf[q * ROWS:(q + 1) * ROWS, half * 640:(half + 1) * 640],
                    rf[half * 640:(half + 1) * 640, :],
                    preferred_element_type=F32,
                )
                add_f = jnp.where(group == q, x[:, :128] + x[:, 128:], add_f)
                x = jnp.dot(
                    sm[q * ROWS:(q + 1) * ROWS, half * 128:(half + 1) * 128],
                    rm[half * 128:(half + 1) * 128, :],
                    preferred_element_type=F32,
                )
                add_m = jnp.where(group == q, x[:, :128] + x[:, 128:], add_m)
            sum_f = sum_f + add_f
            sum_m = sum_m + add_m
        sum_f = sum_f + turn(sum_f, 64)
        sum_f = sum_f + turn(sum_f, 32)
        sum_m = sum_m + turn(sum_m, 64)
        sum_m = sum_m + turn(sum_m, 32)
        total = jnp.where(is_f, sum_f, jnp.where(is_m, sum_m, 0.0))

        for copy in halos:
            copy.wait_send()
        pltpu.make_async_copy(
            send.at[pl.ds(1, PEERS - 1)], send.at[pl.ds(1, PEERS - 1)], send_sem
        ).wait()
        phase = t % 4
        alpha = jnp.float32(pairs[3][0])
        beta = jnp.float32(pairs[3][1])
        for n in range(3):
            alpha = jnp.where(phase == n, jnp.float32(pairs[n][0]), alpha)
            beta = jnp.where(phase == n, jnp.float32(pairs[n][1]), beta)
        r = r_ref[...] + total
        r_ref[...] = r
        d_ref[...] = alpha * d_ref[...] + beta * (r * i_ref[...])
        return carry

    lax.fori_loop(0, STEPS, step, 0)

    for n in range(8):
        acc = jnp.zeros((32, 128), F32)
        for q in range(4):
            at = (n % 4) * 128 + q * 32
            piece = p_ref[at:at + 32, :] + d_ref[at:at + 32, :]
            acc = jnp.where(l32 // 32 == q, turn(piece, 32 * q - (32 if n < 4 else 0)), acc)
        tx2[n] = acc

    def back_start(n, carry):
        mine = own & (n == g * 4 + u_home)

        @pl.when(mine)
        def _():
            rx2[cz] = tx2[n]

        @pl.when(jnp.logical_not(mine))
        def _():
            pltpu.make_async_remote_copy(
                src_ref=tx2.at[n],
                dst_ref=rx2.at[cz],
                send_sem=usend_sem.at[n],
                recv_sem=urecv_sem.at[cz],
                device_id=(n // 4, w * 4 + n % 4, gy),
                device_id_type=MESH,
            ).start()

        return carry

    lax.fori_loop(0, 8, back_start, 0)

    def back_wait(n, carry):
        @pl.when(jnp.logical_not(own & (n == cz)))
        def _():
            pltpu.make_async_copy(rx2.at[n], rx2.at[n], urecv_sem.at[n]).wait()

        @pl.when(jnp.logical_not(own & (n == g * 4 + u_home)))
        def _():
            pltpu.make_async_copy(tx2.at[n], tx2.at[n], usend_sem.at[n]).wait()

        return carry

    lax.fori_loop(0, 8, back_wait, 0)
    for half in range(2):
        for q in range(4):
            acc = jnp.zeros((32, 128), F32)
            for part in range(4):
                acc = jnp.where(l32 // 32 == part, turn(rx2[half * 4 + part], 32 * (part - q)), acc)
            out[q * 32:(q + 1) * 32, half * 128:(half + 1) * 128] = acc


def per_device(source, storage, host_device, host_column, inter_device, inter_slot):
    dma = pltpu.SemaphoreType.DMA
    result = pl.pallas_call(
        kernel,
        out_shape=jax.ShapeDtypeStruct((128, 256), F32),
        in_specs=[pl.BlockSpec(memory_space=pltpu.VMEM)] * 6,
        out_specs=pl.BlockSpec(memory_space=pltpu.VMEM),
        scratch_shapes=[
            pltpu.VMEM((1280, 2048), BF16),
            pltpu.VMEM((256, 2048), BF16),
            pltpu.VMEM((2048, 1280), BF16),
            pltpu.VMEM((2048, 256), BF16),
            pltpu.VMEM((2048, 256), BF16),
            pltpu.VMEM((2048, 256), BF16),
            pltpu.VMEM((1280, 256), BF16),
            pltpu.VMEM((256, 256), BF16),
            pltpu.VMEM((PEERS, MSG, 128), F32),
            pltpu.VMEM((2, PEERS, MSG, 128), F32),
            pltpu.VMEM((2, 128, 128), F32),
            pltpu.VMEM((2, 2, 128, 128), F32),
            pltpu.VMEM((2, 64, 128), F32),
            pltpu.VMEM((2, 2, 64, 128), F32),
            pltpu.VMEM((2, 2, 8, 128), F32),
            pltpu.VMEM((8, 64, 128), F32),
            pltpu.VMEM((8, 64, 128), F32),
            pltpu.VMEM((8, 32, 128), F32),
            pltpu.VMEM((8, 32, 128), F32),
            pltpu.VMEM((256, 128), F32),
            pltpu.VMEM((256, 128), F32),
            pltpu.VMEM((4, 32, 128), I32),
            pltpu.VMEM((8, 128), F32),
            pltpu.VMEM((4, 8, 128), F32),
        ]
        + [pltpu.VMEM((ROWS, 128), F32)] * 5
        + [
            dma,
            dma((2, 2)),
            dma((6,)),
            dma((2, 6)),
            dma((8,)),
            dma((8,)),
            dma((8,)),
            dma((8,)),
            dma,
            dma,
            dma((8,)),
            dma((4,)),
        ],
        compiler_params=pltpu.CompilerParams(
            collective_id=0, has_side_effects=True, vmem_limit_bytes=50 * 1024 * 1024
        ),
    )(
        source.reshape(128, 256),
        storage.reshape(128, 256),
        host_device.reshape(1, 128),
        host_column.reshape(1, 128),
        inter_device.T,
        inter_slot.T,
    )
    return result.reshape(source.shape)


def solution(mesh):
    in_specs = (
        P("grp", "gx", "gy", None),
        P("grp", "gx", "gy", None),
        P(("gx", "gy"), None),
        P(("gx", "gy")),
        P(("gx", "gy"), None),
        P(("gx", "gy"), None),
    )
    return jax.shard_map(
        per_device, mesh=mesh, in_specs=in_specs, out_specs=P("grp", "gx", "gy", None), check_vma=False
    )
```

```python
import jax
import jax.numpy as jnp
from jax import lax
from jax.experimental import pallas as pl
from jax.experimental.pallas import tpu as pltpu
from jax.sharding import PartitionSpec as P

TF = 2.0
TI = 1.0
TM = 0.5
LMIN = 0.3
LMAX = 3.0
STEPS = 7

ROWS = 512
PEERS = 32
MSG = 48

F32 = jnp.float32
BF16 = jnp.bfloat16
I32 = jnp.int32
MESH = pl.DeviceIdType.MESH


def coefficients():
    theta = (LMAX + LMIN) / 2.0
    delta = (LMAX - LMIN) / 2.0
    sigma = theta / delta
    rho = 1.0 / sigma
    pairs = []
    for _ in range(3):
        rho_new = 1.0 / (2.0 * sigma - rho)
        pairs.append((rho_new * rho, 2.0 * rho_new / delta))
        rho = rho_new
    pairs.append((0.0, 1.0 / theta))
    return pairs, theta


def turn(x, shift):
    shift = shift % 128
    return x if shift == 0 else pltpu.roll(x, shift, 1)


def lanes(rows):
    return lax.broadcasted_iota(I32, (rows, 128), 1)


def kernel(
    src, sto, host_dev, host_col, inter_dev, inter_slot, out,
    gf, gm, sf, sm, wf, wm, rf, rm,
    send, recv, hs, hz, ys, hy, hx,
    tx, rx, tx2, rx2, mo, mi, vs, et, er,
    d_ref, r_ref, p_ref, c_ref, i_ref,
    send_sem, recv_sem, hsend_sem, hrecv_sem, tsend_sem, trecv_sem, usend_sem, urecv_sem, msend_sem, mrecv_sem, esend_sem, erecv_sem,
):
    g = lax.axis_index("grp")
    gx = lax.axis_index("gx")
    gy = lax.axis_index("gy")
    x_hi = gx // 16
    cz = (gx // 2) % 8
    core = gx % 2
    w = x_hi * 4 + g * 2 + core

    def place(w_, y_, z_):
        return ((w_ // 2) % 2, (w_ // 4) * 16 + z_ * 2 + w_ % 2, y_)

    def peer(k):
        n = (k + 1) % PEERS
        return place((w + n % 8) % 8, (gy + n // 8 + n % 8) % 4, cz)

    w_home = gx // 4
    u_home = gx % 4
    own = w_home == w

    barrier = pltpu.get_barrier_semaphore()

    def greet(device):
        pl.semaphore_signal(barrier, inc=1, device_id=device, device_id_type=MESH)

    def greet_peer(k, carry):
        greet(peer(k))
        return carry

    lax.fori_loop(0, PEERS - 1, greet_peer, 0)
    greet(place(w, gy, (cz + 1) % 8))
    greet(place(w, gy, (cz + 7) % 8))

    def greet_far(n, carry):
        @pl.when(jnp.logical_not(own & (n == cz)))
        def _():
            greet(place(w_home, gy, n))

        @pl.when(jnp.logical_not(own & (n == g * 4 + u_home)))
        def _():
            greet((n // 4, w * 4 + n % 4, gy))

        return carry

    lax.fori_loop(0, 8, greet_far, 0)

    l128 = lanes(128)
    s128 = lax.broadcasted_iota(I32, (128, 128), 0)
    earlier = jnp.where(l128 < s128, 1.0, 0.0).astype(BF16)

    def column(row):
        return jnp.sum(jnp.where(l128 == s128, row.astype(F32), 0.0), axis=1, keepdims=True)

    edges = jnp.zeros((8, 128), F32)
    s8 = lax.broadcasted_iota(I32, (8, 128), 0)

    def list_edges(edges, devices, rows, base, most):
        before = jnp.zeros((1, 128), F32)
        for dev, row in zip(devices, rows):
            named = column(dev) == l128.astype(F32)
            hit = jnp.where(named, 1.0, 0.0)
            rank = before + jnp.dot(earlier, hit.astype(BF16), preferred_element_type=F32)
            before = before + jnp.sum(hit, axis=0, keepdims=True)
            code = jnp.where(named, column(row) + (1 + 128 * s128).astype(F32), 0.0)
            for r in range(most):
                x = jnp.sum(jnp.where(rank == float(r), code, 0.0), axis=0, keepdims=True)
                edges = edges + jnp.where(s8 == base + r, x, 0.0)
        return edges

    edges = list_edges(
        edges, [inter_dev[0:1, :], inter_dev[1:2, :]], [inter_slot[0:1, :], inter_slot[1:2, :]], 0, 4
    )
    edges = list_edges(edges, [host_dev[...]], [host_col[...]], 4, 2)
    et[...] = edges

    l32 = lanes(32)
    for z in range(8):
        half, part = z // 4, z % 4
        for a, ref in ((0, src), (1, sto)):
            acc = jnp.zeros((32, 128), F32)
            for q in range(4):
                piece = ref[q * 32:(q + 1) * 32, half * 128:(half + 1) * 128]
                acc = jnp.where(l32 // 32 == q, turn(piece, 32 * (q - part)), acc)
            tx[z, a * 32:(a + 1) * 32, :] = acc

    pl.semaphore_wait(barrier, PEERS - 1 + 2 + jnp.where(own, 14, 16))

    def edge_start(z, carry):
        mine = own & (z == cz)

        @pl.when(mine)
        def _():
            er[u_home] = et[...]

        @pl.when(jnp.logical_not(mine))
        def _():
            pltpu.make_async_remote_copy(
                src_ref=et,
                dst_ref=er.at[u_home],
                send_sem=esend_sem.at[z],
                recv_sem=erecv_sem.at[u_home],
                device_id=place(w_home, gy, z),
                device_id_type=MESH,
            ).start()

        return carry

    @pl.when(g == 0)
    def _():
        lax.fori_loop(0, 8, edge_start, 0)

    def far_copy(z):
        return pltpu.make_async_remote_copy(
            src_ref=tx.at[z],
            dst_ref=rx.at[g * 4 + u_home],
            send_sem=tsend_sem.at[z],
            recv_sem=trecv_sem.at[g * 4 + u_home],
            device_id=place(w_home, gy, z),
            device_id_type=MESH,
        )

    def far_start(z, carry):
        mine = own & (z == cz)

        @pl.when(mine)
        def _():
            rx[g * 4 + u_home] = tx[z]

        @pl.when(jnp.logical_not(mine))
        def _():
            far_copy(z).start()

        return carry

    lax.fori_loop(0, 8, far_start, 0)

    def edge_wait(n, carry):
        @pl.when(jnp.logical_not(own & (g == 0) & (n == u_home)))
        def _():
            pltpu.make_async_copy(er.at[n], er.at[n], erecv_sem.at[n]).wait()

        return carry

    lax.fori_loop(0, 4, edge_wait, 0)

    lane1 = lax.broadcasted_iota(I32, (1, 128), 1)
    ub1 = lane1 // 32
    ua1 = lane1 % 32 // 8
    t1 = lane1 % 8
    k32 = lax.broadcasted_iota(I32, (32, 128), 0)
    table = er[...].reshape(32, 128)
    table = jnp.concatenate([table] * 4, axis=0)
    n32 = (k32 + 1) % PEERS
    first_of = ((w + n32 % 8) % 8) * 16 + (gy + n32 // 8 + n32 % 8) % 4
    outgoing = jnp.zeros((32, 128), F32)
    for ub in range(4):
        chosen = jnp.where(first_of + ub * 4 == l32, 1.0, 0.0)
        x = lax.dot_general(
            chosen, table, (((1,), (1,)), ((), ())),
            precision=lax.Precision.HIGHEST, preferred_element_type=F32,
        )
        outgoing = jnp.where(ub1 == ub, x, outgoing)
    mo[...] = jnp.broadcast_to(outgoing[:, None, :], (32, 8, 128)).reshape(256, 128)
    mi[248:256] = mo[248:256]

    def edge_send(k, carry):
        at = pl.multiple_of(k * 8, 8)
        pltpu.make_async_remote_copy(
            src_ref=mo.at[pl.ds(at, 8)],
            dst_ref=mi.at[pl.ds(at, 8)],
            send_sem=msend_sem,
            recv_sem=mrecv_sem,
            device_id=peer(k),
            device_id_type=MESH,
        ).start()
        return carry

    lax.fori_loop(0, PEERS - 1, edge_send, 0)

    def far_wait(n, carry):
        mine = own & (n == g * 4 + u_home)

        @pl.when(jnp.logical_not(mine))
        def _():
            pltpu.make_async_copy(rx.at[n], rx.at[n], trecv_sem.at[n]).wait()

        @pl.when(jnp.logical_not(own & (n == cz)))
        def _():
            pltpu.make_async_copy(tx.at[n], tx.at[n], tsend_sem.at[n]).wait()

        return carry

    lax.fori_loop(0, 8, far_wait, 0)

    ln = lanes(ROWS)
    group = ln // 32
    is_f = ln < 32
    is_m = group == 1

    pairs, theta = coefficients()
    for a, ref in ((0, r_ref), (1, c_ref)):
        for u in range(4):
            fr = rx[4 + u, a * 32:(a + 1) * 32, :]
            ma = rx[u, a * 32:(a + 1) * 32, :]
            for q in range(4):
                ref[u * 128 + q * 32:u * 128 + (q + 1) * 32, :] = jnp.where(
                    l32 < 32,
                    turn(fr, -32 * q),
                    jnp.where(l32 // 32 == 1, turn(ma, 32 - 32 * q), 0.0),
                )
    stored = c_ref[...]
    inverse = 1.0 / (stored + jnp.where(is_f, 4.0 * TF + 4.0 * TI + TM, 6.0 + TM))
    i_ref[...] = inverse
    c_ref[...] = stored
    d_ref[...] = r_ref[...] * inverse * (1.0 / theta)
    p_ref[...] = jnp.zeros((ROWS, 128), F32)

    pltpu.make_async_copy(mi.at[pl.ds(0, 248)], mi.at[pl.ds(0, 248)], mrecv_sem).wait()
    incoming = mi[pl.ds(0, 32, stride=8), :]
    mirror = (8 - n32 % 8) % 8
    mirror = (mirror + 8 * ((16 - n32 // 8 - n32 % 8 - mirror) % 4) + PEERS - 1) % PEERS
    mirror = jnp.where(mirror == l32, 1.0, 0.0)[:, :32]

    def mirrored(x):
        return jnp.dot(mirror, x, precision=lax.Precision.HIGHEST, preferred_element_type=F32)

    def source_row(x):
        x = x.astype(I32)
        return jnp.where(x > 0, ua1 * 128 + ((x - 1) >> 7) + 1, 0)

    def target_row(x):
        x = x.astype(I32)
        return jnp.where(x > 0, ub1 * 128 + ((x - 1) & 127) + 1, 0)

    vs[0] = source_row(outgoing)
    vs[1] = target_row(mirrored(incoming))
    vs[2] = target_row(incoming)
    vs[3] = source_row(mirrored(outgoing))

    inter_at = jnp.where(t1 < 4, ua1 * 4 + ub1, -100)
    host_at = jnp.where((t1 == 4) | (t1 == 5), ua1 * 2 + t1 - 4, -100)
    out_at = jnp.maximum(inter_at + 8, host_at)
    back_at = jnp.maximum(inter_at + 16, host_at + 32)
    i80 = lax.broadcasted_iota(I32, (80, 128), 0)
    first80 = i80 < 40
    i80 = i80 % 40
    i16 = lax.broadcasted_iota(I32, (16, 128), 0)
    first16 = i16 < 8
    i16 = i16 % 8
    ql = lax.broadcasted_iota(I32, (256, 512), 0)
    qt = ql % 8
    qh = jnp.where(qt < 4, qt, (ql % 128) // 32)
    q_rep = jnp.where(
        lax.broadcasted_iota(I32, (256, 512), 1) // 128 == qh, jnp.where(ql < 128, 32.0, 1.0), 0.0
    ).astype(BF16)
    ql = lax.broadcasted_iota(I32, (16, 256), 1)
    qt = ql % 8
    qh = jnp.where(qt < 4, qt, (ql % 128) // 32)
    q_row = jnp.where(
        lax.broadcasted_iota(I32, (16, 256), 0) == qh, jnp.where(ql < 128, 32.0, 1.0), 0.0
    ).astype(BF16)

    def halves(x):
        return jnp.concatenate([(x >> 5).astype(F32), (x & 31).astype(F32)], axis=1).astype(BF16)

    def build_g(j, carry):
        def pair(n, first):
            return jnp.where(first, vs[n, pl.ds(2 * j, 1), :], vs[n, pl.ds(2 * j + 1, 1), :])

        at = pl.multiple_of(j * 80, 80)
        x = jnp.where(i80 == out_at, pair(0, first80), 0)
        x = x + jnp.where(i80 == inter_at + 24, pair(1, first80), 0)
        rows = jnp.dot(halves(x), q_rep, preferred_element_type=F32).astype(I32)
        for q in range(4):
            for c in range(4):
                hit = rows[:, q * 128:(q + 1) * 128] == lane1 + (c * 128 + 1)
                gf[pl.ds(at, 80), q * ROWS + c * 128:q * ROWS + (c + 1) * 128] = jnp.where(
                    hit, 1.0, 0.0
                ).astype(BF16)
        x = jnp.where(i80 == inter_at, pair(2, first80), 0)
        x = x + jnp.where(i80 == back_at, pair(3, first80), 0)
        rf[pl.ds(at, 80), :] = halves(x)
        at = pl.multiple_of(j * 16, 16)
        x = jnp.where(i16 == host_at, pair(1, first16), 0)
        rows = jnp.dot(halves(x), q_rep, preferred_element_type=F32).astype(I32)
        for q in range(4):
            for c in range(4):
                hit = rows[:, q * 128:(q + 1) * 128] == lane1 + (c * 128 + 1)
                gm[pl.ds(at, 16), q * ROWS + c * 128:q * ROWS + (c + 1) * 128] = jnp.where(
                    hit, 1.0, 0.0
                ).astype(BF16)
        rm[pl.ds(at, 16), :] = halves(jnp.where(i16 == host_at, pair(2, first16), 0))
        return carry

    lax.fori_loop(0, 16, build_g, 0)

    low = jnp.where(cz > 0, 1.0, 0.0)
    high = jnp.where(cz < 7, 1.0, 0.0)
    left = jnp.where(w > 0, 1.0, 0.0)
    right = jnp.where(w < 7, 1.0, 0.0)
    near = jnp.where(gy > 0, 1.0, 0.0)
    beyond = jnp.where(gy < 3, 1.0, 0.0)
    def packed(x):
        acc = x[0:128]
        for q in range(1, 4):
            acc = jnp.where(l128 // 32 == q, turn(x[q * 128:(q + 1) * 128], 32 * q), acc)
        return acc

    def unpacked(x):
        return jnp.concatenate([turn(x, -32 * q) for q in range(4)], axis=0)

    def halo_copies(par):

        def halo(n, source, dest, device):
            return pltpu.make_async_remote_copy(
                src_ref=source,
                dst_ref=dest,
                send_sem=hsend_sem.at[n],
                recv_sem=hrecv_sem.at[par, n],
                device_id=device,
                device_id_type=MESH,
            )

        return [
            halo(0, hs.at[0], hz.at[par, 0], place(w, gy, (cz + 1) % 8)),
            halo(1, hs.at[1], hz.at[par, 1], place(w, gy, (cz + 7) % 8)),
            halo(2, ys.at[1], hy.at[par, 0], place(w, (gy + 1) % 4, cz)),
            halo(3, ys.at[0], hy.at[par, 1], place(w, (gy + 3) % 4, cz)),
            halo(4, d_ref.at[pl.ds(ROWS - 8, 8)], hx.at[par, 0], place((w + 1) % 8, gy, cz)),
            halo(5, d_ref.at[pl.ds(0, 8)], hx.at[par, 1], place((w + 7) % 8, gy, cz)),
        ]
    def launch(t):
        par = t % 2
        halos = halo_copies(par)
        d = d_ref[...]
        high_part = d.astype(BF16).astype(F32)
        low_part = d - high_part
        for s in range(4):
            for part, x in ((0, turn(high_part, 32 * s)), (1, turn(low_part, 32 * s))):
                q = (s + 1) % 4
                wf[s * ROWS:(s + 1) * ROWS, part * 128:(part + 1) * 128] = jnp.where(
                    group == s, x, 0.0
                ).astype(BF16)
                wm[q * ROWS:(q + 1) * ROWS, part * 128:(part + 1) * 128] = jnp.where(
                    group == q, x, 0.0
                ).astype(BF16)

        def message(k, half):
            return pltpu.make_async_remote_copy(
                src_ref=send.at[k],
                dst_ref=recv.at[par, k],
                send_sem=send_sem,
                recv_sem=recv_sem.at[par, half],
                device_id=peer(k),
                device_id_type=MESH,
            )

        def gather(c, carry):
            at = c * 320 if isinstance(c, int) else pl.multiple_of(c * 320, 320)
            x = jnp.dot(gf[pl.ds(at, 320), :], wf[...], preferred_element_type=F32)
            send[pl.ds(c * 8, 8), 0:40, :] = (x[:, :128] + x[:, 128:]).reshape(8, 40, 128)
            at = c * 64 if isinstance(c, int) else pl.multiple_of(c * 64, 64)
            x = jnp.dot(gm[pl.ds(at, 64), :], wm[...], preferred_element_type=F32)
            send[pl.ds(c * 8, 8), 40:48, :] = (x[:, :128] + x[:, 128:]).reshape(8, 8, 128)
            for n in range(8):
                k = c * 8 + n
                if n < 7 or isinstance(c, int):
                    message(k, c // 2).start()
                else:
                    @pl.when(c < 3)
                    def _():
                        message(k, c // 2).start()
            return carry

        gather(0, 0)
        hs[0] = packed(jnp.where(ln < 16, turn(d, -16), turn(d, -47)))
        hs[1] = packed(jnp.where(ln < 16, d, turn(d, -16)))
        ys[0] = d_ref[pl.ds(0, 64, stride=8), :]
        ys[1] = d_ref[pl.ds(7, 64, stride=8), :]
        for copy in halos:
            copy.start()
        lax.fori_loop(1, 4, gather, 0)
        recv[par, PEERS - 1] = send[PEERS - 1]

    def finish(t):
        par = t % 2
        halos = halo_copies(par)
        d = d_ref[...]
        col = ln % 16
        before = turn(d, 1)
        after = turn(d, -1)
        nb_f = jnp.where(col != 0, before, 0.0) + jnp.where(col != 15, after, 0.0)
        nb_f = nb_f + jnp.where(ln >= 16, turn(d, 16), 0.0) + jnp.where(ln < 16, turn(d, -16), 0.0)
        nb_m = jnp.where(ln != 32, before, 0.0) + jnp.where(ln != 63, after, 0.0)
        nb_m = nb_m + jnp.concatenate([jnp.zeros((8, 128), F32), d[:ROWS - 8]], axis=0)
        nb_m = nb_m + jnp.concatenate([d[8:], jnp.zeros((8, 128), F32)], axis=0)
        sub = lax.broadcasted_iota(I32, (ROWS, 128), 0) % 8
        nb_m = nb_m + jnp.where(sub != 0, pltpu.roll(d, 1, 0), 0.0)
        nb_m = nb_m + jnp.where(sub != 7, pltpu.roll(d, ROWS - 1, 0), 0.0)
        for copy in halos:
            copy.wait_recv()
        from_low = unpacked(hz[par, 0]) * low
        from_high = unpacked(hz[par, 1]) * high
        nb_f = nb_f + jnp.where(ln < 16, from_low, turn(from_high, 16))
        nb_m = nb_m + jnp.where(ln == 32, turn(from_low, 16), 0.0)
        nb_m = nb_m + jnp.where(ln == 63, turn(from_high, 47), 0.0)
        y0 = jnp.broadcast_to((hy[par, 0] * near)[:, None, :], (64, 8, 128)).reshape(ROWS, 128)
        y1 = jnp.broadcast_to((hy[par, 1] * beyond)[:, None, :], (64, 8, 128)).reshape(ROWS, 128)
        nb_m = nb_m + jnp.where(sub == 0, y0, 0.0) + jnp.where(sub == 7, y1, 0.0)
        nb_m = nb_m + jnp.concatenate(
            [hx[par, 0] * left, jnp.zeros((ROWS - 16, 128), F32), hx[par, 1] * right], axis=0
        )
        nb = jnp.where(is_f, TF * nb_f, jnp.where(is_m, nb_m, 0.0))
        p_ref[...] = p_ref[...] + d
        r_ref[...] = r_ref[...] - (c_ref[...] * d - nb)

        sum_f = jnp.zeros((ROWS, 128), F32)
        sum_m = jnp.zeros((ROWS, 128), F32)
        for half in range(2):
            came = recv.at[par, pl.ds(0, 16)] if half == 0 else recv.at[par, pl.ds(16, 15)]
            pltpu.make_async_copy(came, came, recv_sem.at[par, half]).wait()
            x = recv[par, half * 16:(half + 1) * 16, 8:48, :].reshape(640, 128)
            hi = x.astype(BF16)
            rf[half * 640:(half + 1) * 640, 0:128] = hi
            rf[half * 640:(half + 1) * 640, 128:256] = (x - hi.astype(F32)).astype(BF16)
            x = recv[par, half * 16:(half + 1) * 16, 0:8, :].reshape(128, 128)
            hi = x.astype(BF16)
            rm[half * 128:(half + 1) * 128, 0:128] = hi
            rm[half * 128:(half + 1) * 128, 128:256] = (x - hi.astype(F32)).astype(BF16)
            add_f = jnp.zeros((ROWS, 128), F32)
            add_m = jnp.zeros((ROWS, 128), F32)
            for q in range(4):
                x = jnp.dot(
                    sf[q * ROWS:(q + 1) * ROWS, half * 640:(half + 1) * 640],
                    rf[half * 640:(half + 1) * 640, :],
                    preferred_element_type=F32,
                )
                add_f = jnp.where(group == q, x[:, :128] + x[:, 128:], add_f)
                x = jnp.dot(
                    sm[q * ROWS:(q + 1) * ROWS, half * 128:(half + 1) * 128],
                    rm[half * 128:(half + 1) * 128, :],
                    preferred_element_type=F32,
                )
                add_m = jnp.where(group == q, x[:, :128] + x[:, 128:], add_m)
            sum_f = sum_f + add_f
            sum_m = sum_m + add_m
        sum_f = sum_f + turn(sum_f, 64)
        sum_f = sum_f + turn(sum_f, 32)
        sum_m = sum_m + turn(sum_m, 64)
        sum_m = sum_m + turn(sum_m, 32)
        total = jnp.where(is_f, sum_f, jnp.where(is_m, sum_m, 0.0))

        for copy in halos:
            copy.wait_send()
        pltpu.make_async_copy(
            send.at[pl.ds(0, PEERS - 1)], send.at[pl.ds(0, PEERS - 1)], send_sem
        ).wait()
        phase = t % 4
        alpha = jnp.float32(pairs[3][0])
        beta = jnp.float32(pairs[3][1])
        for n in range(3):
            alpha = jnp.where(phase == n, jnp.float32(pairs[n][0]), alpha)
            beta = jnp.where(phase == n, jnp.float32(pairs[n][1]), beta)
        r = r_ref[...] + total
        r_ref[...] = r
        d_ref[...] = alpha * d_ref[...] + beta * (r * i_ref[...])

    launch(0)

    across = (((1,), (1,)), ((), ()))
    sbf = lax.dot_general(q_row, rf[...], across, preferred_element_type=F32).astype(I32)
    sbm = lax.dot_general(q_row, rm[...], across, preferred_element_type=F32).astype(I32)
    within = lax.broadcasted_iota(I32, (1, 1280), 1) % 40
    weight = jnp.where(within < 32, TI, TM)

    def build_s(j, carry):
        at = pl.multiple_of(j * 16, 16)
        block = lax.broadcasted_iota(I32, (16, 1280), 0) + (at + 1)
        for q in range(4):
            sf[pl.ds(at + q * ROWS, 16), :] = jnp.where(sbf[q:q + 1, :] == block, weight, 0.0).astype(BF16)
            sm[pl.ds(at + q * ROWS, 16), :] = jnp.where(
                sbm[q:q + 1, :] == block[:, :256], TM, 0.0
            ).astype(BF16)
        return carry

    lax.fori_loop(0, 32, build_s, 0)

    entering = jnp.where(lax.broadcasted_iota(I32, (1280, 128), 0) % 40 < 16, 1.0, 0.0).astype(BF16)
    ones = jnp.ones((256, 128), BF16)
    indeg = jnp.zeros((ROWS, 128), F32)
    hosted = jnp.zeros((ROWS, 128), F32)
    for q in range(4):
        indeg = indeg + jnp.dot(sf[q * ROWS:(q + 1) * ROWS, :], entering, preferred_element_type=F32)
        hosted = hosted + jnp.dot(sm[q * ROWS:(q + 1) * ROWS, :], ones, preferred_element_type=F32)

    c_ref[...] = c_ref[...] + jnp.where(is_f, 4.0 * TF + 2.0 * TI + TM + indeg, 6.0 + hosted)
    pltpu.make_async_copy(mo.at[pl.ds(0, 248)], mo.at[pl.ds(0, 248)], msend_sem).wait()

    def edge_sent(z, carry):
        @pl.when(jnp.logical_not(own & (z == cz)))
        def _():
            pltpu.make_async_copy(et, et, esend_sem.at[z]).wait()

        return carry

    @pl.when(g == 0)
    def _():
        lax.fori_loop(0, 8, edge_sent, 0)

    def step(t, carry):
        finish(t)

        @pl.when(t < STEPS - 1)
        def _():
            launch(t + 1)

        return carry

    lax.fori_loop(0, STEPS, step, 0)

    for n in range(8):
        acc = jnp.zeros((32, 128), F32)
        for q in range(4):
            at = (n % 4) * 128 + q * 32
            piece = p_ref[at:at + 32, :] + d_ref[at:at + 32, :]
            acc = jnp.where(l32 // 32 == q, turn(piece, 32 * q - (32 if n < 4 else 0)), acc)
        tx2[n] = acc

    def back_start(n, carry):
        mine = own & (n == g * 4 + u_home)

        @pl.when(mine)
        def _():
            rx2[cz] = tx2[n]

        @pl.when(jnp.logical_not(mine))
        def _():
            pltpu.make_async_remote_copy(
                src_ref=tx2.at[n],
                dst_ref=rx2.at[cz],
                send_sem=usend_sem.at[n],
                recv_sem=urecv_sem.at[cz],
                device_id=(n // 4, w * 4 + n % 4, gy),
                device_id_type=MESH,
            ).start()

        return carry

    lax.fori_loop(0, 8, back_start, 0)

    def back_wait(n, carry):
        @pl.when(jnp.logical_not(own & (n == cz)))
        def _():
            pltpu.make_async_copy(rx2.at[n], rx2.at[n], urecv_sem.at[n]).wait()

        @pl.when(jnp.logical_not(own & (n == g * 4 + u_home)))
        def _():
            pltpu.make_async_copy(tx2.at[n], tx2.at[n], usend_sem.at[n]).wait()

        return carry

    lax.fori_loop(0, 8, back_wait, 0)
    for half in range(2):
        for q in range(4):
            acc = jnp.zeros((32, 128), F32)
            for part in range(4):
                acc = jnp.where(l32 // 32 == part, turn(rx2[half * 4 + part], 32 * (part - q)), acc)
            out[q * 32:(q + 1) * 32, half * 128:(half + 1) * 128] = acc


def per_device(source, storage, host_device, host_column, inter_device, inter_slot):
    dma = pltpu.SemaphoreType.DMA
    result = pl.pallas_call(
        kernel,
        out_shape=jax.ShapeDtypeStruct((128, 256), F32),
        in_specs=[pl.BlockSpec(memory_space=pltpu.VMEM)] * 6,
        out_specs=pl.BlockSpec(memory_space=pltpu.VMEM),
        scratch_shapes=[
            pltpu.VMEM((1280, 2048), BF16),
            pltpu.VMEM((256, 2048), BF16),
            pltpu.VMEM((2048, 1280), BF16),
            pltpu.VMEM((2048, 256), BF16),
            pltpu.VMEM((2048, 256), BF16),
            pltpu.VMEM((2048, 256), BF16),
            pltpu.VMEM((1280, 256), BF16),
            pltpu.VMEM((256, 256), BF16),
            pltpu.VMEM((PEERS, MSG, 128), F32),
            pltpu.VMEM((2, PEERS, MSG, 128), F32),
            pltpu.VMEM((2, 128, 128), F32),
            pltpu.VMEM((2, 2, 128, 128), F32),
            pltpu.VMEM((2, 64, 128), F32),
            pltpu.VMEM((2, 2, 64, 128), F32),
            pltpu.VMEM((2, 2, 8, 128), F32),
            pltpu.VMEM((8, 64, 128), F32),
            pltpu.VMEM((8, 64, 128), F32),
            pltpu.VMEM((8, 32, 128), F32),
            pltpu.VMEM((8, 32, 128), F32),
            pltpu.VMEM((256, 128), F32),
            pltpu.VMEM((256, 128), F32),
            pltpu.VMEM((4, 32, 128), I32),
            pltpu.VMEM((8, 128), F32),
            pltpu.VMEM((4, 8, 128), F32),
        ]
        + [pltpu.VMEM((ROWS, 128), F32)] * 5
        + [
            dma,
            dma((2, 2)),
            dma((6,)),
            dma((2, 6)),
            dma((8,)),
            dma((8,)),
            dma((8,)),
            dma((8,)),
            dma,
            dma,
            dma((8,)),
            dma((4,)),
        ],
        compiler_params=pltpu.CompilerParams(
            collective_id=0, has_side_effects=True, vmem_limit_bytes=50 * 1024 * 1024
        ),
    )(
        source.reshape(128, 256),
        storage.reshape(128, 256),
        host_device.reshape(1, 128),
        host_column.reshape(1, 128),
        inter_device.T,
        inter_slot.T,
    )
    return result.reshape(source.shape)


def solution(mesh):
    in_specs = (
        P("grp", "gx", "gy", None),
        P("grp", "gx", "gy", None),
        P(("gx", "gy"), None),
        P(("gx", "gy")),
        P(("gx", "gy"), None),
        P(("gx", "gy"), None),
    )
    return jax.shard_map(
        per_device, mesh=mesh, in_specs=in_specs, out_specs=P("grp", "gx", "gy", None), check_vma=False
    )
```

```python
import jax
import jax.numpy as jnp
from jax import lax
from jax.experimental import pallas as pl
from jax.experimental.pallas import tpu as pltpu
from jax.sharding import PartitionSpec as P

TF = 2.0
TI = 1.0
TM = 0.5
LMIN = 0.3
LMAX = 3.0
STEPS = 7

ROWS = 512
PEERS = 32
MSG = 48

F32 = jnp.float32
BF16 = jnp.bfloat16
I32 = jnp.int32
MESH = pl.DeviceIdType.MESH


def coefficients():
    theta = (LMAX + LMIN) / 2.0
    delta = (LMAX - LMIN) / 2.0
    sigma = theta / delta
    rho = 1.0 / sigma
    pairs = []
    for _ in range(3):
        rho_new = 1.0 / (2.0 * sigma - rho)
        pairs.append((rho_new * rho, 2.0 * rho_new / delta))
        rho = rho_new
    pairs.append((0.0, 1.0 / theta))
    return pairs, theta


def turn(x, shift):
    shift = shift % 128
    return x if shift == 0 else pltpu.roll(x, shift, 1)


def lanes(rows):
    return lax.broadcasted_iota(I32, (rows, 128), 1)


def kernel(
    src, sto, host_dev, host_col, inter_dev, inter_slot, out,
    gf, gm, sf, sm, wf, wm, rf, rm,
    send, recv, hs, hz, ys, hy, hx,
    tx, rx, tx2, rx2, mo, mi, vs, et, er,
    d_ref, r_ref, p_ref, c_ref, i_ref,
    send_sem, recv_sem, hsend_sem, hrecv_sem, tsend_sem, trecv_sem, usend_sem, urecv_sem, msend_sem, mrecv_sem, esend_sem, erecv_sem,
):
    g = lax.axis_index("grp")
    gx = lax.axis_index("gx")
    gy = lax.axis_index("gy")
    x_hi = gx // 16
    cz = (gx // 2) % 8
    core = gx % 2
    w = x_hi * 4 + g * 2 + core

    def place(w_, y_, z_):
        return ((w_ // 2) % 2, (w_ // 4) * 16 + z_ * 2 + w_ % 2, y_)

    def peer(k):
        n = 31 - k
        return place((w + n % 8) % 8, (gy + n // 8 + n % 8) % 4, cz)

    w_home = gx // 4
    u_home = gx % 4
    own = w_home == w

    barrier = pltpu.get_barrier_semaphore()

    def greet(device):
        pl.semaphore_signal(barrier, inc=1, device_id=device, device_id_type=MESH)

    def greet_peer(k, carry):
        greet(peer(k))
        return carry


    def greet_far(n, carry):
        @pl.when(jnp.logical_not(own & (n == cz)))
        def _():
            greet(place(w_home, gy, n))

        @pl.when(jnp.logical_not(own & (n == g * 4 + u_home)))
        def _():
            greet((n // 4, w * 4 + n % 4, gy))

        return carry

    lax.fori_loop(0, 8, greet_far, 0)
    lax.fori_loop(0, PEERS - 1, greet_peer, 0)
    greet(place(w, gy, (cz + 1) % 8))
    greet(place(w, gy, (cz + 7) % 8))

    l128 = lanes(128)
    s128 = lax.broadcasted_iota(I32, (128, 128), 0)
    earlier = jnp.where(l128 < s128, 1.0, 0.0).astype(BF16)

    def column(row):
        return jnp.sum(jnp.where(l128 == s128, row.astype(F32), 0.0), axis=1, keepdims=True)

    edges = jnp.zeros((8, 128), F32)
    s8 = lax.broadcasted_iota(I32, (8, 128), 0)

    def list_edges(edges, devices, rows, base, most):
        before = jnp.zeros((1, 128), F32)
        for dev, row in zip(devices, rows):
            named = column(dev) == l128.astype(F32)
            hit = jnp.where(named, 1.0, 0.0)
            rank = before + jnp.dot(earlier, hit.astype(BF16), preferred_element_type=F32)
            before = before + jnp.sum(hit, axis=0, keepdims=True)
            code = jnp.where(named, column(row) + (1 + 128 * s128).astype(F32), 0.0)
            for r in range(most):
                x = jnp.sum(jnp.where(rank == float(r), code, 0.0), axis=0, keepdims=True)
                edges = edges + jnp.where(s8 == base + r, x, 0.0)
        return edges

    edges = list_edges(
        edges, [inter_dev[0:1, :], inter_dev[1:2, :]], [inter_slot[0:1, :], inter_slot[1:2, :]], 0, 4
    )
    edges = list_edges(edges, [host_dev[...]], [host_col[...]], 4, 2)
    et[...] = edges

    l32 = lanes(32)
    for z in range(8):
        half, part = z // 4, z % 4
        for a, ref in ((0, src), (1, sto)):
            acc = jnp.zeros((32, 128), F32)
            for q in range(4):
                piece = ref[q * 32:(q + 1) * 32, half * 128:(half + 1) * 128]
                acc = jnp.where(l32 // 32 == q, turn(piece, 32 * (q - part)), acc)
            tx[z, a * 32:(a + 1) * 32, :] = acc

    pl.semaphore_wait(barrier, PEERS - 1 + 2 + jnp.where(own, 14, 16))

    def edge_start(z, carry):
        mine = own & (z == cz)

        @pl.when(mine)
        def _():
            er[u_home] = et[...]

        @pl.when(jnp.logical_not(mine))
        def _():
            pltpu.make_async_remote_copy(
                src_ref=et,
                dst_ref=er.at[u_home],
                send_sem=esend_sem.at[z],
                recv_sem=erecv_sem.at[u_home],
                device_id=place(w_home, gy, z),
                device_id_type=MESH,
            ).start()

        return carry

    @pl.when(g == 0)
    def _():
        lax.fori_loop(0, 8, edge_start, 0)

    def far_copy(z):
        return pltpu.make_async_remote_copy(
            src_ref=tx.at[z],
            dst_ref=rx.at[g * 4 + u_home],
            send_sem=tsend_sem.at[z],
            recv_sem=trecv_sem.at[g * 4 + u_home],
            device_id=place(w_home, gy, z),
            device_id_type=MESH,
        )

    def far_start(z, carry):
        mine = own & (z == cz)

        @pl.when(mine)
        def _():
            rx[g * 4 + u_home] = tx[z]

        @pl.when(jnp.logical_not(mine))
        def _():
            far_copy(z).start()

        return carry

    lax.fori_loop(0, 8, far_start, 0)

    def edge_wait(n, carry):
        @pl.when(jnp.logical_not(own & (g == 0) & (n == u_home)))
        def _():
            pltpu.make_async_copy(er.at[n], er.at[n], erecv_sem.at[n]).wait()

        return carry

    lax.fori_loop(0, 4, edge_wait, 0)

    lane1 = lax.broadcasted_iota(I32, (1, 128), 1)
    ub1 = lane1 // 32
    ua1 = lane1 % 32 // 8
    t1 = lane1 % 8
    k32 = lax.broadcasted_iota(I32, (32, 128), 0)
    table = er[...].reshape(32, 128)
    table = jnp.concatenate([table] * 4, axis=0)
    n32 = 31 - k32
    first_of = ((w + n32 % 8) % 8) * 16 + (gy + n32 // 8 + n32 % 8) % 4
    outgoing = jnp.zeros((32, 128), F32)
    for ub in range(4):
        chosen = jnp.where(first_of + ub * 4 == l32, 1.0, 0.0)
        x = lax.dot_general(
            chosen, table, (((1,), (1,)), ((), ())),
            precision=lax.Precision.HIGHEST, preferred_element_type=F32,
        )
        outgoing = jnp.where(ub1 == ub, x, outgoing)
    mo[...] = jnp.broadcast_to(outgoing[:, None, :], (32, 8, 128)).reshape(256, 128)
    mi[248:256] = mo[248:256]

    def edge_send(k, carry):
        at = pl.multiple_of(k * 8, 8)
        pltpu.make_async_remote_copy(
            src_ref=mo.at[pl.ds(at, 8)],
            dst_ref=mi.at[pl.ds(at, 8)],
            send_sem=msend_sem,
            recv_sem=mrecv_sem,
            device_id=peer(k),
            device_id_type=MESH,
        ).start()
        return carry

    lax.fori_loop(0, PEERS - 1, edge_send, 0)

    def far_wait(n, carry):
        mine = own & (n == g * 4 + u_home)

        @pl.when(jnp.logical_not(mine))
        def _():
            pltpu.make_async_copy(rx.at[n], rx.at[n], trecv_sem.at[n]).wait()

        @pl.when(jnp.logical_not(own & (n == cz)))
        def _():
            pltpu.make_async_copy(tx.at[n], tx.at[n], tsend_sem.at[n]).wait()

        return carry

    lax.fori_loop(0, 8, far_wait, 0)

    ln = lanes(ROWS)
    group = ln // 32
    is_f = ln < 32
    is_m = group == 1

    pairs, theta = coefficients()
    for a, ref in ((0, r_ref), (1, c_ref)):
        for u in range(4):
            fr = rx[4 + u, a * 32:(a + 1) * 32, :]
            ma = rx[u, a * 32:(a + 1) * 32, :]
            for q in range(4):
                ref[u * 128 + q * 32:u * 128 + (q + 1) * 32, :] = jnp.where(
                    l32 < 32,
                    turn(fr, -32 * q),
                    jnp.where(l32 // 32 == 1, turn(ma, 32 - 32 * q), 0.0),
                )
    stored = c_ref[...]
    inverse = 1.0 / (stored + jnp.where(is_f, 4.0 * TF + 4.0 * TI + TM, 6.0 + TM))
    i_ref[...] = inverse
    c_ref[...] = stored
    d_ref[...] = r_ref[...] * inverse * (1.0 / theta)
    p_ref[...] = jnp.zeros((ROWS, 128), F32)

    pltpu.make_async_copy(mi.at[pl.ds(0, 248)], mi.at[pl.ds(0, 248)], mrecv_sem).wait()
    incoming = mi[pl.ds(0, 32, stride=8), :]
    mirror = (8 - n32 % 8) % 8
    mirror = 31 - (mirror + 8 * ((16 - n32 // 8 - n32 % 8 - mirror) % 4))
    mirror = jnp.where(mirror == l32, 1.0, 0.0)[:, :32]

    def mirrored(x):
        return jnp.dot(mirror, x, precision=lax.Precision.HIGHEST, preferred_element_type=F32)

    def source_row(x):
        x = x.astype(I32)
        return jnp.where(x > 0, ua1 * 128 + ((x - 1) >> 7) + 1, 0)

    def target_row(x):
        x = x.astype(I32)
        return jnp.where(x > 0, ub1 * 128 + ((x - 1) & 127) + 1, 0)

    vs[0] = source_row(outgoing)
    vs[1] = target_row(mirrored(incoming))
    vs[2] = target_row(incoming)
    vs[3] = source_row(mirrored(outgoing))

    inter_at = jnp.where(t1 < 4, ua1 * 4 + ub1, -100)
    host_at = jnp.where((t1 == 4) | (t1 == 5), ua1 * 2 + t1 - 4, -100)
    out_at = jnp.maximum(inter_at + 8, host_at)
    back_at = jnp.maximum(inter_at + 16, host_at + 32)
    i80 = lax.broadcasted_iota(I32, (80, 128), 0)
    first80 = i80 < 40
    i80 = i80 % 40
    i16 = lax.broadcasted_iota(I32, (16, 128), 0)
    first16 = i16 < 8
    i16 = i16 % 8
    ql = lax.broadcasted_iota(I32, (256, 512), 0)
    qt = ql % 8
    qh = jnp.where(qt < 4, qt, (ql % 128) // 32)
    q_rep = jnp.where(
        lax.broadcasted_iota(I32, (256, 512), 1) // 128 == qh, jnp.where(ql < 128, 32.0, 1.0), 0.0
    ).astype(BF16)
    ql = lax.broadcasted_iota(I32, (16, 256), 1)
    qt = ql % 8
    qh = jnp.where(qt < 4, qt, (ql % 128) // 32)
    q_row = jnp.where(
        lax.broadcasted_iota(I32, (16, 256), 0) == qh, jnp.where(ql < 128, 32.0, 1.0), 0.0
    ).astype(BF16)

    def halves(x):
        return jnp.concatenate([(x >> 5).astype(F32), (x & 31).astype(F32)], axis=1).astype(BF16)

    def build_g(j, carry):
        def pair(n, first):
            return jnp.where(first, vs[n, pl.ds(2 * j, 1), :], vs[n, pl.ds(2 * j + 1, 1), :])

        at = pl.multiple_of(j * 80, 80)
        x = jnp.where(i80 == out_at, pair(0, first80), 0)
        x = x + jnp.where(i80 == inter_at + 24, pair(1, first80), 0)
        rows = jnp.dot(halves(x), q_rep, preferred_element_type=F32).astype(I32)
        for q in range(4):
            for c in range(4):
                hit = rows[:, q * 128:(q + 1) * 128] == lane1 + (c * 128 + 1)
                gf[pl.ds(at, 80), q * ROWS + c * 128:q * ROWS + (c + 1) * 128] = jnp.where(
                    hit, 1.0, 0.0
                ).astype(BF16)
        x = jnp.where(i80 == inter_at, pair(2, first80), 0)
        x = x + jnp.where(i80 == back_at, pair(3, first80), 0)
        rf[pl.ds(at, 80), :] = halves(x)
        at = pl.multiple_of(j * 16, 16)
        x = jnp.where(i16 == host_at, pair(1, first16), 0)
        rows = jnp.dot(halves(x), q_rep, preferred_element_type=F32).astype(I32)
        for q in range(4):
            for c in range(4):
                hit = rows[:, q * 128:(q + 1) * 128] == lane1 + (c * 128 + 1)
                gm[pl.ds(at, 16), q * ROWS + c * 128:q * ROWS + (c + 1) * 128] = jnp.where(
                    hit, 1.0, 0.0
                ).astype(BF16)
        rm[pl.ds(at, 16), :] = halves(jnp.where(i16 == host_at, pair(2, first16), 0))
        return carry

    lax.fori_loop(0, 16, build_g, 0)

    low = jnp.where(cz > 0, 1.0, 0.0)
    high = jnp.where(cz < 7, 1.0, 0.0)
    left = jnp.where(w > 0, 1.0, 0.0)
    right = jnp.where(w < 7, 1.0, 0.0)
    near = jnp.where(gy > 0, 1.0, 0.0)
    beyond = jnp.where(gy < 3, 1.0, 0.0)
    def packed(x):
        acc = x[0:128]
        for q in range(1, 4):
            acc = jnp.where(l128 // 32 == q, turn(x[q * 128:(q + 1) * 128], 32 * q), acc)
        return acc

    def unpacked(x):
        return jnp.concatenate([turn(x, -32 * q) for q in range(4)], axis=0)

    def halo_copies(par):

        def halo(n, source, dest, device):
            return pltpu.make_async_remote_copy(
                src_ref=source,
                dst_ref=dest,
                send_sem=hsend_sem.at[n],
                recv_sem=hrecv_sem.at[par, n],
                device_id=device,
                device_id_type=MESH,
            )

        return [
            halo(0, hs.at[0], hz.at[par, 0], place(w, gy, (cz + 1) % 8)),
            halo(1, hs.at[1], hz.at[par, 1], place(w, gy, (cz + 7) % 8)),
            halo(2, ys.at[1], hy.at[par, 0], place(w, (gy + 1) % 4, cz)),
            halo(3, ys.at[0], hy.at[par, 1], place(w, (gy + 3) % 4, cz)),
            halo(4, d_ref.at[pl.ds(ROWS - 8, 8)], hx.at[par, 0], place((w + 1) % 8, gy, cz)),
            halo(5, d_ref.at[pl.ds(0, 8)], hx.at[par, 1], place((w + 7) % 8, gy, cz)),
        ]
    def launch(t):
        par = t % 2
        halos = halo_copies(par)
        d = d_ref[...]
        high_part = d.astype(BF16).astype(F32)
        low_part = d - high_part
        for s in range(4):
            for part, x in ((0, turn(high_part, 32 * s)), (1, turn(low_part, 32 * s))):
                q = (s + 1) % 4
                wf[s * ROWS:(s + 1) * ROWS, part * 128:(part + 1) * 128] = jnp.where(
                    group == s, x, 0.0
                ).astype(BF16)
                wm[q * ROWS:(q + 1) * ROWS, part * 128:(part + 1) * 128] = jnp.where(
                    group == q, x, 0.0
                ).astype(BF16)

        def message(k, half):
            return pltpu.make_async_remote_copy(
                src_ref=send.at[k],
                dst_ref=recv.at[par, k],
                send_sem=send_sem,
                recv_sem=recv_sem.at[par, half],
                device_id=peer(k),
                device_id_type=MESH,
            )

        def gather(c, carry):
            at = c * 320 if isinstance(c, int) else pl.multiple_of(c * 320, 320)
            x = jnp.dot(gf[pl.ds(at, 320), :], wf[...], preferred_element_type=F32)
            send[pl.ds(c * 8, 8), 0:40, :] = (x[:, :128] + x[:, 128:]).reshape(8, 40, 128)
            at = c * 64 if isinstance(c, int) else pl.multiple_of(c * 64, 64)
            x = jnp.dot(gm[pl.ds(at, 64), :], wm[...], preferred_element_type=F32)
            send[pl.ds(c * 8, 8), 40:48, :] = (x[:, :128] + x[:, 128:]).reshape(8, 8, 128)
            for n in range(8):
                k = c * 8 + n
                if n < 7 or isinstance(c, int):
                    message(k, c // 2).start()
                else:
                    @pl.when(c < 3)
                    def _():
                        message(k, c // 2).start()
            return carry

        gather(0, 0)
        hs[0] = packed(jnp.where(ln < 16, turn(d, -16), turn(d, -47)))
        hs[1] = packed(jnp.where(ln < 16, d, turn(d, -16)))
        ys[0] = d_ref[pl.ds(0, 64, stride=8), :]
        ys[1] = d_ref[pl.ds(7, 64, stride=8), :]
        for copy in halos:
            copy.start()
        lax.fori_loop(1, 4, gather, 0)
        recv[par, PEERS - 1] = send[PEERS - 1]

    def finish(t):
        par = t % 2
        halos = halo_copies(par)
        d = d_ref[...]
        col = ln % 16
        before = turn(d, 1)
        after = turn(d, -1)
        nb_f = jnp.where(col != 0, before, 0.0) + jnp.where(col != 15, after, 0.0)
        nb_f = nb_f + jnp.where(ln >= 16, turn(d, 16), 0.0) + jnp.where(ln < 16, turn(d, -16), 0.0)
        nb_m = jnp.where(ln != 32, before, 0.0) + jnp.where(ln != 63, after, 0.0)
        nb_m = nb_m + jnp.concatenate([jnp.zeros((8, 128), F32), d[:ROWS - 8]], axis=0)
        nb_m = nb_m + jnp.concatenate([d[8:], jnp.zeros((8, 128), F32)], axis=0)
        sub = lax.broadcasted_iota(I32, (ROWS, 128), 0) % 8
        nb_m = nb_m + jnp.where(sub != 0, pltpu.roll(d, 1, 0), 0.0)
        nb_m = nb_m + jnp.where(sub != 7, pltpu.roll(d, ROWS - 1, 0), 0.0)
        for copy in halos:
            copy.wait_recv()
        from_low = unpacked(hz[par, 0]) * low
        from_high = unpacked(hz[par, 1]) * high
        nb_f = nb_f + jnp.where(ln < 16, from_low, turn(from_high, 16))
        nb_m = nb_m + jnp.where(ln == 32, turn(from_low, 16), 0.0)
        nb_m = nb_m + jnp.where(ln == 63, turn(from_high, 47), 0.0)
        y0 = jnp.broadcast_to((hy[par, 0] * near)[:, None, :], (64, 8, 128)).reshape(ROWS, 128)
        y1 = jnp.broadcast_to((hy[par, 1] * beyond)[:, None, :], (64, 8, 128)).reshape(ROWS, 128)
        nb_m = nb_m + jnp.where(sub == 0, y0, 0.0) + jnp.where(sub == 7, y1, 0.0)
        nb_m = nb_m + jnp.concatenate(
            [hx[par, 0] * left, jnp.zeros((ROWS - 16, 128), F32), hx[par, 1] * right], axis=0
        )
        nb = jnp.where(is_f, TF * nb_f, jnp.where(is_m, nb_m, 0.0))
        p_ref[...] = p_ref[...] + d
        r_ref[...] = r_ref[...] - (c_ref[...] * d - nb)

        sum_f = jnp.zeros((ROWS, 128), F32)
        sum_m = jnp.zeros((ROWS, 128), F32)
        for half in range(2):
            came = recv.at[par, pl.ds(0, 16)] if half == 0 else recv.at[par, pl.ds(16, 15)]
            pltpu.make_async_copy(came, came, recv_sem.at[par, half]).wait()
            x = recv[par, half * 16:(half + 1) * 16, 8:48, :].reshape(640, 128)
            hi = x.astype(BF16)
            rf[half * 640:(half + 1) * 640, 0:128] = hi
            rf[half * 640:(half + 1) * 640, 128:256] = (x - hi.astype(F32)).astype(BF16)
            x = recv[par, half * 16:(half + 1) * 16, 0:8, :].reshape(128, 128)
            hi = x.astype(BF16)
            rm[half * 128:(half + 1) * 128, 0:128] = hi
            rm[half * 128:(half + 1) * 128, 128:256] = (x - hi.astype(F32)).astype(BF16)
            add_f = jnp.zeros((ROWS, 128), F32)
            add_m = jnp.zeros((ROWS, 128), F32)
            for q in range(4):
                x = jnp.dot(
                    sf[q * ROWS:(q + 1) * ROWS, half * 640:(half + 1) * 640],
                    rf[half * 640:(half + 1) * 640, :],
                    preferred_element_type=F32,
                )
                add_f = jnp.where(group == q, x[:, :128] + x[:, 128:], add_f)
                x = jnp.dot(
                    sm[q * ROWS:(q + 1) * ROWS, half * 128:(half + 1) * 128],
                    rm[half * 128:(half + 1) * 128, :],
                    preferred_element_type=F32,
                )
                add_m = jnp.where(group == q, x[:, :128] + x[:, 128:], add_m)
            sum_f = sum_f + add_f
            sum_m = sum_m + add_m
        sum_f = sum_f + turn(sum_f, 64)
        sum_f = sum_f + turn(sum_f, 32)
        sum_m = sum_m + turn(sum_m, 64)
        sum_m = sum_m + turn(sum_m, 32)
        total = jnp.where(is_f, sum_f, jnp.where(is_m, sum_m, 0.0))

        for copy in halos:
            copy.wait_send()
        pltpu.make_async_copy(
            send.at[pl.ds(0, PEERS - 1)], send.at[pl.ds(0, PEERS - 1)], send_sem
        ).wait()
        phase = t % 4
        alpha = jnp.float32(pairs[3][0])
        beta = jnp.float32(pairs[3][1])
        for n in range(3):
            alpha = jnp.where(phase == n, jnp.float32(pairs[n][0]), alpha)
            beta = jnp.where(phase == n, jnp.float32(pairs[n][1]), beta)
        r = r_ref[...] + total
        r_ref[...] = r
        d_ref[...] = alpha * d_ref[...] + beta * (r * i_ref[...])

    launch(0)

    across = (((1,), (1,)), ((), ()))
    sbf = lax.dot_general(q_row, rf[...], across, preferred_element_type=F32).astype(I32)
    sbm = lax.dot_general(q_row, rm[...], across, preferred_element_type=F32).astype(I32)
    within = lax.broadcasted_iota(I32, (1, 1280), 1) % 40
    weight = jnp.where(within < 32, TI, TM)

    def build_s(j, carry):
        at = pl.multiple_of(j * 16, 16)
        block = lax.broadcasted_iota(I32, (16, 1280), 0) + (at + 1)
        for q in range(4):
            sf[pl.ds(at + q * ROWS, 16), :] = jnp.where(sbf[q:q + 1, :] == block, weight, 0.0).astype(BF16)
            sm[pl.ds(at + q * ROWS, 16), :] = jnp.where(
                sbm[q:q + 1, :] == block[:, :256], TM, 0.0
            ).astype(BF16)
        return carry

    lax.fori_loop(0, 32, build_s, 0)

    entering = jnp.where(lax.broadcasted_iota(I32, (1280, 128), 0) % 40 < 16, 1.0, 0.0).astype(BF16)
    ones = jnp.ones((256, 128), BF16)
    indeg = jnp.zeros((ROWS, 128), F32)
    hosted = jnp.zeros((ROWS, 128), F32)
    for q in range(4):
        indeg = indeg + jnp.dot(sf[q * ROWS:(q + 1) * ROWS, :], entering, preferred_element_type=F32)
        hosted = hosted + jnp.dot(sm[q * ROWS:(q + 1) * ROWS, :], ones, preferred_element_type=F32)

    c_ref[...] = c_ref[...] + jnp.where(is_f, 4.0 * TF + 2.0 * TI + TM + indeg, 6.0 + hosted)
    pltpu.make_async_copy(mo.at[pl.ds(0, 248)], mo.at[pl.ds(0, 248)], msend_sem).wait()

    def edge_sent(z, carry):
        @pl.when(jnp.logical_not(own & (z == cz)))
        def _():
            pltpu.make_async_copy(et, et, esend_sem.at[z]).wait()

        return carry

    @pl.when(g == 0)
    def _():
        lax.fori_loop(0, 8, edge_sent, 0)

    def step(t, carry):
        finish(t)

        @pl.when(t < STEPS - 1)
        def _():
            launch(t + 1)

        return carry

    lax.fori_loop(0, STEPS, step, 0)

    for n in range(8):
        acc = jnp.zeros((32, 128), F32)
        for q in range(4):
            at = (n % 4) * 128 + q * 32
            piece = p_ref[at:at + 32, :] + d_ref[at:at + 32, :]
            acc = jnp.where(l32 // 32 == q, turn(piece, 32 * q - (32 if n < 4 else 0)), acc)
        tx2[n] = acc

    def back_start(n, carry):
        mine = own & (n == g * 4 + u_home)

        @pl.when(mine)
        def _():
            rx2[cz] = tx2[n]

        @pl.when(jnp.logical_not(mine))
        def _():
            pltpu.make_async_remote_copy(
                src_ref=tx2.at[n],
                dst_ref=rx2.at[cz],
                send_sem=usend_sem.at[n],
                recv_sem=urecv_sem.at[cz],
                device_id=(n // 4, w * 4 + n % 4, gy),
                device_id_type=MESH,
            ).start()

        return carry

    lax.fori_loop(0, 8, back_start, 0)

    def back_wait(n, carry):
        @pl.when(jnp.logical_not(own & (n == cz)))
        def _():
            pltpu.make_async_copy(rx2.at[n], rx2.at[n], urecv_sem.at[n]).wait()

        @pl.when(jnp.logical_not(own & (n == g * 4 + u_home)))
        def _():
            pltpu.make_async_copy(tx2.at[n], tx2.at[n], usend_sem.at[n]).wait()

        return carry

    lax.fori_loop(0, 8, back_wait, 0)
    for half in range(2):
        for q in range(4):
            acc = jnp.zeros((32, 128), F32)
            for part in range(4):
                acc = jnp.where(l32 // 32 == part, turn(rx2[half * 4 + part], 32 * (part - q)), acc)
            out[q * 32:(q + 1) * 32, half * 128:(half + 1) * 128] = acc


def per_device(source, storage, host_device, host_column, inter_device, inter_slot):
    dma = pltpu.SemaphoreType.DMA
    result = pl.pallas_call(
        kernel,
        out_shape=jax.ShapeDtypeStruct((128, 256), F32),
        in_specs=[pl.BlockSpec(memory_space=pltpu.VMEM)] * 6,
        out_specs=pl.BlockSpec(memory_space=pltpu.VMEM),
        scratch_shapes=[
            pltpu.VMEM((1280, 2048), BF16),
            pltpu.VMEM((256, 2048), BF16),
            pltpu.VMEM((2048, 1280), BF16),
            pltpu.VMEM((2048, 256), BF16),
            pltpu.VMEM((2048, 256), BF16),
            pltpu.VMEM((2048, 256), BF16),
            pltpu.VMEM((1280, 256), BF16),
            pltpu.VMEM((256, 256), BF16),
            pltpu.VMEM((PEERS, MSG, 128), F32),
            pltpu.VMEM((2, PEERS, MSG, 128), F32),
            pltpu.VMEM((2, 128, 128), F32),
            pltpu.VMEM((2, 2, 128, 128), F32),
            pltpu.VMEM((2, 64, 128), F32),
            pltpu.VMEM((2, 2, 64, 128), F32),
            pltpu.VMEM((2, 2, 8, 128), F32),
            pltpu.VMEM((8, 64, 128), F32),
            pltpu.VMEM((8, 64, 128), F32),
            pltpu.VMEM((8, 32, 128), F32),
            pltpu.VMEM((8, 32, 128), F32),
            pltpu.VMEM((256, 128), F32),
            pltpu.VMEM((256, 128), F32),
            pltpu.VMEM((4, 32, 128), I32),
            pltpu.VMEM((8, 128), F32),
            pltpu.VMEM((4, 8, 128), F32),
        ]
        + [pltpu.VMEM((ROWS, 128), F32)] * 5
        + [
            dma,
            dma((2, 2)),
            dma((6,)),
            dma((2, 6)),
            dma((8,)),
            dma((8,)),
            dma((8,)),
            dma((8,)),
            dma,
            dma,
            dma((8,)),
            dma((4,)),
        ],
        compiler_params=pltpu.CompilerParams(
            collective_id=0, has_side_effects=True, vmem_limit_bytes=50 * 1024 * 1024
        ),
    )(
        source.reshape(128, 256),
        storage.reshape(128, 256),
        host_device.reshape(1, 128),
        host_column.reshape(1, 128),
        inter_device.T,
        inter_slot.T,
    )
    return result.reshape(source.shape)


def solution(mesh):
    in_specs = (
        P("grp", "gx", "gy", None),
        P("grp", "gx", "gy", None),
        P(("gx", "gy"), None),
        P(("gx", "gy")),
        P(("gx", "gy"), None),
        P(("gx", "gy"), None),
    )
    return jax.shard_map(
        per_device, mesh=mesh, in_specs=in_specs, out_specs=P("grp", "gx", "gy", None), check_vma=False
    )
```

```python
import jax
import jax.numpy as jnp
from jax import lax
from jax.experimental import pallas as pl
from jax.experimental.pallas import tpu as pltpu
from jax.sharding import PartitionSpec as P

TF = 2.0
TI = 1.0
TM = 0.5
LMIN = 0.3
LMAX = 3.0
STEPS = 7

ROWS = 512
PEERS = 32
MSG = 48

F32 = jnp.float32
BF16 = jnp.bfloat16
I32 = jnp.int32
MESH = pl.DeviceIdType.MESH


def coefficients():
    theta = (LMAX + LMIN) / 2.0
    delta = (LMAX - LMIN) / 2.0
    sigma = theta / delta
    rho = 1.0 / sigma
    pairs = []
    for _ in range(3):
        rho_new = 1.0 / (2.0 * sigma - rho)
        pairs.append((rho_new * rho, 2.0 * rho_new / delta))
        rho = rho_new
    pairs.append((0.0, 1.0 / theta))
    return pairs, theta


def turn(x, shift):
    shift = shift % 128
    return x if shift == 0 else pltpu.roll(x, shift, 1)


def lanes(rows):
    return lax.broadcasted_iota(I32, (rows, 128), 1)


def kernel(
    src, sto, host_dev, host_col, inter_dev, inter_slot, out,
    gf, gm, sf, sm, wf, wm, rf, rm,
    send, recv, hs, hz, ys, hy, hx,
    tx, rx, tx2, rx2, mo, mi, vs, et, er,
    d_ref, r_ref, p_ref, c_ref, i_ref,
    send_sem, recv_sem, hsend_sem, hrecv_sem, tsend_sem, trecv_sem, usend_sem, urecv_sem, msend_sem, mrecv_sem, esend_sem, erecv_sem,
):
    g = lax.axis_index("grp")
    gx = lax.axis_index("gx")
    gy = lax.axis_index("gy")
    x_hi = gx // 16
    cz = (gx // 2) % 8
    core = gx % 2
    w = x_hi * 4 + g * 2 + core

    def place(w_, y_, z_):
        return ((w_ // 2) % 2, (w_ // 4) * 16 + z_ * 2 + w_ % 2, y_)

    def peer(k):
        n = 31 - k
        return place((w + n % 8) % 8, (gy + n // 8 + n % 8) % 4, cz)

    w_home = gx // 4
    u_home = gx % 4
    own = w_home == w

    barrier = pltpu.get_barrier_semaphore()

    def greet(device):
        pl.semaphore_signal(barrier, inc=1, device_id=device, device_id_type=MESH)

    def greet_peer(k, carry):
        greet(peer(k))
        return carry


    def greet_far(n, carry):
        @pl.when(jnp.logical_not(own & (n == cz)))
        def _():
            greet(place(w_home, gy, n))

        @pl.when(jnp.logical_not(own & (n == g * 4 + u_home)))
        def _():
            greet((n // 4, w * 4 + n % 4, gy))

        return carry

    lax.fori_loop(0, 8, greet_far, 0)
    lax.fori_loop(0, PEERS - 1, greet_peer, 0)
    greet(place(w, gy, (cz + 1) % 8))
    greet(place(w, gy, (cz + 7) % 8))

    l128 = lanes(128)
    s128 = lax.broadcasted_iota(I32, (128, 128), 0)
    earlier = jnp.where(l128 < s128, 1.0, 0.0).astype(BF16)

    def column(row):
        return jnp.sum(jnp.where(l128 == s128, row.astype(F32), 0.0), axis=1, keepdims=True)

    edges = jnp.zeros((8, 128), F32)
    s8 = lax.broadcasted_iota(I32, (8, 128), 0)

    def list_edges(edges, devices, rows, base, most):
        before = jnp.zeros((1, 128), F32)
        for dev, row in zip(devices, rows):
            named = column(dev) == l128.astype(F32)
            hit = jnp.where(named, 1.0, 0.0)
            rank = before + jnp.dot(earlier, hit.astype(BF16), preferred_element_type=F32)
            before = before + jnp.sum(hit, axis=0, keepdims=True)
            code = jnp.where(named, column(row) + (1 + 128 * s128).astype(F32), 0.0)
            for r in range(most):
                x = jnp.sum(jnp.where(rank == float(r), code, 0.0), axis=0, keepdims=True)
                edges = edges + jnp.where(s8 == base + r, x, 0.0)
        return edges

    edges = list_edges(
        edges, [inter_dev[0:1, :], inter_dev[1:2, :]], [inter_slot[0:1, :], inter_slot[1:2, :]], 0, 4
    )
    edges = list_edges(edges, [host_dev[...]], [host_col[...]], 4, 2)
    et[...] = edges

    l32 = lanes(32)
    for z in range(8):
        half, part = z // 4, z % 4
        for a, ref in ((0, src), (1, sto)):
            acc = jnp.zeros((32, 128), F32)
            for q in range(4):
                piece = ref[q * 32:(q + 1) * 32, half * 128:(half + 1) * 128]
                acc = jnp.where(l32 // 32 == q, turn(piece, 32 * (q - part)), acc)
            tx[z, a * 32:(a + 1) * 32, :] = acc

    pl.semaphore_wait(barrier, PEERS - 1 + 2 + jnp.where(own, 14, 16))

    def edge_start(z, carry):
        mine = own & (z == cz)

        @pl.when(mine)
        def _():
            er[u_home] = et[...]

        @pl.when(jnp.logical_not(mine))
        def _():
            pltpu.make_async_remote_copy(
                src_ref=et,
                dst_ref=er.at[u_home],
                send_sem=esend_sem.at[z],
                recv_sem=erecv_sem.at[u_home],
                device_id=place(w_home, gy, z),
                device_id_type=MESH,
            ).start()

        return carry

    @pl.when(g == 0)
    def _():
        lax.fori_loop(0, 8, edge_start, 0)

    def far_copy(z):
        return pltpu.make_async_remote_copy(
            src_ref=tx.at[z],
            dst_ref=rx.at[g * 4 + u_home],
            send_sem=tsend_sem.at[z],
            recv_sem=trecv_sem.at[g * 4 + u_home],
            device_id=place(w_home, gy, z),
            device_id_type=MESH,
        )

    def far_start(z, carry):
        mine = own & (z == cz)

        @pl.when(mine)
        def _():
            rx[g * 4 + u_home] = tx[z]

        @pl.when(jnp.logical_not(mine))
        def _():
            far_copy(z).start()

        return carry

    lax.fori_loop(0, 8, far_start, 0)

    def edge_wait(n, carry):
        @pl.when(jnp.logical_not(own & (g == 0) & (n == u_home)))
        def _():
            pltpu.make_async_copy(er.at[n], er.at[n], erecv_sem.at[n]).wait()

        return carry

    lax.fori_loop(0, 4, edge_wait, 0)

    lane1 = lax.broadcasted_iota(I32, (1, 128), 1)
    ub1 = lane1 // 32
    ua1 = lane1 % 32 // 8
    t1 = lane1 % 8
    k32 = lax.broadcasted_iota(I32, (32, 128), 0)
    table = er[...].reshape(32, 128)
    table = jnp.concatenate([table] * 4, axis=0)
    n32 = 31 - k32
    first_of = ((w + n32 % 8) % 8) * 16 + (gy + n32 // 8 + n32 % 8) % 4
    outgoing = jnp.zeros((32, 128), F32)
    for ub in range(4):
        chosen = jnp.where(first_of + ub * 4 == l32, 1.0, 0.0)
        x = lax.dot_general(
            chosen, table, (((1,), (1,)), ((), ())),
            precision=lax.Precision.HIGHEST, preferred_element_type=F32,
        )
        outgoing = jnp.where(ub1 == ub, x, outgoing)
    mo[...] = jnp.broadcast_to(outgoing[:, None, :], (32, 8, 128)).reshape(256, 128)
    mi[248:256] = mo[248:256]

    def edge_send(k, carry):
        at = pl.multiple_of(k * 8, 8)
        pltpu.make_async_remote_copy(
            src_ref=mo.at[pl.ds(at, 8)],
            dst_ref=mi.at[pl.ds(at, 8)],
            send_sem=msend_sem,
            recv_sem=mrecv_sem,
            device_id=peer(k),
            device_id_type=MESH,
        ).start()
        return carry

    lax.fori_loop(0, PEERS - 1, edge_send, 0)

    def far_wait(n, carry):
        mine = own & (n == g * 4 + u_home)

        @pl.when(jnp.logical_not(mine))
        def _():
            pltpu.make_async_copy(rx.at[n], rx.at[n], trecv_sem.at[n]).wait()

        @pl.when(jnp.logical_not(own & (n == cz)))
        def _():
            pltpu.make_async_copy(tx.at[n], tx.at[n], tsend_sem.at[n]).wait()

        return carry

    lax.fori_loop(0, 8, far_wait, 0)

    ln = lanes(ROWS)
    group = ln // 32
    is_f = ln < 32
    is_m = group == 1

    pairs, theta = coefficients()
    for a, ref in ((0, r_ref), (1, c_ref)):
        for u in range(4):
            fr = rx[4 + u, a * 32:(a + 1) * 32, :]
            ma = rx[u, a * 32:(a + 1) * 32, :]
            for q in range(4):
                ref[u * 128 + q * 32:u * 128 + (q + 1) * 32, :] = jnp.where(
                    l32 < 32,
                    turn(fr, -32 * q),
                    jnp.where(l32 // 32 == 1, turn(ma, 32 - 32 * q), 0.0),
                )
    stored = c_ref[...]
    inverse = 1.0 / (stored + jnp.where(is_f, 4.0 * TF + 4.0 * TI + TM, 6.0 + TM))
    i_ref[...] = inverse
    c_ref[...] = stored
    d_ref[...] = r_ref[...] * inverse * (1.0 / theta)
    p_ref[...] = jnp.zeros((ROWS, 128), F32)

    mirror = (8 - n32 % 8) % 8
    mirror = 31 - (mirror + 8 * ((16 - n32 // 8 - n32 % 8 - mirror) % 4))
    mirror = jnp.where(mirror == l32, 1.0, 0.0)[:, :32]

    def mirrored(x):
        return jnp.dot(mirror, x, precision=lax.Precision.HIGHEST, preferred_element_type=F32)

    def source_row(x):
        x = x.astype(I32)
        return jnp.where(x > 0, ua1 * 128 + ((x - 1) >> 7) + 1, 0)

    def target_row(x):
        x = x.astype(I32)
        return jnp.where(x > 0, ub1 * 128 + ((x - 1) & 127) + 1, 0)

    vs[0] = source_row(outgoing)
    vs[3] = source_row(mirrored(outgoing))

    inter_at = jnp.where(t1 < 4, ua1 * 4 + ub1, -100)
    host_at = jnp.where((t1 == 4) | (t1 == 5), ua1 * 2 + t1 - 4, -100)
    out_at = jnp.maximum(inter_at + 8, host_at)
    back_at = jnp.maximum(inter_at + 16, host_at + 32)
    i80 = lax.broadcasted_iota(I32, (80, 128), 0)
    first80 = i80 < 40
    i80 = i80 % 40
    i16 = lax.broadcasted_iota(I32, (16, 128), 0)
    first16 = i16 < 8
    i16 = i16 % 8
    ql = lax.broadcasted_iota(I32, (256, 512), 0)
    qt = ql % 8
    qh = jnp.where(qt < 4, qt, (ql % 128) // 32)
    q_rep = jnp.where(
        lax.broadcasted_iota(I32, (256, 512), 1) // 128 == qh, jnp.where(ql < 128, 32.0, 1.0), 0.0
    ).astype(BF16)
    ql = lax.broadcasted_iota(I32, (16, 256), 1)
    qt = ql % 8
    qh = jnp.where(qt < 4, qt, (ql % 128) // 32)
    q_row = jnp.where(
        lax.broadcasted_iota(I32, (16, 256), 0) == qh, jnp.where(ql < 128, 32.0, 1.0), 0.0
    ).astype(BF16)

    def halves(x):
        return jnp.concatenate([(x >> 5).astype(F32), (x & 31).astype(F32)], axis=1).astype(BF16)

    pltpu.make_async_copy(mi.at[pl.ds(0, 248)], mi.at[pl.ds(0, 248)], mrecv_sem).wait()
    incoming = mi[pl.ds(0, 32, stride=8), :]
    vs[1] = target_row(mirrored(incoming))
    vs[2] = target_row(incoming)

    def build_g(j, carry):
        def pair(n, first):
            return jnp.where(first, vs[n, pl.ds(2 * j, 1), :], vs[n, pl.ds(2 * j + 1, 1), :])

        at = pl.multiple_of(j * 80, 80)
        x = jnp.where(i80 == out_at, pair(0, first80), 0)
        x = x + jnp.where(i80 == inter_at + 24, pair(1, first80), 0)
        rows = jnp.dot(halves(x), q_rep, preferred_element_type=F32).astype(I32)
        for q in range(4):
            for c in range(4):
                hit = rows[:, q * 128:(q + 1) * 128] == lane1 + (c * 128 + 1)
                gf[pl.ds(at, 80), q * ROWS + c * 128:q * ROWS + (c + 1) * 128] = jnp.where(
                    hit, 1.0, 0.0
                ).astype(BF16)
        x = jnp.where(i80 == inter_at, pair(2, first80), 0)
        x = x + jnp.where(i80 == back_at, pair(3, first80), 0)
        rf[pl.ds(at, 80), :] = halves(x)
        at = pl.multiple_of(j * 16, 16)
        x = jnp.where(i16 == host_at, pair(1, first16), 0)
        rows = jnp.dot(halves(x), q_rep, preferred_element_type=F32).astype(I32)
        for q in range(4):
            for c in range(4):
                hit = rows[:, q * 128:(q + 1) * 128] == lane1 + (c * 128 + 1)
                gm[pl.ds(at, 16), q * ROWS + c * 128:q * ROWS + (c + 1) * 128] = jnp.where(
                    hit, 1.0, 0.0
                ).astype(BF16)
        rm[pl.ds(at, 16), :] = halves(jnp.where(i16 == host_at, pair(2, first16), 0))
        return carry

    lax.fori_loop(0, 16, build_g, 0)

    low = jnp.where(cz > 0, 1.0, 0.0)
    high = jnp.where(cz < 7, 1.0, 0.0)
    left = jnp.where(w > 0, 1.0, 0.0)
    right = jnp.where(w < 7, 1.0, 0.0)
    near = jnp.where(gy > 0, 1.0, 0.0)
    beyond = jnp.where(gy < 3, 1.0, 0.0)
    def packed(x):
        acc = x[0:128]
        for q in range(1, 4):
            acc = jnp.where(l128 // 32 == q, turn(x[q * 128:(q + 1) * 128], 32 * q), acc)
        return acc

    def unpacked(x):
        return jnp.concatenate([turn(x, -32 * q) for q in range(4)], axis=0)

    def halo_copies(par):

        def halo(n, source, dest, device):
            return pltpu.make_async_remote_copy(
                src_ref=source,
                dst_ref=dest,
                send_sem=hsend_sem.at[n],
                recv_sem=hrecv_sem.at[par, n],
                device_id=device,
                device_id_type=MESH,
            )

        return [
            halo(0, hs.at[0], hz.at[par, 0], place(w, gy, (cz + 1) % 8)),
            halo(1, hs.at[1], hz.at[par, 1], place(w, gy, (cz + 7) % 8)),
            halo(2, ys.at[1], hy.at[par, 0], place(w, (gy + 1) % 4, cz)),
            halo(3, ys.at[0], hy.at[par, 1], place(w, (gy + 3) % 4, cz)),
            halo(4, d_ref.at[pl.ds(ROWS - 8, 8)], hx.at[par, 0], place((w + 1) % 8, gy, cz)),
            halo(5, d_ref.at[pl.ds(0, 8)], hx.at[par, 1], place((w + 7) % 8, gy, cz)),
        ]
    def launch(t):
        par = t % 2
        halos = halo_copies(par)
        d = d_ref[...]
        high_part = d.astype(BF16).astype(F32)
        low_part = d - high_part
        for s in range(4):
            for part, x in ((0, turn(high_part, 32 * s)), (1, turn(low_part, 32 * s))):
                q = (s + 1) % 4
                wf[s * ROWS:(s + 1) * ROWS, part * 128:(part + 1) * 128] = jnp.where(
                    group == s, x, 0.0
                ).astype(BF16)
                wm[q * ROWS:(q + 1) * ROWS, part * 128:(part + 1) * 128] = jnp.where(
                    group == q, x, 0.0
                ).astype(BF16)

        def message(k, half):
            return pltpu.make_async_remote_copy(
                src_ref=send.at[k],
                dst_ref=recv.at[par, k],
                send_sem=send_sem,
                recv_sem=recv_sem.at[par, half],
                device_id=peer(k),
                device_id_type=MESH,
            )

        def gather(c, carry):
            at = c * 320 if isinstance(c, int) else pl.multiple_of(c * 320, 320)
            x = jnp.dot(gf[pl.ds(at, 320), :], wf[...], preferred_element_type=F32)
            send[pl.ds(c * 8, 8), 0:40, :] = (x[:, :128] + x[:, 128:]).reshape(8, 40, 128)
            at = c * 64 if isinstance(c, int) else pl.multiple_of(c * 64, 64)
            x = jnp.dot(gm[pl.ds(at, 64), :], wm[...], preferred_element_type=F32)
            send[pl.ds(c * 8, 8), 40:48, :] = (x[:, :128] + x[:, 128:]).reshape(8, 8, 128)
            for n in range(8):
                k = c * 8 + n
                if n < 7 or isinstance(c, int):
                    message(k, c // 2).start()
                else:
                    @pl.when(c < 3)
                    def _():
                        message(k, c // 2).start()
            return carry

        gather(0, 0)
        hs[0] = packed(jnp.where(ln < 16, turn(d, -16), turn(d, -47)))
        hs[1] = packed(jnp.where(ln < 16, d, turn(d, -16)))
        ys[0] = d_ref[pl.ds(0, 64, stride=8), :]
        ys[1] = d_ref[pl.ds(7, 64, stride=8), :]
        for copy in halos:
            copy.start()
        lax.fori_loop(1, 4, gather, 0)
        recv[par, PEERS - 1] = send[PEERS - 1]

    def finish(t):
        par = t % 2
        halos = halo_copies(par)
        d = d_ref[...]
        col = ln % 16
        before = turn(d, 1)
        after = turn(d, -1)
        nb_f = jnp.where(col != 0, before, 0.0) + jnp.where(col != 15, after, 0.0)
        nb_f = nb_f + jnp.where(ln >= 16, turn(d, 16), 0.0) + jnp.where(ln < 16, turn(d, -16), 0.0)
        nb_m = jnp.where(ln != 32, before, 0.0) + jnp.where(ln != 63, after, 0.0)
        nb_m = nb_m + jnp.concatenate([jnp.zeros((8, 128), F32), d[:ROWS - 8]], axis=0)
        nb_m = nb_m + jnp.concatenate([d[8:], jnp.zeros((8, 128), F32)], axis=0)
        sub = lax.broadcasted_iota(I32, (ROWS, 128), 0) % 8
        nb_m = nb_m + jnp.where(sub != 0, pltpu.roll(d, 1, 0), 0.0)
        nb_m = nb_m + jnp.where(sub != 7, pltpu.roll(d, ROWS - 1, 0), 0.0)
        for copy in halos:
            copy.wait_recv()
        from_low = unpacked(hz[par, 0]) * low
        from_high = unpacked(hz[par, 1]) * high
        nb_f = nb_f + jnp.where(ln < 16, from_low, turn(from_high, 16))
        nb_m = nb_m + jnp.where(ln == 32, turn(from_low, 16), 0.0)
        nb_m = nb_m + jnp.where(ln == 63, turn(from_high, 47), 0.0)
        y0 = jnp.broadcast_to((hy[par, 0] * near)[:, None, :], (64, 8, 128)).reshape(ROWS, 128)
        y1 = jnp.broadcast_to((hy[par, 1] * beyond)[:, None, :], (64, 8, 128)).reshape(ROWS, 128)
        nb_m = nb_m + jnp.where(sub == 0, y0, 0.0) + jnp.where(sub == 7, y1, 0.0)
        nb_m = nb_m + jnp.concatenate(
            [hx[par, 0] * left, jnp.zeros((ROWS - 16, 128), F32), hx[par, 1] * right], axis=0
        )
        nb = jnp.where(is_f, TF * nb_f, jnp.where(is_m, nb_m, 0.0))
        p_ref[...] = p_ref[...] + d
        r_ref[...] = r_ref[...] - (c_ref[...] * d - nb)

        sum_f = jnp.zeros((ROWS, 128), F32)
        sum_m = jnp.zeros((ROWS, 128), F32)
        for half in range(2):
            came = recv.at[par, pl.ds(0, 16)] if half == 0 else recv.at[par, pl.ds(16, 15)]
            pltpu.make_async_copy(came, came, recv_sem.at[par, half]).wait()
            x = recv[par, half * 16:(half + 1) * 16, 8:48, :].reshape(640, 128)
            hi = x.astype(BF16)
            rf[half * 640:(half + 1) * 640, 0:128] = hi
            rf[half * 640:(half + 1) * 640, 128:256] = (x - hi.astype(F32)).astype(BF16)
            x = recv[par, half * 16:(half + 1) * 16, 0:8, :].reshape(128, 128)
            hi = x.astype(BF16)
            rm[half * 128:(half + 1) * 128, 0:128] = hi
            rm[half * 128:(half + 1) * 128, 128:256] = (x - hi.astype(F32)).astype(BF16)
            add_f = jnp.zeros((ROWS, 128), F32)
            add_m = jnp.zeros((ROWS, 128), F32)
            for q in range(4):
                x = jnp.dot(
                    sf[q * ROWS:(q + 1) * ROWS, half * 640:(half + 1) * 640],
                    rf[half * 640:(half + 1) * 640, :],
                    preferred_element_type=F32,
                )
                add_f = jnp.where(group == q, x[:, :128] + x[:, 128:], add_f)
                x = jnp.dot(
                    sm[q * ROWS:(q + 1) * ROWS, half * 128:(half + 1) * 128],
                    rm[half * 128:(half + 1) * 128, :],
                    preferred_element_type=F32,
                )
                add_m = jnp.where(group == q, x[:, :128] + x[:, 128:], add_m)
            sum_f = sum_f + add_f
            sum_m = sum_m + add_m
        sum_f = sum_f + turn(sum_f, 64)
        sum_f = sum_f + turn(sum_f, 32)
        sum_m = sum_m + turn(sum_m, 64)
        sum_m = sum_m + turn(sum_m, 32)
        total = jnp.where(is_f, sum_f, jnp.where(is_m, sum_m, 0.0))

        for copy in halos:
            copy.wait_send()
        pltpu.make_async_copy(
            send.at[pl.ds(0, PEERS - 1)], send.at[pl.ds(0, PEERS - 1)], send_sem
        ).wait()
        phase = t % 4
        alpha = jnp.float32(pairs[3][0])
        beta = jnp.float32(pairs[3][1])
        for n in range(3):
            alpha = jnp.where(phase == n, jnp.float32(pairs[n][0]), alpha)
            beta = jnp.where(phase == n, jnp.float32(pairs[n][1]), beta)
        r = r_ref[...] + total
        r_ref[...] = r
        d_ref[...] = alpha * d_ref[...] + beta * (r * i_ref[...])

    launch(0)

    across = (((1,), (1,)), ((), ()))
    sbf = lax.dot_general(q_row, rf[...], across, preferred_element_type=F32).astype(I32)
    sbm = lax.dot_general(q_row, rm[...], across, preferred_element_type=F32).astype(I32)
    within = lax.broadcasted_iota(I32, (1, 1280), 1) % 40
    weight = jnp.where(within < 32, TI, TM)

    def build_s(j, carry):
        at = pl.multiple_of(j * 16, 16)
        block = lax.broadcasted_iota(I32, (16, 1280), 0) + (at + 1)
        for q in range(4):
            sf[pl.ds(at + q * ROWS, 16), :] = jnp.where(sbf[q:q + 1, :] == block, weight, 0.0).astype(BF16)
            sm[pl.ds(at + q * ROWS, 16), :] = jnp.where(
                sbm[q:q + 1, :] == block[:, :256], TM, 0.0
            ).astype(BF16)
        return carry

    lax.fori_loop(0, 32, build_s, 0)

    entering = jnp.where(lax.broadcasted_iota(I32, (1280, 128), 0) % 40 < 16, 1.0, 0.0).astype(BF16)
    ones = jnp.ones((256, 128), BF16)
    indeg = jnp.zeros((ROWS, 128), F32)
    hosted = jnp.zeros((ROWS, 128), F32)
    for q in range(4):
        indeg = indeg + jnp.dot(sf[q * ROWS:(q + 1) * ROWS, :], entering, preferred_element_type=F32)
        hosted = hosted + jnp.dot(sm[q * ROWS:(q + 1) * ROWS, :], ones, preferred_element_type=F32)

    c_ref[...] = c_ref[...] + jnp.where(is_f, 4.0 * TF + 2.0 * TI + TM + indeg, 6.0 + hosted)
    pltpu.make_async_copy(mo.at[pl.ds(0, 248)], mo.at[pl.ds(0, 248)], msend_sem).wait()

    def edge_sent(z, carry):
        @pl.when(jnp.logical_not(own & (z == cz)))
        def _():
            pltpu.make_async_copy(et, et, esend_sem.at[z]).wait()

        return carry

    @pl.when(g == 0)
    def _():
        lax.fori_loop(0, 8, edge_sent, 0)

    def step(t, carry):
        finish(t)

        @pl.when(t < STEPS - 1)
        def _():
            launch(t + 1)

        return carry

    lax.fori_loop(0, STEPS, step, 0)

    for n in range(8):
        acc = jnp.zeros((32, 128), F32)
        for q in range(4):
            at = (n % 4) * 128 + q * 32
            piece = p_ref[at:at + 32, :] + d_ref[at:at + 32, :]
            acc = jnp.where(l32 // 32 == q, turn(piece, 32 * q - (32 if n < 4 else 0)), acc)
        tx2[n] = acc

    def back_start(n, carry):
        mine = own & (n == g * 4 + u_home)

        @pl.when(mine)
        def _():
            rx2[cz] = tx2[n]

        @pl.when(jnp.logical_not(mine))
        def _():
            pltpu.make_async_remote_copy(
                src_ref=tx2.at[n],
                dst_ref=rx2.at[cz],
                send_sem=usend_sem.at[n],
                recv_sem=urecv_sem.at[cz],
                device_id=(n // 4, w * 4 + n % 4, gy),
                device_id_type=MESH,
            ).start()

        return carry

    lax.fori_loop(0, 8, back_start, 0)

    def back_wait(n, carry):
        @pl.when(jnp.logical_not(own & (n == cz)))
        def _():
            pltpu.make_async_copy(rx2.at[n], rx2.at[n], urecv_sem.at[n]).wait()

        @pl.when(jnp.logical_not(own & (n == g * 4 + u_home)))
        def _():
            pltpu.make_async_copy(tx2.at[n], tx2.at[n], usend_sem.at[n]).wait()

        return carry

    lax.fori_loop(0, 8, back_wait, 0)
    for half in range(2):
        for q in range(4):
            acc = jnp.zeros((32, 128), F32)
            for part in range(4):
                acc = jnp.where(l32 // 32 == part, turn(rx2[half * 4 + part], 32 * (part - q)), acc)
            out[q * 32:(q + 1) * 32, half * 128:(half + 1) * 128] = acc


def per_device(source, storage, host_device, host_column, inter_device, inter_slot):
    dma = pltpu.SemaphoreType.DMA
    result = pl.pallas_call(
        kernel,
        out_shape=jax.ShapeDtypeStruct((128, 256), F32),
        in_specs=[pl.BlockSpec(memory_space=pltpu.VMEM)] * 6,
        out_specs=pl.BlockSpec(memory_space=pltpu.VMEM),
        scratch_shapes=[
            pltpu.VMEM((1280, 2048), BF16),
            pltpu.VMEM((256, 2048), BF16),
            pltpu.VMEM((2048, 1280), BF16),
            pltpu.VMEM((2048, 256), BF16),
            pltpu.VMEM((2048, 256), BF16),
            pltpu.VMEM((2048, 256), BF16),
            pltpu.VMEM((1280, 256), BF16),
            pltpu.VMEM((256, 256), BF16),
            pltpu.VMEM((PEERS, MSG, 128), F32),
            pltpu.VMEM((2, PEERS, MSG, 128), F32),
            pltpu.VMEM((2, 128, 128), F32),
            pltpu.VMEM((2, 2, 128, 128), F32),
            pltpu.VMEM((2, 64, 128), F32),
            pltpu.VMEM((2, 2, 64, 128), F32),
            pltpu.VMEM((2, 2, 8, 128), F32),
            pltpu.VMEM((8, 64, 128), F32),
            pltpu.VMEM((8, 64, 128), F32),
            pltpu.VMEM((8, 32, 128), F32),
            pltpu.VMEM((8, 32, 128), F32),
            pltpu.VMEM((256, 128), F32),
            pltpu.VMEM((256, 128), F32),
            pltpu.VMEM((4, 32, 128), I32),
            pltpu.VMEM((8, 128), F32),
            pltpu.VMEM((4, 8, 128), F32),
        ]
        + [pltpu.VMEM((ROWS, 128), F32)] * 5
        + [
            dma,
            dma((2, 2)),
            dma((6,)),
            dma((2, 6)),
            dma((8,)),
            dma((8,)),
            dma((8,)),
            dma((8,)),
            dma,
            dma,
            dma((8,)),
            dma((4,)),
        ],
        compiler_params=pltpu.CompilerParams(
            collective_id=0, has_side_effects=True, vmem_limit_bytes=50 * 1024 * 1024
        ),
    )(
        source.reshape(128, 256),
        storage.reshape(128, 256),
        host_device.reshape(1, 128),
        host_column.reshape(1, 128),
        inter_device.T,
        inter_slot.T,
    )
    return result.reshape(source.shape)


def solution(mesh):
    in_specs = (
        P("grp", "gx", "gy", None),
        P("grp", "gx", "gy", None),
        P(("gx", "gy"), None),
        P(("gx", "gy")),
        P(("gx", "gy"), None),
        P(("gx", "gy"), None),
    )
    return jax.shard_map(
        per_device, mesh=mesh, in_specs=in_specs, out_specs=P("grp", "gx", "gy", None), check_vma=False
    )
```

```python
import jax
import jax.numpy as jnp
from jax import lax
from jax.experimental import pallas as pl
from jax.experimental.pallas import tpu as pltpu
from jax.sharding import PartitionSpec as P

TF = 2.0
TI = 1.0
TM = 0.5
LMIN = 0.3
LMAX = 3.0
STEPS = 7

ROWS = 512
PEERS = 32
MSG = 48

F32 = jnp.float32
BF16 = jnp.bfloat16
I32 = jnp.int32
MESH = pl.DeviceIdType.MESH


def coefficients():
    theta = (LMAX + LMIN) / 2.0
    delta = (LMAX - LMIN) / 2.0
    sigma = theta / delta
    rho = 1.0 / sigma
    pairs = []
    for _ in range(3):
        rho_new = 1.0 / (2.0 * sigma - rho)
        pairs.append((rho_new * rho, 2.0 * rho_new / delta))
        rho = rho_new
    pairs.append((0.0, 1.0 / theta))
    return pairs, theta


def turn(x, shift):
    shift = shift % 128
    return x if shift == 0 else pltpu.roll(x, shift, 1)


def lanes(rows):
    return lax.broadcasted_iota(I32, (rows, 128), 1)


def kernel(
    src, sto, host_dev, host_col, inter_dev, inter_slot, out,
    gf, gm, sf, sm, wf, wm, rf, rm,
    send, recv, hs, hz, ys, hy, hx,
    tx, rx, tx2, rx2, mo, mi, vs, et, er,
    d_ref, r_ref, p_ref, c_ref, i_ref,
    send_sem, recv_sem, hsend_sem, hrecv_sem, tsend_sem, trecv_sem, usend_sem, urecv_sem, msend_sem, mrecv_sem, esend_sem, erecv_sem,
):
    g = lax.axis_index("grp")
    gx = lax.axis_index("gx")
    gy = lax.axis_index("gy")
    x_hi = gx // 16
    cz = (gx // 2) % 8
    core = gx % 2
    w = x_hi * 4 + g * 2 + core

    def place(w_, y_, z_):
        return ((w_ // 2) % 2, (w_ // 4) * 16 + z_ * 2 + w_ % 2, y_)

    def peer(k):
        n = 31 - k
        return place((w + n % 8) % 8, (gy + n // 8 + n % 8) % 4, cz)

    w_home = gx // 4
    u_home = gx % 4
    own = w_home == w

    barrier = pltpu.get_barrier_semaphore()

    def greet(device):
        pl.semaphore_signal(barrier, inc=1, device_id=device, device_id_type=MESH)

    def greet_peer(k, carry):
        greet(peer(k))
        return carry


    def greet_far(n, carry):
        @pl.when(jnp.logical_not(own & (n == cz)))
        def _():
            greet(place(w_home, gy, n))

        @pl.when(jnp.logical_not(own & (n == g * 4 + u_home)))
        def _():
            greet((n // 4, w * 4 + n % 4, gy))

        return carry

    lax.fori_loop(0, 8, greet_far, 0)
    lax.fori_loop(0, PEERS - 1, greet_peer, 0)
    greet(place(w, gy, (cz + 1) % 8))
    greet(place(w, gy, (cz + 7) % 8))

    l128 = lanes(128)
    s128 = lax.broadcasted_iota(I32, (128, 128), 0)
    earlier = jnp.where(l128 < s128, 1.0, 0.0).astype(BF16)

    def column(row):
        return jnp.sum(jnp.where(l128 == s128, row.astype(F32), 0.0), axis=1, keepdims=True)

    edges = jnp.zeros((8, 128), F32)
    s8 = lax.broadcasted_iota(I32, (8, 128), 0)

    def list_edges(edges, devices, rows, base, most):
        before = jnp.zeros((1, 128), F32)
        for dev, row in zip(devices, rows):
            named = column(dev) == l128.astype(F32)
            hit = jnp.where(named, 1.0, 0.0)
            rank = before + jnp.dot(earlier, hit.astype(BF16), preferred_element_type=F32)
            before = before + jnp.sum(hit, axis=0, keepdims=True)
            code = jnp.where(named, column(row) + (1 + 128 * s128).astype(F32), 0.0)
            for r in range(most):
                x = jnp.sum(jnp.where(rank == float(r), code, 0.0), axis=0, keepdims=True)
                edges = edges + jnp.where(s8 == base + r, x, 0.0)
        return edges

    edges = list_edges(
        edges, [inter_dev[0:1, :], inter_dev[1:2, :]], [inter_slot[0:1, :], inter_slot[1:2, :]], 0, 4
    )
    edges = list_edges(edges, [host_dev[...]], [host_col[...]], 4, 2)
    et[...] = edges

    l32 = lanes(32)
    for z in range(8):
        half, part = z // 4, z % 4
        for a, ref in ((0, src), (1, sto)):
            acc = jnp.zeros((32, 128), F32)
            for q in range(4):
                piece = ref[q * 32:(q + 1) * 32, half * 128:(half + 1) * 128]
                acc = jnp.where(l32 // 32 == q, turn(piece, 32 * (q - part)), acc)
            tx[z, a * 32:(a + 1) * 32, :] = acc

    pl.semaphore_wait(barrier, PEERS - 1 + 2 + jnp.where(own, 14, 16))

    def edge_start(z, carry):
        mine = own & (z == cz)

        @pl.when(mine)
        def _():
            er[u_home] = et[...]

        @pl.when(jnp.logical_not(mine))
        def _():
            pltpu.make_async_remote_copy(
                src_ref=et,
                dst_ref=er.at[u_home],
                send_sem=esend_sem.at[z],
                recv_sem=erecv_sem.at[u_home],
                device_id=place(w_home, gy, z),
                device_id_type=MESH,
            ).start()

        return carry

    @pl.when(g == 0)
    def _():
        lax.fori_loop(0, 8, edge_start, 0)

    def far_copy(z):
        return pltpu.make_async_remote_copy(
            src_ref=tx.at[z],
            dst_ref=rx.at[g * 4 + u_home],
            send_sem=tsend_sem.at[z],
            recv_sem=trecv_sem.at[g * 4 + u_home],
            device_id=place(w_home, gy, z),
            device_id_type=MESH,
        )

    def far_start(z, carry):
        mine = own & (z == cz)

        @pl.when(mine)
        def _():
            rx[g * 4 + u_home] = tx[z]

        @pl.when(jnp.logical_not(mine))
        def _():
            far_copy(z).start()

        return carry

    lax.fori_loop(0, 8, far_start, 0)

    def edge_wait(n, carry):
        @pl.when(jnp.logical_not(own & (g == 0) & (n == u_home)))
        def _():
            pltpu.make_async_copy(er.at[n], er.at[n], erecv_sem.at[n]).wait()

        return carry

    lax.fori_loop(0, 4, edge_wait, 0)

    lane1 = lax.broadcasted_iota(I32, (1, 128), 1)
    ub1 = lane1 // 32
    ua1 = lane1 % 32 // 8
    t1 = lane1 % 8
    k32 = lax.broadcasted_iota(I32, (32, 128), 0)
    table = er[...].reshape(32, 128)
    table = jnp.concatenate([table] * 4, axis=0)
    n32 = 31 - k32
    first_of = ((w + n32 % 8) % 8) * 16 + (gy + n32 // 8 + n32 % 8) % 4
    outgoing = jnp.zeros((32, 128), F32)
    for ub in range(4):
        chosen = jnp.where(first_of + ub * 4 == l32, 1.0, 0.0)
        x = lax.dot_general(
            chosen, table, (((1,), (1,)), ((), ())),
            precision=lax.Precision.HIGHEST, preferred_element_type=F32,
        )
        outgoing = jnp.where(ub1 == ub, x, outgoing)
    mo[...] = jnp.broadcast_to(outgoing[:, None, :], (32, 8, 128)).reshape(256, 128)
    mi[248:256] = mo[248:256]

    def edge_send(k, carry):
        at = pl.multiple_of(k * 8, 8)
        pltpu.make_async_remote_copy(
            src_ref=mo.at[pl.ds(at, 8)],
            dst_ref=mi.at[pl.ds(at, 8)],
            send_sem=msend_sem,
            recv_sem=mrecv_sem,
            device_id=peer(k),
            device_id_type=MESH,
        ).start()
        return carry

    lax.fori_loop(0, PEERS - 1, edge_send, 0)

    def far_wait(n, carry):
        mine = own & (n == g * 4 + u_home)

        @pl.when(jnp.logical_not(mine))
        def _():
            pltpu.make_async_copy(rx.at[n], rx.at[n], trecv_sem.at[n]).wait()

        @pl.when(jnp.logical_not(own & (n == cz)))
        def _():
            pltpu.make_async_copy(tx.at[n], tx.at[n], tsend_sem.at[n]).wait()

        return carry

    lax.fori_loop(0, 8, far_wait, 0)

    ln = lanes(ROWS)
    group = ln // 32
    is_f = ln < 32
    is_m = group == 1

    pairs, theta = coefficients()
    for a, ref in ((0, r_ref), (1, c_ref)):
        for u in range(4):
            fr = rx[4 + u, a * 32:(a + 1) * 32, :]
            ma = rx[u, a * 32:(a + 1) * 32, :]
            for q in range(4):
                ref[u * 128 + q * 32:u * 128 + (q + 1) * 32, :] = jnp.where(
                    l32 < 32,
                    turn(fr, -32 * q),
                    jnp.where(l32 // 32 == 1, turn(ma, 32 - 32 * q), 0.0),
                )
    stored = c_ref[...]
    inverse = 1.0 / (stored + jnp.where(is_f, 4.0 * TF + 4.0 * TI + TM, 6.0 + TM))
    i_ref[...] = inverse
    c_ref[...] = stored
    d_ref[...] = r_ref[...] * inverse * (1.0 / theta)
    p_ref[...] = jnp.zeros((ROWS, 128), F32)

    mirror = (8 - n32 % 8) % 8
    mirror = 31 - (mirror + 8 * ((16 - n32 // 8 - n32 % 8 - mirror) % 4))
    mirror = jnp.where(mirror == l32, 1.0, 0.0)[:, :32]

    def mirrored(x):
        return jnp.dot(mirror, x, precision=lax.Precision.HIGHEST, preferred_element_type=F32)

    def source_row(x):
        x = x.astype(I32)
        return jnp.where(x > 0, ua1 * 128 + ((x - 1) >> 7) + 1, 0)

    def target_row(x):
        x = x.astype(I32)
        return jnp.where(x > 0, ub1 * 128 + ((x - 1) & 127) + 1, 0)

    vs[0] = source_row(outgoing)
    vs[3] = source_row(mirrored(outgoing))

    inter_at = jnp.where(t1 < 4, ua1 * 4 + ub1, -100)
    host_at = jnp.where((t1 == 4) | (t1 == 5), ua1 * 2 + t1 - 4, -100)
    out_at = jnp.maximum(inter_at + 8, host_at)
    back_at = jnp.maximum(inter_at + 16, host_at + 32)
    i80 = lax.broadcasted_iota(I32, (80, 128), 0)
    first80 = i80 < 40
    i80 = i80 % 40
    i16 = lax.broadcasted_iota(I32, (16, 128), 0)
    first16 = i16 < 8
    i16 = i16 % 8
    ql = lax.broadcasted_iota(I32, (256, 512), 0)
    qt = ql % 8
    qh = jnp.where(qt < 4, qt, (ql % 128) // 32)
    q_rep = jnp.where(
        lax.broadcasted_iota(I32, (256, 512), 1) // 128 == qh, jnp.where(ql < 128, 32.0, 1.0), 0.0
    ).astype(BF16)
    ql = lax.broadcasted_iota(I32, (16, 256), 1)
    qt = ql % 8
    qh = jnp.where(qt < 4, qt, (ql % 128) // 32)
    q_row = jnp.where(
        lax.broadcasted_iota(I32, (16, 256), 0) == qh, jnp.where(ql < 128, 32.0, 1.0), 0.0
    ).astype(BF16)

    def halves(x):
        return jnp.concatenate([(x >> 5).astype(F32), (x & 31).astype(F32)], axis=1).astype(BF16)

    pltpu.make_async_copy(mi.at[pl.ds(0, 248)], mi.at[pl.ds(0, 248)], mrecv_sem).wait()
    incoming = mi[pl.ds(0, 32, stride=8), :]
    vs[1] = target_row(mirrored(incoming))
    vs[2] = target_row(incoming)

    def build_g(j, carry):
        def pair(n, first):
            return jnp.where(first, vs[n, pl.ds(2 * j, 1), :], vs[n, pl.ds(2 * j + 1, 1), :])

        at = pl.multiple_of(j * 80, 80)
        x = jnp.where(i80 == out_at, pair(0, first80), 0)
        x = x + jnp.where(i80 == inter_at + 24, pair(1, first80), 0)
        rows = jnp.dot(halves(x), q_rep, preferred_element_type=F32).astype(I32)
        for q in range(4):
            for c in range(4):
                hit = rows[:, q * 128:(q + 1) * 128] == lane1 + (c * 128 + 1)
                gf[pl.ds(at, 80), q * ROWS + c * 128:q * ROWS + (c + 1) * 128] = jnp.where(
                    hit, 1.0, 0.0
                ).astype(BF16)
        x = jnp.where(i80 == inter_at, pair(2, first80), 0)
        x = x + jnp.where(i80 == back_at, pair(3, first80), 0)
        rf[pl.ds(at, 80), :] = halves(x)
        at = pl.multiple_of(j * 16, 16)
        x = jnp.where(i16 == host_at, pair(1, first16), 0)
        rows = jnp.dot(halves(x), q_rep, preferred_element_type=F32).astype(I32)
        for q in range(4):
            for c in range(4):
                hit = rows[:, q * 128:(q + 1) * 128] == lane1 + (c * 128 + 1)
                gm[pl.ds(at, 16), q * ROWS + c * 128:q * ROWS + (c + 1) * 128] = jnp.where(
                    hit, 1.0, 0.0
                ).astype(BF16)
        rm[pl.ds(at, 16), :] = halves(jnp.where(i16 == host_at, pair(2, first16), 0))
        return carry

    lax.fori_loop(0, 16, build_g, 0)

    low = jnp.where(cz > 0, 1.0, 0.0)
    high = jnp.where(cz < 7, 1.0, 0.0)
    left = jnp.where(w > 0, 1.0, 0.0)
    right = jnp.where(w < 7, 1.0, 0.0)
    near = jnp.where(gy > 0, 1.0, 0.0)
    beyond = jnp.where(gy < 3, 1.0, 0.0)
    def packed(x):
        acc = x[0:128]
        for q in range(1, 4):
            acc = jnp.where(l128 // 32 == q, turn(x[q * 128:(q + 1) * 128], 32 * q), acc)
        return acc

    def unpacked(x):
        return jnp.concatenate([turn(x, -32 * q) for q in range(4)], axis=0)

    def halo_copies(par):

        def halo(n, source, dest, device):
            return pltpu.make_async_remote_copy(
                src_ref=source,
                dst_ref=dest,
                send_sem=hsend_sem.at[n],
                recv_sem=hrecv_sem.at[par, n],
                device_id=device,
                device_id_type=MESH,
            )

        return [
            halo(0, hs.at[0], hz.at[par, 0], place(w, gy, (cz + 1) % 8)),
            halo(1, hs.at[1], hz.at[par, 1], place(w, gy, (cz + 7) % 8)),
            halo(2, ys.at[1], hy.at[par, 0], place(w, (gy + 1) % 4, cz)),
            halo(3, ys.at[0], hy.at[par, 1], place(w, (gy + 3) % 4, cz)),
            halo(4, d_ref.at[pl.ds(ROWS - 8, 8)], hx.at[par, 0], place((w + 1) % 8, gy, cz)),
            halo(5, d_ref.at[pl.ds(0, 8)], hx.at[par, 1], place((w + 7) % 8, gy, cz)),
        ]
    def launch(t):
        par = t % 2
        halos = halo_copies(par)
        d = d_ref[...]
        high_part = d.astype(BF16).astype(F32)
        low_part = d - high_part
        for s in range(4):
            for part, x in ((0, turn(high_part, 32 * s)), (1, turn(low_part, 32 * s))):
                q = (s + 1) % 4
                wf[s * ROWS:(s + 1) * ROWS, part * 128:(part + 1) * 128] = jnp.where(
                    group == s, x, 0.0
                ).astype(BF16)
                wm[q * ROWS:(q + 1) * ROWS, part * 128:(part + 1) * 128] = jnp.where(
                    group == q, x, 0.0
                ).astype(BF16)

        def message(k, half):
            return pltpu.make_async_remote_copy(
                src_ref=send.at[k],
                dst_ref=recv.at[par, k],
                send_sem=send_sem,
                recv_sem=recv_sem.at[par, half],
                device_id=peer(k),
                device_id_type=MESH,
            )

        def gather(c, carry):
            at = c * 320 if isinstance(c, int) else pl.multiple_of(c * 320, 320)
            x = jnp.dot(gf[pl.ds(at, 320), :], wf[...], preferred_element_type=F32)
            send[pl.ds(c * 8, 8), 0:40, :] = (x[:, :128] + x[:, 128:]).reshape(8, 40, 128)
            at = c * 64 if isinstance(c, int) else pl.multiple_of(c * 64, 64)
            x = jnp.dot(gm[pl.ds(at, 64), :], wm[...], preferred_element_type=F32)
            send[pl.ds(c * 8, 8), 40:48, :] = (x[:, :128] + x[:, 128:]).reshape(8, 8, 128)
            for n in range(8):
                k = c * 8 + n
                if n < 7 or isinstance(c, int):
                    message(k, c // 2).start()
                else:
                    @pl.when(c < 3)
                    def _():
                        message(k, c // 2).start()
            return carry

        gather(0, 0)
        ys[0] = d_ref[pl.ds(0, 64, stride=8), :]
        ys[1] = d_ref[pl.ds(7, 64, stride=8), :]
        for copy in halos[2:]:
            copy.start()
        lax.fori_loop(1, 4, gather, 0)
        hs[0] = packed(jnp.where(ln < 16, turn(d, -16), turn(d, -47)))
        hs[1] = packed(jnp.where(ln < 16, d, turn(d, -16)))
        for copy in halos[:2]:
            copy.start()
        recv[par, PEERS - 1] = send[PEERS - 1]

    def finish(t):
        par = t % 2
        halos = halo_copies(par)
        d = d_ref[...]
        col = ln % 16
        before = turn(d, 1)
        after = turn(d, -1)
        nb_f = jnp.where(col != 0, before, 0.0) + jnp.where(col != 15, after, 0.0)
        nb_f = nb_f + jnp.where(ln >= 16, turn(d, 16), 0.0) + jnp.where(ln < 16, turn(d, -16), 0.0)
        nb_m = jnp.where(ln != 32, before, 0.0) + jnp.where(ln != 63, after, 0.0)
        nb_m = nb_m + jnp.concatenate([jnp.zeros((8, 128), F32), d[:ROWS - 8]], axis=0)
        nb_m = nb_m + jnp.concatenate([d[8:], jnp.zeros((8, 128), F32)], axis=0)
        sub = lax.broadcasted_iota(I32, (ROWS, 128), 0) % 8
        nb_m = nb_m + jnp.where(sub != 0, pltpu.roll(d, 1, 0), 0.0)
        nb_m = nb_m + jnp.where(sub != 7, pltpu.roll(d, ROWS - 1, 0), 0.0)
        for copy in halos:
            copy.wait_recv()
        from_low = unpacked(hz[par, 0]) * low
        from_high = unpacked(hz[par, 1]) * high
        nb_f = nb_f + jnp.where(ln < 16, from_low, turn(from_high, 16))
        nb_m = nb_m + jnp.where(ln == 32, turn(from_low, 16), 0.0)
        nb_m = nb_m + jnp.where(ln == 63, turn(from_high, 47), 0.0)
        y0 = jnp.broadcast_to((hy[par, 0] * near)[:, None, :], (64, 8, 128)).reshape(ROWS, 128)
        y1 = jnp.broadcast_to((hy[par, 1] * beyond)[:, None, :], (64, 8, 128)).reshape(ROWS, 128)
        nb_m = nb_m + jnp.where(sub == 0, y0, 0.0) + jnp.where(sub == 7, y1, 0.0)
        nb_m = nb_m + jnp.concatenate(
            [hx[par, 0] * left, jnp.zeros((ROWS - 16, 128), F32), hx[par, 1] * right], axis=0
        )
        nb = jnp.where(is_f, TF * nb_f, jnp.where(is_m, nb_m, 0.0))
        p_ref[...] = p_ref[...] + d
        r_ref[...] = r_ref[...] - (c_ref[...] * d - nb)

        sum_f = jnp.zeros((ROWS, 128), F32)
        sum_m = jnp.zeros((ROWS, 128), F32)
        for half in range(2):
            came = recv.at[par, pl.ds(0, 16)] if half == 0 else recv.at[par, pl.ds(16, 15)]
            pltpu.make_async_copy(came, came, recv_sem.at[par, half]).wait()
            x = recv[par, half * 16:(half + 1) * 16, 8:48, :].reshape(640, 128)
            hi = x.astype(BF16)
            rf[half * 640:(half + 1) * 640, 0:128] = hi
            rf[half * 640:(half + 1) * 640, 128:256] = (x - hi.astype(F32)).astype(BF16)
            x = recv[par, half * 16:(half + 1) * 16, 0:8, :].reshape(128, 128)
            hi = x.astype(BF16)
            rm[half * 128:(half + 1) * 128, 0:128] = hi
            rm[half * 128:(half + 1) * 128, 128:256] = (x - hi.astype(F32)).astype(BF16)
            add_f = jnp.zeros((ROWS, 128), F32)
            add_m = jnp.zeros((ROWS, 128), F32)
            for q in range(4):
                x = jnp.dot(
                    sf[q * ROWS:(q + 1) * ROWS, half * 640:(half + 1) * 640],
                    rf[half * 640:(half + 1) * 640, :],
                    preferred_element_type=F32,
                )
                add_f = jnp.where(group == q, x[:, :128] + x[:, 128:], add_f)
                x = jnp.dot(
                    sm[q * ROWS:(q + 1) * ROWS, half * 128:(half + 1) * 128],
                    rm[half * 128:(half + 1) * 128, :],
                    preferred_element_type=F32,
                )
                add_m = jnp.where(group == q, x[:, :128] + x[:, 128:], add_m)
            sum_f = sum_f + add_f
            sum_m = sum_m + add_m
        sum_f = sum_f + turn(sum_f, 64)
        sum_f = sum_f + turn(sum_f, 32)
        sum_m = sum_m + turn(sum_m, 64)
        sum_m = sum_m + turn(sum_m, 32)
        total = jnp.where(is_f, sum_f, jnp.where(is_m, sum_m, 0.0))

        for copy in halos:
            copy.wait_send()
        pltpu.make_async_copy(
            send.at[pl.ds(0, PEERS - 1)], send.at[pl.ds(0, PEERS - 1)], send_sem
        ).wait()
        phase = t % 4
        alpha = jnp.float32(pairs[3][0])
        beta = jnp.float32(pairs[3][1])
        for n in range(3):
            alpha = jnp.where(phase == n, jnp.float32(pairs[n][0]), alpha)
            beta = jnp.where(phase == n, jnp.float32(pairs[n][1]), beta)
        r = r_ref[...] + total
        r_ref[...] = r
        d_ref[...] = alpha * d_ref[...] + beta * (r * i_ref[...])

    launch(0)

    across = (((1,), (1,)), ((), ()))
    sbf = lax.dot_general(q_row, rf[...], across, preferred_element_type=F32).astype(I32)
    sbm = lax.dot_general(q_row, rm[...], across, preferred_element_type=F32).astype(I32)
    within = lax.broadcasted_iota(I32, (1, 1280), 1) % 40
    weight = jnp.where(within < 32, TI, TM)

    def build_s(j, carry):
        at = pl.multiple_of(j * 16, 16)
        block = lax.broadcasted_iota(I32, (16, 1280), 0) + (at + 1)
        for q in range(4):
            sf[pl.ds(at + q * ROWS, 16), :] = jnp.where(sbf[q:q + 1, :] == block, weight, 0.0).astype(BF16)
            sm[pl.ds(at + q * ROWS, 16), :] = jnp.where(
                sbm[q:q + 1, :] == block[:, :256], TM, 0.0
            ).astype(BF16)
        return carry

    lax.fori_loop(0, 32, build_s, 0)

    entering = jnp.where(lax.broadcasted_iota(I32, (1280, 128), 0) % 40 < 16, 1.0, 0.0).astype(BF16)
    ones = jnp.ones((256, 128), BF16)
    indeg = jnp.zeros((ROWS, 128), F32)
    hosted = jnp.zeros((ROWS, 128), F32)
    for q in range(4):
        indeg = indeg + jnp.dot(sf[q * ROWS:(q + 1) * ROWS, :], entering, preferred_element_type=F32)
        hosted = hosted + jnp.dot(sm[q * ROWS:(q + 1) * ROWS, :], ones, preferred_element_type=F32)

    c_ref[...] = c_ref[...] + jnp.where(is_f, 4.0 * TF + 2.0 * TI + TM + indeg, 6.0 + hosted)
    pltpu.make_async_copy(mo.at[pl.ds(0, 248)], mo.at[pl.ds(0, 248)], msend_sem).wait()

    def edge_sent(z, carry):
        @pl.when(jnp.logical_not(own & (z == cz)))
        def _():
            pltpu.make_async_copy(et, et, esend_sem.at[z]).wait()

        return carry

    @pl.when(g == 0)
    def _():
        lax.fori_loop(0, 8, edge_sent, 0)

    def step(t, carry):
        finish(t)

        @pl.when(t < STEPS - 1)
        def _():
            launch(t + 1)

        return carry

    lax.fori_loop(0, STEPS, step, 0)

    for n in range(8):
        acc = jnp.zeros((32, 128), F32)
        for q in range(4):
            at = (n % 4) * 128 + q * 32
            piece = p_ref[at:at + 32, :] + d_ref[at:at + 32, :]
            acc = jnp.where(l32 // 32 == q, turn(piece, 32 * q - (32 if n < 4 else 0)), acc)
        tx2[n] = acc

    def back_start(n, carry):
        mine = own & (n == g * 4 + u_home)

        @pl.when(mine)
        def _():
            rx2[cz] = tx2[n]

        @pl.when(jnp.logical_not(mine))
        def _():
            pltpu.make_async_remote_copy(
                src_ref=tx2.at[n],
                dst_ref=rx2.at[cz],
                send_sem=usend_sem.at[n],
                recv_sem=urecv_sem.at[cz],
                device_id=(n // 4, w * 4 + n % 4, gy),
                device_id_type=MESH,
            ).start()

        return carry

    lax.fori_loop(0, 8, back_start, 0)

    def back_wait(n, carry):
        @pl.when(jnp.logical_not(own & (n == cz)))
        def _():
            pltpu.make_async_copy(rx2.at[n], rx2.at[n], urecv_sem.at[n]).wait()

        @pl.when(jnp.logical_not(own & (n == g * 4 + u_home)))
        def _():
            pltpu.make_async_copy(tx2.at[n], tx2.at[n], usend_sem.at[n]).wait()

        return carry

    lax.fori_loop(0, 8, back_wait, 0)
    for half in range(2):
        for q in range(4):
            acc = jnp.zeros((32, 128), F32)
            for part in range(4):
                acc = jnp.where(l32 // 32 == part, turn(rx2[half * 4 + part], 32 * (part - q)), acc)
            out[q * 32:(q + 1) * 32, half * 128:(half + 1) * 128] = acc


def per_device(source, storage, host_device, host_column, inter_device, inter_slot):
    dma = pltpu.SemaphoreType.DMA
    result = pl.pallas_call(
        kernel,
        out_shape=jax.ShapeDtypeStruct((128, 256), F32),
        in_specs=[pl.BlockSpec(memory_space=pltpu.VMEM)] * 6,
        out_specs=pl.BlockSpec(memory_space=pltpu.VMEM),
        scratch_shapes=[
            pltpu.VMEM((1280, 2048), BF16),
            pltpu.VMEM((256, 2048), BF16),
            pltpu.VMEM((2048, 1280), BF16),
            pltpu.VMEM((2048, 256), BF16),
            pltpu.VMEM((2048, 256), BF16),
            pltpu.VMEM((2048, 256), BF16),
            pltpu.VMEM((1280, 256), BF16),
            pltpu.VMEM((256, 256), BF16),
            pltpu.VMEM((PEERS, MSG, 128), F32),
            pltpu.VMEM((2, PEERS, MSG, 128), F32),
            pltpu.VMEM((2, 128, 128), F32),
            pltpu.VMEM((2, 2, 128, 128), F32),
            pltpu.VMEM((2, 64, 128), F32),
            pltpu.VMEM((2, 2, 64, 128), F32),
            pltpu.VMEM((2, 2, 8, 128), F32),
            pltpu.VMEM((8, 64, 128), F32),
            pltpu.VMEM((8, 64, 128), F32),
            pltpu.VMEM((8, 32, 128), F32),
            pltpu.VMEM((8, 32, 128), F32),
            pltpu.VMEM((256, 128), F32),
            pltpu.VMEM((256, 128), F32),
            pltpu.VMEM((4, 32, 128), I32),
            pltpu.VMEM((8, 128), F32),
            pltpu.VMEM((4, 8, 128), F32),
        ]
        + [pltpu.VMEM((ROWS, 128), F32)] * 5
        + [
            dma,
            dma((2, 2)),
            dma((6,)),
            dma((2, 6)),
            dma((8,)),
            dma((8,)),
            dma((8,)),
            dma((8,)),
            dma,
            dma,
            dma((8,)),
            dma((4,)),
        ],
        compiler_params=pltpu.CompilerParams(
            collective_id=0, has_side_effects=True, vmem_limit_bytes=50 * 1024 * 1024
        ),
    )(
        source.reshape(128, 256),
        storage.reshape(128, 256),
        host_device.reshape(1, 128),
        host_column.reshape(1, 128),
        inter_device.T,
        inter_slot.T,
    )
    return result.reshape(source.shape)


def solution(mesh):
    in_specs = (
        P("grp", "gx", "gy", None),
        P("grp", "gx", "gy", None),
        P(("gx", "gy"), None),
        P(("gx", "gy")),
        P(("gx", "gy"), None),
        P(("gx", "gy"), None),
    )
    return jax.shard_map(
        per_device, mesh=mesh, in_specs=in_specs, out_specs=P("grp", "gx", "gy", None), check_vma=False
    )
```
